32 devices in a mesh: parts: 2 (over y), tm: 16 (over z, x, core).
Axes of the slice: x: 2, y: 2, z: 4, core: 2. Of those that a mesh axis runs over, the one named last changes fastest.
Arguments:
- frames: bfloat16 [2048, 2048], P('tm', 'parts'), parts along dimension 1, may hold values from -6 to 6
- levels: int32 [2048], P(('parts', 'tm')), parts along dimension 0, may hold values from 0 to 15
- initial_state: float32 [256], P('parts'), parts along dimension 0, may hold values from -6 to 6
- transitions: float32 [16, 128, 128], replicated, may hold values from -1 to 1
- gain: bfloat16 [128, 128], replicated, may hold values from -1 to 1
- pixel_mode: int32 [2048], replicated, may hold values from 0 to 127
- pixel_weight: bfloat16 [2048], replicated, may hold values from 0.099609375 to 0.5
Outputs:
- estimates: float32 [2048, 128], P(('parts', 'tm')), parts along dimension 0
The draws below stay inside these ranges and needn't reach their ends.
There are 2 independent parts, one for each index of `parts`. The reference program is written for one: setup_inputs(seed, part) draws one part's arguments, and reference() takes and returns one part's arrays. A program takes and returns all parts, laid end to end along the dimension named above; an argument that names none is the same for every part. Nothing has to cross between parts.
All inputs are finite; a program needn't handle non-finite values.
Results may differ from the reference program's by a relative error of at most 0.0026.
Values may be sent and summed in bfloat16 or wider, within the bound.
No kernel may reach another device: no remote copies, remote signals or barrier semaphores. Data moves between devices by JAX's collectives and lax.ppermute only.
A program may use at most 128 MiB of HBM per device.

```python
import math
import jax
import jax.numpy as jnp
from jax import lax

MODAL_DIMENSION = 128
PIX = 2048
LEVELS = 16
FRAMES = 1024


def mode_traits(key):
    modes = MODAL_DIMENSION // 2
    perm = jax.random.permutation(jax.random.fold_in(key, 1), modes)
    slow_count = modes // 2
    lagging_mode_choice = perm < slow_count
    keep = jax.random.uniform(jax.random.fold_in(key, 2), (modes,), jnp.float32, 0.3, 0.8)
    slow_rate = jnp.exp(jnp.log(keep) / FRAMES)
    fast_rate = jax.random.uniform(jax.random.fold_in(key, 3), (modes,), jnp.float32, 0.95, 0.975)
    capture_frequency = jnp.where(lagging_mode_choice, slow_rate, fast_rate)
    base = jax.random.uniform(jax.random.fold_in(key, 4), (modes,), jnp.float32, 0.05, 1.5)
    return (lagging_mode_choice, capture_frequency, base)


def draw_levels(key, part):
    holds = FRAMES // 16
    values = jax.random.randint(jax.random.fold_in(key, 21), (holds,), 1, LEVELS)
    values = values.at[0].set(LEVELS - 1)
    plan = jnp.repeat(values, 16)
    spots = jax.random.randint(jax.random.fold_in(key, 22), (4,), 0, FRAMES)
    plan = plan.at[spots].set(0)
    return plan.astype(jnp.int32)


def draw_transitions(key, part):
    lagging_mode_choice, capture_frequency, base = mode_traits(key)
    tension = jax.random.uniform(jax.random.fold_in(key, 5), (LEVELS,), jnp.float32, 0.7, 1.3)
    image_count_per_group = jax.random.uniform(jax.random.fold_in(key, 6), (MODAL_DIMENSION // 2,), jnp.float32, 0.5, 0.8)
    omega = base[None, :] * jnp.sqrt(tension)[:, None]
    tier_indices = jnp.arange(LEVELS)
    neighborhood_extent = capture_frequency[None, :] * jnp.where((tier_indices[:, None] == 0) & lagging_mode_choice[None, :], image_count_per_group[None, :], 1.0)
    cosine = neighborhood_extent * jnp.cos(omega)
    sine = neighborhood_extent * jnp.sin(omega)
    rows = jnp.arange(MODAL_DIMENSION)
    row_mode = rows // 2
    row_part = rows % 2
    partner = rows + 1 - 2 * row_part
    same = row_mode[:, None] == row_mode[None, :]
    cos_rows = cosine[:, row_mode][:, :, None]
    sin_rows = sine[:, row_mode][:, :, None]
    block = jnp.where(row_part[:, None] == row_part[None, :], cos_rows, jnp.where(row_part[:, None] < row_part[None, :], sin_rows, -sin_rows))
    rotation = jnp.where(same[None, :, :], block, 0.0)
    diag_val = cosine[:, row_mode]
    off_val = jnp.where(row_part[None, :] == 0, sine[:, row_mode], -sine[:, row_mode])
    amp = jnp.sqrt(jnp.float32(0.2) / (jnp.float32(MODAL_DIMENSION) * jnp.float32(FRAMES)))
    noise = jax.random.uniform(jax.random.fold_in(key, 7), (LEVELS, MODAL_DIMENSION, MODAL_DIMENSION), jnp.float32, -1.0, 1.0)
    upper = rows[:, None] < rows[None, :]
    lower = rows[:, None] > rows[None, :]
    skew = amp * jnp.where(upper[None, :, :], noise, jnp.where(lower[None, :, :], -jnp.transpose(noise, (0, 2, 1)), 0.0))
    skew_partner = jnp.take(skew, partner, axis=1)
    table = rotation + diag_val[:, :, None] * skew + off_val[:, :, None] * skew_partner
    return table.astype(jnp.float32)


def draw_gain(key, part):
    lagging_mode_choice, capture_frequency, base = mode_traits(key)
    row_rate = capture_frequency[jnp.arange(MODAL_DIMENSION) // 2]
    scale = jnp.sqrt(1.0 - row_rate * row_rate)
    raw = jax.random.normal(jax.random.fold_in(key, 8), (MODAL_DIMENSION, MODAL_DIMENSION), jnp.float32)
    return (scale[:, None] * raw / jnp.sqrt(jnp.float32(MODAL_DIMENSION))).astype(jnp.bfloat16)


def with_ends(entries, key, least, high):
    longest = entries.shape.index(max(entries.shape))
    spots = []
    for shift in (0, 1):
        where = [jax.random.randint(jax.random.fold_in(key, axis), (), 0, length) for axis, length in enumerate(entries.shape)]
        where[longest] = (where[longest] + shift) % entries.shape[longest]
        spots.append(tuple(where))
    return entries.at[spots[0]].set(least).at[spots[1]].set(high)


def shard_levels(key, dims, pieces, smallest, high):
    def one(dim, parts):
        steps = jax.random.uniform(jax.random.fold_in(jax.random.fold_in(key, 6), dim), (parts,), jnp.float32, smallest / len(pieces), high / len(pieces))
        return jnp.repeat(jnp.exp(steps), dims[dim] // parts).reshape((-1,) + (1,) * (len(dims) - dim - 1))

    level = one(*pieces[0])
    for cut in pieces[1:]:
        level = level * one(*cut)
    return level


def normal_values(own_key, shape, scale, bound, pieces=(), kind=jnp.bfloat16):
    result = jax.random.normal(own_key, shape, jnp.float32) * scale
    if len(pieces) > 0:
        result = shard_levels(own_key, shape, pieces, -0.22, 0.18) * result
    return jnp.clip(result, min=-bound, max=bound).astype(kind)


def setup_inputs(seed: int = 0, part: int = 0) -> dict:
    arg_keys = jax.random.split(jax.random.key(seed), 8)
    own_keys = jax.random.split(jax.random.fold_in(arg_keys[7], part), 8)
    frames = normal_values(own_keys[0], (PIX, FRAMES), 1.0, 6.0, ((0, 16),))
    levels = draw_levels(jax.random.fold_in(jax.random.fold_in(arg_keys[7], part), 71), part)
    initial_state = normal_values(own_keys[2], (MODAL_DIMENSION,), 1.0, 6.0, (), jnp.float32)
    transitions = draw_transitions(jax.random.fold_in(arg_keys[7], 71), part)
    gain = draw_gain(jax.random.fold_in(arg_keys[7], 71), part)
    pixel_mode = with_ends(jax.random.randint(arg_keys[5], (PIX,), 0, MODAL_DIMENSION), jax.random.fold_in(arg_keys[5], 1), 0, MODAL_DIMENSION - 1).astype(jnp.int32)
    pixel_weight = jnp.clip(jnp.exp(jax.random.uniform(arg_keys[6], (PIX,), jnp.float32, math.log(0.099609375), math.log(0.5))), 0.099609375, 0.5).astype(jnp.bfloat16)
    return {"frames": frames, "levels": levels, "initial_state": initial_state, "transitions": transitions, "gain": gain, "pixel_mode": pixel_mode, "pixel_weight": pixel_weight}


def reference(frames, levels, initial_state, transitions, gain, pixel_mode, pixel_weight):
    channels = jnp.arange(MODAL_DIMENSION, dtype=jnp.int32)
    projector = jnp.where(pixel_mode[None, :] == channels[:, None], pixel_weight[None, :], jnp.zeros((), jnp.bfloat16))
    measured = lax.dot_general(frames, projector, (((0,), (1,)), ((), ())), preferred_element_type=jnp.float32).astype(jnp.bfloat16)
    drive = lax.dot_general(measured, gain, (((1,), (1,)), ((), ())), preferred_element_type=jnp.float32)

    def advance(carried, inputs):
        tension, push = inputs
        moved = jnp.dot(transitions[tension], carried, precision=lax.Precision.HIGHEST) + push
        return moved, moved

    _, estimates = lax.scan(advance, initial_state, (levels, drive))
    return estimates
```

```python
import functools

import jax
import jax.numpy as jnp
from jax import lax
from jax.experimental import pallas as pl
from jax.experimental.pallas import tpu as pltpu
from jax.sharding import PartitionSpec as P

F32 = jnp.float32
BF16 = jnp.bfloat16
MIB = 1 << 20
NT = (((1,), (1,)), ((), ()))
VMEM = pl.BlockSpec(memory_space=pltpu.VMEM)
SMEM = pl.BlockSpec(memory_space=pltpu.SMEM)


def params(mib):
    return pltpu.CompilerParams(vmem_limit_bytes=mib * MIB)


def split3(x):
    high = x.astype(BF16)
    rest = x - high.astype(F32)
    mid = rest.astype(BF16)
    low = (rest - mid.astype(F32)).astype(BF16)
    return high, mid, low


def pair(x):
    high = x.astype(BF16)
    mid = (x - high.astype(F32)).astype(BF16)
    return jnp.concatenate([high, mid], axis=1)


def mm(left, right):
    lh, lm, ll = left
    rh, rm, rl = right
    wide = jnp.concatenate([rh, rm], axis=1)
    main = jnp.dot(
        jnp.concatenate([lh, lm], axis=1),
        jnp.concatenate([wide, wide], axis=0),
        preferred_element_type=F32,
    )
    rest = jnp.dot(
        jnp.concatenate([lh, ll], axis=1),
        jnp.concatenate([rl, rh], axis=0),
        preferred_element_type=F32,
    )
    n = rh.shape[1]
    return main[:, :n] + (main[:, n:] + rest)


def vm(vec, mat):
    high = vec.astype(BF16).astype(F32)
    rows = jnp.concatenate([high, vec - high], axis=0).astype(BF16)
    out = jnp.dot(rows, mat, preferred_element_type=F32)
    n = vec.shape[1]
    out = out[:, :n] + out[:, n:]
    return out[:8] + out[8:]


def transpose_kernel(frames_ref, out_ref):
    out_ref[...] = frames_ref[...].T


def tree_kernel(steps, levels_ref, trans_ref, left_ref, right_ref, table_ref, total_ref, tlow_ref, llow_ref, rlow_ref):
    kinds, n, _ = trans_ref.shape

    def prepare(k, c):
        high, mid, low = split3(trans_ref[k].T)
        table_ref[k] = jnp.concatenate([high, mid], axis=1)
        tlow_ref[k] = low
        return c

    lax.fori_loop(0, kinds, prepare, 0)

    def load(hm_ref, low_ref, k):
        hm = hm_ref[k]
        return hm[:, :n], hm[:, n:], low_ref[k]

    def store(hm_ref, low_ref, k, x):
        high, mid, low = split3(x)
        hm_ref[k] = jnp.concatenate([high, mid], axis=1)
        low_ref[k] = low

    def first(t):
        return mm(load(table_ref, tlow_ref, levels_ref[t]), load(table_ref, tlow_ref, levels_ref[t + 1]))

    def node(k):
        return mm(load(left_ref, llow_ref, k), load(right_ref, rlow_ref, k))

    base = steps // 4

    def first_pairs(ks):
        made = [(first(4 * k), first(4 * k + 2)) for k in ks]
        for k, (a, b) in zip(ks, made):
            store(left_ref, llow_ref, k, a)
            store(right_ref, rlow_ref, k, b)

    def later_pairs(ks):
        made = [(node(2 * (k - base)), node(2 * (k - base) + 1)) for k in ks]
        for k, (a, b) in zip(ks, made):
            store(left_ref, llow_ref, k, a)
            store(right_ref, rlow_ref, k, b)

    def loop(fn, start, count):
        def body(i, c):
            fn([start + 2 * i, start + 2 * i + 1])
            return c

        lax.fori_loop(0, count // 2, body, 0)

    loop(first_pairs, 0, base)
    count, start = base // 2, base
    while count >= 2:
        loop(later_pairs, start, count)
        start += count
        count //= 2
    later_pairs([start])
    total_ref[...] = node(start)


def group_kernel(size, pos_ref, *refs):
    maps = refs[:size]
    prefix_ref, whole_ref, all_ref = refs[size:]
    n = whole_ref.shape[0]
    member = pos_ref[0] % size
    for r in range(size):
        all_ref[(member + r) % size] = maps[r][...]
    prefix_ref[...] = pair((jax.lax.broadcasted_iota(jnp.int32, (n, n), 0) == jax.lax.broadcasted_iota(jnp.int32, (n, n), 1)).astype(F32))
    run = all_ref[0]
    for q in range(1, size):
        @pl.when(member == q)
        def _(run=run):
            prefix_ref[...] = pair(run)
        run = mm(split3(run), split3(all_ref[q]))
    whole_ref[...] = run


def row(ref, t):
    return jnp.broadcast_to(ref[pl.ds(t, 1), :], (8, ref.shape[1]))


def local_kernel(size, groups, pos_ref, levels_ref, x_ref, mode_ref, weight_ref, gain_ref, init_ref, table_ref, right_ref, total_ref, *refs):
    members = refs[: size - 1]
    wholes = refs[size - 1 : size - 1 + groups - 2]
    lefts_ref, sent_ref, drive_ref = refs[size - 1 + groups - 2 :]
    segments, steps, width = x_ref.shape
    n = gain_ref.shape[0]
    channel = lax.broadcasted_iota(jnp.int32, (n, width), 0)
    measured = jnp.zeros((steps, n), F32)
    for k in range(segments):
        weight = jnp.broadcast_to(weight_ref[pl.ds(k, 1), :].astype(F32), (n, width))
        projector = jnp.where(mode_ref[pl.ds(k, 1), :] == channel, weight, 0.0).astype(BF16)
        measured += lax.dot_general(x_ref[k], projector, NT, preferred_element_type=F32)
    drive_ref[...] = lax.dot_general(measured.astype(BF16), gain_ref[...], NT, preferred_element_type=F32)

    states = [row(drive_ref, t) for t in range(steps)]
    at, offset = 0, 0
    for level in range(steps.bit_length() - 1):
        later = []
        for i in range(len(states) // 2):
            mat = table_ref[levels_ref[2 * i + 1]] if level == 0 else right_ref[offset + i]
            lefts_ref[pl.ds(at + i, 1), :] = states[2 * i][:1]
            later.append(vm(states[2 * i], mat) + states[2 * i + 1])
        at += len(later)
        if level > 0:
            offset += len(later)
        states = later
    total = states[0]
    lefts_ref[pl.ds(at, 1), :] = total[:1]

    position = pos_ref[0]
    first = jnp.where(position == 0, row(init_ref, 0), 0.0)
    carried = total + vm(first, pair(total_ref[...]))
    sent_ref[...] = jnp.zeros_like(sent_ref)
    member = position % size
    group = position // size
    for r in range(1, size):
        @pl.when(member + r < size)
        def _(carried=carried, r=r):
            sent_ref[position + r] = carried[:1]
        carried = jnp.where(member + r < size, vm(carried, pair(members[r - 1][...])), carried)
    for r in range(1, groups):
        @pl.when(group + r < groups)
        def _(carried=carried, r=r):
            for q in range(size):
                sent_ref[(group + r) * size + q] = carried[:1]
        if r < groups - 1:
            carried = vm(carried, pair(wholes[r - 1][...]))


def final_kernel(size, pos_ref, levels_ref, got_ref, init_ref, prefix_ref, table_ref, left_ref, total_ref, lefts_ref, out_ref):
    steps, n = lefts_ref.shape
    position = pos_ref[0]
    start = position // size * size
    sender = lax.broadcasted_iota(jnp.int32, got_ref.shape, 0)
    got = got_ref[...]
    before = jnp.sum(jnp.where(sender < start, got, 0.0), axis=0)
    beside = jnp.sum(jnp.where(sender >= start, got, 0.0), axis=0)
    before = jnp.broadcast_to(before, (8, n))
    beside = jnp.broadcast_to(beside, (8, n))
    first = jnp.where(position == 0, row(init_ref, 0), 0.0)
    state = vm(before, prefix_ref[...]) + beside + first
    levels = steps.bit_length() - 1
    starts = [state]
    sizes = [steps >> (level + 1) for level in range(levels)]
    for level in reversed(range(levels)):
        at, offset = sum(sizes[:level]), sum(sizes[1:level])
        later = []
        for i, x in enumerate(starts):
            mat = table_ref[levels_ref[2 * i]] if level == 0 else left_ref[offset + i]
            later += [x, vm(x, mat) + row(lefts_ref, at + i)]
        starts = later
    for t in range(1, steps):
        out_ref[pl.ds(t - 1, 1), :] = starts[t][:1]
    out_ref[pl.ds(steps - 1, 1), :] = (vm(state, pair(total_ref[...])) + row(lefts_ref, steps - 1))[:1]


def shards(count, frames, levels, initial_state, transitions, gain, pixel_mode, pixel_weight):
    n = gain.shape[0]
    pixels, length = frames.shape
    steps = length // count
    size = 1
    while count % (2 * size) == 0 and 4 * size * size <= count:
        size *= 2
    groups = count // size
    position = lax.axis_index("tm").astype(jnp.int32)[None]
    initial_state = initial_state[None]
    pairs = steps // 2 - 1

    if pixels % 128 == 0:
        turned = pl.pallas_call(
            transpose_kernel,
            out_shape=jax.ShapeDtypeStruct((length, pixels), BF16),
            in_specs=[VMEM],
            out_specs=VMEM,
            compiler_params=params(16),
            name="turn_frames",
        )(frames).reshape(count, steps, pixels)
        x = lax.all_to_all(turned, "tm", split_axis=0, concat_axis=0, tiled=True)
    else:
        x = lax.all_to_all(frames, "tm", split_axis=1, concat_axis=0, tiled=True).T[None]
    mode = pixel_mode.reshape(x.shape[0], x.shape[2])
    weight = pixel_weight.reshape(x.shape[0], x.shape[2])

    left, right, table, total = pl.pallas_call(
        functools.partial(tree_kernel, steps),
        out_shape=[
            jax.ShapeDtypeStruct((pairs, n, 2 * n), BF16),
            jax.ShapeDtypeStruct((pairs, n, 2 * n), BF16),
            jax.ShapeDtypeStruct((transitions.shape[0], n, 2 * n), BF16),
            jax.ShapeDtypeStruct((n, n), F32),
        ],
        in_specs=[SMEM, VMEM],
        out_specs=[VMEM] * 4,
        scratch_shapes=[
            pltpu.VMEM((transitions.shape[0], n, n), BF16),
            pltpu.VMEM((pairs, n, n), BF16),
            pltpu.VMEM((pairs, n, n), BF16),
        ],
        compiler_params=params(32),
        name="tree_of_maps",
    )(levels, transitions)

    members = [
        lax.ppermute(total, "tm", [(j // size * size + (j + r) % size, j) for j in range(count)])
        for r in range(1, size)
    ]
    prefix, whole = pl.pallas_call(
        functools.partial(group_kernel, size),
        out_shape=[jax.ShapeDtypeStruct((n, 2 * n), BF16), jax.ShapeDtypeStruct((n, n), F32)],
        in_specs=[SMEM] + [VMEM] * size,
        out_specs=[VMEM] * 2,
        scratch_shapes=[pltpu.VMEM((size, n, n), F32)],
        compiler_params=params(16),
        name="group_maps",
    )(position, total, *members)
    wholes = [
        lax.ppermute(whole, "tm", [(j + r * size, j) for j in range(count - r * size)])
        for r in range(1, groups - 1)
    ]

    lefts, sent = pl.pallas_call(
        functools.partial(local_kernel, size, groups),
        out_shape=[jax.ShapeDtypeStruct((steps, n), F32), jax.ShapeDtypeStruct((count, 1, n), F32)],
        in_specs=[SMEM, SMEM] + [VMEM] * (8 + size - 1 + groups - 2),
        out_specs=[VMEM] * 2,
        scratch_shapes=[pltpu.VMEM((steps, n), F32)],
        compiler_params=params(32),
        name="local_states",
    )(position, levels, x, mode, weight, gain, initial_state, table, right, total, *members, *wholes)
    got = lax.all_to_all(sent, "tm", split_axis=0, concat_axis=0, tiled=True)
    return pl.pallas_call(
        functools.partial(final_kernel, size),
        out_shape=jax.ShapeDtypeStruct((steps, n), F32),
        in_specs=[SMEM, SMEM] + [VMEM] * 7,
        out_specs=VMEM,
        compiler_params=params(32),
        name="estimates",
    )(position, levels, got, initial_state, prefix, table, left, total, lefts)


def solution(mesh):
    in_specs = (P("tm", "parts"), P(("parts", "tm")), P("parts"), P(), P(), P(), P())
    out_specs = P(("parts", "tm"), None)
    return jax.shard_map(
        functools.partial(shards, mesh.shape["tm"]),
        mesh=mesh,
        in_specs=in_specs,
        out_specs=out_specs,
        check_vma=False,
    )
```

```python
import functools

import jax
import jax.numpy as jnp
from jax import lax
from jax.experimental import pallas as pl
from jax.experimental.pallas import tpu as pltpu
from jax.sharding import PartitionSpec as P

F32 = jnp.float32
BF16 = jnp.bfloat16
MIB = 1 << 20
NT = (((1,), (1,)), ((), ()))
VMEM = pl.BlockSpec(memory_space=pltpu.VMEM)
SMEM = pl.BlockSpec(memory_space=pltpu.SMEM)


def params(mib):
    return pltpu.CompilerParams(vmem_limit_bytes=mib * MIB)


def split3(x):
    high = x.astype(BF16)
    rest = x - high.astype(F32)
    mid = rest.astype(BF16)
    low = (rest - mid.astype(F32)).astype(BF16)
    return high, mid, low


def pair(x):
    high = x.astype(BF16)
    mid = (x - high.astype(F32)).astype(BF16)
    return jnp.concatenate([high, mid], axis=1)


def mm(left, right):
    lh, lm, ll = left
    rh, rm, rl = right
    wide = jnp.concatenate([rh, rm], axis=1)
    main = jnp.dot(
        jnp.concatenate([lh, lm], axis=1),
        jnp.concatenate([wide, wide], axis=0),
        preferred_element_type=F32,
    )
    rest = jnp.dot(
        jnp.concatenate([lh, ll], axis=1),
        jnp.concatenate([rl, rh], axis=0),
        preferred_element_type=F32,
    )
    n = rh.shape[1]
    return main[:, :n] + (main[:, n:] + rest)


def vm(vec, mat):
    high = vec.astype(BF16).astype(F32)
    rows = jnp.concatenate([high, vec - high], axis=0).astype(BF16)
    out = jnp.dot(rows, mat, preferred_element_type=F32)
    n = vec.shape[1]
    out = out[:, :n] + out[:, n:]
    return out[:8] + out[8:]


def transpose_kernel(frames_ref, out_ref):
    out_ref[...] = frames_ref[...].T


def tree_kernel(steps, levels_ref, trans_ref, left_ref, right_ref, table_ref, total_ref, tlow_ref, llow_ref, rlow_ref):
    kinds, n, _ = trans_ref.shape

    def prepare(k, c):
        high, mid, low = split3(trans_ref[k].T)
        table_ref[k] = jnp.concatenate([high, mid], axis=1)
        tlow_ref[k] = low
        return c

    lax.fori_loop(0, kinds, prepare, 0)

    def load(hm_ref, low_ref, k):
        hm = hm_ref[k]
        return hm[:, :n], hm[:, n:], low_ref[k]

    def store(hm_ref, low_ref, k, x):
        high, mid, low = split3(x)
        hm_ref[k] = jnp.concatenate([high, mid], axis=1)
        low_ref[k] = low

    def first(t):
        return mm(load(table_ref, tlow_ref, levels_ref[t]), load(table_ref, tlow_ref, levels_ref[t + 1]))

    def node(k):
        return mm(load(left_ref, llow_ref, k), load(right_ref, rlow_ref, k))

    base = steps // 4

    def first_pairs(ks):
        made = [(first(4 * k), first(4 * k + 2)) for k in ks]
        for k, (a, b) in zip(ks, made):
            store(left_ref, llow_ref, k, a)
            store(right_ref, rlow_ref, k, b)

    def later_pairs(ks):
        made = [(node(2 * (k - base)), node(2 * (k - base) + 1)) for k in ks]
        for k, (a, b) in zip(ks, made):
            store(left_ref, llow_ref, k, a)
            store(right_ref, rlow_ref, k, b)

    def loop(fn, start, count):
        def body(i, c):
            fn([start + 2 * i, start + 2 * i + 1])
            return c

        lax.fori_loop(0, count // 2, body, 0)

    loop(first_pairs, 0, base)
    count, start = base // 2, base
    while count >= 2:
        loop(later_pairs, start, count)
        start += count
        count //= 2
    later_pairs([start])
    total = node(start)
    for r in range(total_ref.shape[0]):
        total_ref[r] = total


def group_kernel(pos_ref, maps_ref, prefix_ref, whole_ref):
    size, n, _ = maps_ref.shape
    member = pos_ref[0] % size
    rows, cols = (lax.broadcasted_iota(jnp.int32, (n, n), d) for d in (0, 1))
    prefix_ref[...] = pair((rows == cols).astype(F32))
    run = maps_ref[0]
    for q in range(1, size):
        @pl.when(member == q)
        def _(run=run):
            prefix_ref[...] = pair(run)
        run = mm(split3(run), split3(maps_ref[q]))
    for r in range(whole_ref.shape[0]):
        whole_ref[r] = run


def row(ref, t):
    return jnp.broadcast_to(ref[pl.ds(t, 1), :], (8, ref.shape[1]))


def local_kernel(pos_ref, levels_ref, x_ref, mode_ref, weight_ref, gain_ref, init_ref, table_ref, right_ref, total_ref, members_ref, wholes_ref, lefts_ref, sent_ref, drive_ref):
    size, groups = members_ref.shape[0], wholes_ref.shape[0]
    segments, steps, width = x_ref.shape
    n = gain_ref.shape[0]
    channel = lax.broadcasted_iota(jnp.int32, (n, width), 0)
    measured = jnp.zeros((steps, n), F32)
    for k in range(segments):
        weight = jnp.broadcast_to(weight_ref[pl.ds(k, 1), :].astype(F32), (n, width))
        projector = jnp.where(mode_ref[pl.ds(k, 1), :] == channel, weight, 0.0).astype(BF16)
        measured += lax.dot_general(x_ref[k], projector, NT, preferred_element_type=F32)
    drive_ref[...] = lax.dot_general(measured.astype(BF16), gain_ref[...], NT, preferred_element_type=F32)

    states = [row(drive_ref, t) for t in range(steps)]
    at, offset = 0, 0
    for level in range(steps.bit_length() - 1):
        later = []
        for i in range(len(states) // 2):
            mat = table_ref[levels_ref[2 * i + 1]] if level == 0 else right_ref[offset + i]
            lefts_ref[pl.ds(at + i, 1), :] = states[2 * i][:1]
            later.append(vm(states[2 * i], mat) + states[2 * i + 1])
        at += len(later)
        if level > 0:
            offset += len(later)
        states = later
    total = states[0]
    lefts_ref[pl.ds(at, 1), :] = total[:1]

    position = pos_ref[0]
    first = jnp.where(position == 0, row(init_ref, 0), 0.0)
    carried = total + vm(first, pair(total_ref[0]))
    sent_ref[...] = jnp.zeros_like(sent_ref)
    member = position % size
    group = position // size
    for q in range(1, size):
        @pl.when(member < q)
        def _(carried=carried, q=q):
            sent_ref[group * size + q] = carried
        carried = jnp.where(member < q, vm(carried, pair(members_ref[q])), carried)
    for z in range(1, groups):
        @pl.when(group < z)
        def _(carried=carried, z=z):
            for q in range(size):
                sent_ref[z * size + q] = carried
        if z < groups - 1:
            carried = jnp.where(group < z, vm(carried, pair(wholes_ref[z])), carried)


def final_kernel(size, pos_ref, levels_ref, got_ref, init_ref, prefix_ref, table_ref, left_ref, total_ref, lefts_ref, out_ref):
    steps, n = lefts_ref.shape
    position = pos_ref[0]
    start = position // size * size
    sender = lax.broadcasted_iota(jnp.int32, got_ref.shape, 0)
    got = got_ref[...]
    before = jnp.sum(jnp.where(sender < start, got, 0.0), axis=0)
    beside = jnp.sum(jnp.where(sender >= start, got, 0.0), axis=0)
    first = jnp.where(position == 0, row(init_ref, 0), 0.0)
    state = vm(before, prefix_ref[...]) + beside + first
    levels = steps.bit_length() - 1
    starts = [state]
    sizes = [steps >> (level + 1) for level in range(levels)]
    for level in reversed(range(levels)):
        at, offset = sum(sizes[:level]), sum(sizes[1:level])
        later = []
        for i, x in enumerate(starts):
            mat = table_ref[levels_ref[2 * i]] if level == 0 else left_ref[offset + i]
            later += [x, vm(x, mat) + row(lefts_ref, at + i)]
        starts = later
    for t in range(1, steps):
        out_ref[pl.ds(t - 1, 1), :] = starts[t][:1]
    out_ref[pl.ds(steps - 1, 1), :] = (vm(state, pair(total_ref[0])) + row(lefts_ref, steps - 1))[:1]


def shards(count, frames, levels, initial_state, transitions, gain, pixel_mode, pixel_weight):
    n = gain.shape[0]
    pixels, length = frames.shape
    steps = length // count
    size = 1
    while count % (2 * size) == 0 and 4 * size * size <= count:
        size *= 2
    groups = count // size
    position = lax.axis_index("tm").astype(jnp.int32)[None]
    initial_state = initial_state[None]
    pairs = steps // 2 - 1

    if pixels % 128 == 0:
        turned = pl.pallas_call(
            transpose_kernel,
            out_shape=jax.ShapeDtypeStruct((length, pixels), BF16),
            in_specs=[VMEM],
            out_specs=VMEM,
            compiler_params=params(2),
            name="turn_frames",
        )(frames).reshape(count, steps, pixels)
        x = lax.all_to_all(turned, "tm", split_axis=0, concat_axis=0, tiled=True)
    else:
        x = lax.all_to_all(frames, "tm", split_axis=1, concat_axis=0, tiled=True).T[None]
    mode = pixel_mode.reshape(x.shape[0], x.shape[2])
    weight = pixel_weight.reshape(x.shape[0], x.shape[2])

    left, right, table, total = pl.pallas_call(
        functools.partial(tree_kernel, steps),
        out_shape=[
            jax.ShapeDtypeStruct((pairs, n, 2 * n), BF16),
            jax.ShapeDtypeStruct((pairs, n, 2 * n), BF16),
            jax.ShapeDtypeStruct((transitions.shape[0], n, 2 * n), BF16),
            jax.ShapeDtypeStruct((size, n, n), F32),
        ],
        in_specs=[SMEM, VMEM],
        out_specs=[VMEM] * 4,
        scratch_shapes=[
            pltpu.VMEM((transitions.shape[0], n, n), BF16),
            pltpu.VMEM((pairs, n, n), BF16),
            pltpu.VMEM((pairs, n, n), BF16),
        ],
        compiler_params=params(12),
        name="tree_of_maps",
    )(levels, transitions)

    beside = [[g * size + q for q in range(size)] for g in range(groups)]
    across = [[g * size + q for g in range(groups)] for q in range(size)]
    members = lax.all_to_all(total, "tm", 0, 0, axis_index_groups=beside, tiled=True)
    prefix, whole = pl.pallas_call(
        group_kernel,
        out_shape=[jax.ShapeDtypeStruct((n, 2 * n), BF16), jax.ShapeDtypeStruct((groups, n, n), F32)],
        in_specs=[SMEM, VMEM],
        out_specs=[VMEM] * 2,
        compiler_params=params(4),
        name="group_maps",
    )(position, members)
    wholes = lax.all_to_all(whole, "tm", 0, 0, axis_index_groups=across, tiled=True)

    lefts, sent = pl.pallas_call(
        local_kernel,
        out_shape=[jax.ShapeDtypeStruct((steps, n), F32), jax.ShapeDtypeStruct((count, 8, n), F32)],
        in_specs=[SMEM, SMEM] + [VMEM] * 10,
        out_specs=[VMEM] * 2,
        scratch_shapes=[pltpu.VMEM((steps, n), F32)],
        compiler_params=params(8),
        name="local_states",
    )(position, levels, x, mode, weight, gain, initial_state, table, right, total, members, wholes)
    got = lax.all_to_all(sent, "tm", split_axis=0, concat_axis=0, tiled=True)
    return pl.pallas_call(
        functools.partial(final_kernel, size),
        out_shape=jax.ShapeDtypeStruct((steps, n), F32),
        in_specs=[SMEM, SMEM] + [VMEM] * 7,
        out_specs=VMEM,
        compiler_params=params(8),
        name="estimates",
    )(position, levels, got, initial_state, prefix, table, left, total, lefts)


def solution(mesh):
    in_specs = (P("tm", "parts"), P(("parts", "tm")), P("parts"), P(), P(), P(), P())
    out_specs = P(("parts", "tm"), None)
    return jax.shard_map(
        functools.partial(shards, mesh.shape["tm"]),
        mesh=mesh,
        in_specs=in_specs,
        out_specs=out_specs,
        check_vma=False,
    )
```

```python
import functools

import jax
import jax.numpy as jnp
from jax import lax
from jax.experimental import pallas as pl
from jax.experimental.pallas import tpu as pltpu
from jax.sharding import PartitionSpec as P

F32 = jnp.float32
BF16 = jnp.bfloat16
MIB = 1 << 20
NT = (((1,), (1,)), ((), ()))
VMEM = pl.BlockSpec(memory_space=pltpu.VMEM)
SMEM = pl.BlockSpec(memory_space=pltpu.SMEM)
HBM = pl.BlockSpec(memory_space=pltpu.HBM)
ANY = pl.BlockSpec(memory_space=pl.ANY)
shape = jax.ShapeDtypeStruct


def call(kernel, name, mib, flops, moved, **kw):
    return pl.pallas_call(
        kernel,
        name=name,
        compiler_params=pltpu.CompilerParams(vmem_limit_bytes=mib * MIB),
        cost_estimate=pl.CostEstimate(flops=flops, bytes_accessed=moved, transcendentals=0),
        **kw,
    )


def pair(x):
    high = x.astype(BF16)
    mid = (x - high.astype(F32)).astype(BF16)
    return jnp.concatenate([high, mid], axis=1)


def mm(left, right):
    n = right.shape[0]
    out = jnp.dot(left, jnp.concatenate([right, right], axis=0), preferred_element_type=F32)
    return out[:, :n] + out[:, n:]


def mm3(left, left_low, right, right_low):
    n = right.shape[0]
    rest = jnp.dot(
        jnp.concatenate([left[:, :n], left_low], axis=1),
        jnp.concatenate([right_low, right[:, :n]], axis=0),
        preferred_element_type=F32,
    )
    return mm(left, right) + rest


def vm(vec, mat):
    high = vec.astype(BF16).astype(F32)
    rows = jnp.concatenate([high, vec - high], axis=0).astype(BF16)
    out = jnp.dot(rows, mat, preferred_element_type=F32)
    n = vec.shape[1]
    out = out[:, :n] + out[:, n:]
    return out[:8] + out[8:]


def row(ref, t):
    return jnp.broadcast_to(ref[pl.ds(t, 1), :], (8, ref.shape[1]))


def front_kernel(turn, trans_ref, *refs):
    if turn:
        frames_ref, table_ref, low_ref, turned_ref, trans, frames, turned, sems = refs
        into = pltpu.make_async_copy(frames_ref, frames, sems.at[0])
        into.start()
    else:
        table_ref, low_ref, trans, sems = refs
    maps = pltpu.make_async_copy(trans_ref, trans, sems.at[1])
    maps.start()
    if turn:
        into.wait()
        turned[...] = frames[...].T
        out = pltpu.make_async_copy(turned, turned_ref, sems.at[2])
        out.start()
    maps.wait()

    def prepare(k, c):
        x = trans[k].T
        both = pair(x)
        n = x.shape[0]
        table_ref[k] = both
        low_ref[k] = (x - both[:, :n].astype(F32) - both[:, n:].astype(F32)).astype(BF16)
        return c

    lax.fori_loop(0, trans.shape[0], prepare, 0)
    if turn:
        out.wait()


def tree_kernel(steps, levels_ref, table_ref, low_ref, left_hbm, right_hbm, total_ref, left_ref, right_ref, sems):
    base = steps // 4

    def first(t):
        a, b = levels_ref[0, t], levels_ref[0, t + 1]
        return mm3(table_ref[a], low_ref[a], table_ref[b], low_ref[b])

    def node(k):
        return mm(left_ref[k], right_ref[k])

    def first_pairs(ks):
        made = [(first(4 * k), first(4 * k + 2)) for k in ks]
        for k, (a, b) in zip(ks, made):
            left_ref[k] = pair(a)
            right_ref[k] = pair(b)

    def later_pairs(ks):
        made = [(node(2 * (k - base)), node(2 * (k - base) + 1)) for k in ks]
        for k, (a, b) in zip(ks, made):
            left_ref[k] = pair(a)
            right_ref[k] = pair(b)

    def loop(fn, start, count):
        def body(i, c):
            fn([start + 2 * i, start + 2 * i + 1])
            return c

        lax.fori_loop(0, count // 2, body, 0)

    def store(start, count, k):
        copies = [
            pltpu.make_async_copy(ref.at[pl.ds(start, count)], hbm.at[pl.ds(start, count)], sems.at[k + i])
            for i, (ref, hbm) in enumerate([(left_ref, left_hbm), (right_ref, right_hbm)])
        ]
        for copy in copies:
            copy.start()
        return copies

    loop(first_pairs, 0, base)
    copies = store(0, base, 0)
    count, start = base // 2, base
    while count >= 2:
        loop(later_pairs, start, count)
        start += count
        count //= 2
    later_pairs([start])
    copies += store(base, base - 1, 2)
    total_ref[...] = pair(node(start))
    for copy in copies:
        copy.wait()


def local_kernel(pos_ref, levels_ref, x_ref, mode_ref, weight_ref, gain_ref, init_ref, table_ref, total_ref, right_hbm, lefts_ref, shift_ref, drive_ref, right_ref, sems):
    segments, steps, width = x_ref.shape
    n = gain_ref.shape[0]
    base = steps // 4
    copies = [
        pltpu.make_async_copy(right_hbm.at[pl.ds(a, b)], right_ref.at[pl.ds(a, b)], sems.at[i])
        for i, (a, b) in enumerate([(0, base), (base, base - 1)])
    ]
    for copy in copies:
        copy.start()
    channel = lax.broadcasted_iota(jnp.int32, (n, width), 0)
    measured = jnp.zeros((steps, n), F32)
    for k in range(segments):
        weight = jnp.broadcast_to(weight_ref[pl.ds(k, 1), :].astype(F32), (n, width))
        projector = jnp.where(mode_ref[pl.ds(k, 1), :] == channel, weight, 0.0).astype(BF16)
        measured += lax.dot_general(x_ref[k], projector, NT, preferred_element_type=F32)
    drive_ref[...] = lax.dot_general(measured.astype(BF16), gain_ref[...], NT, preferred_element_type=F32)

    states = [row(drive_ref, t) for t in range(steps)]
    at, offset = 0, 0
    for level in range(steps.bit_length() - 1):
        if level in (1, 2):
            copies[level - 1].wait()
        later = []
        for i in range(len(states) // 2):
            mat = table_ref[levels_ref[0, 2 * i + 1]] if level == 0 else right_ref[offset + i]
            lefts_ref[pl.ds(at + i, 1), :] = states[2 * i][:1]
            later.append(vm(states[2 * i], mat) + states[2 * i + 1])
        at += len(later)
        if level > 0:
            offset += len(later)
        states = later
    lefts_ref[pl.ds(at, 1), :] = states[0][:1]
    first = jnp.where(pos_ref[0] == 0, row(init_ref, 0), 0.0)
    shift_ref[...] = states[0] + vm(first, total_ref[...])


def group_kernel(size, pos_ref, *refs):
    maps = refs[:size]
    all_ref, prefix_ref, whole_ref = refs[size:]
    n = whole_ref.shape[0]
    member = pos_ref[0] % size
    for r in range(size):
        all_ref[(member + r) % size] = maps[r][...]
    rows, cols = (lax.broadcasted_iota(jnp.int32, (n, n), d) for d in (0, 1))
    prefix_ref[...] = pair((rows == cols).astype(F32))
    run = all_ref[0]
    for q in range(1, size):
        @pl.when(member == q)
        def _(run=run):
            prefix_ref[...] = run
        run = pair(mm(run, all_ref[q]))
    whole_ref[...] = run


def beside_kernel(size, pos_ref, all_ref, *refs):
    shifts = refs[:size]
    before_ref, whole_ref, held_ref = refs[size:]
    member = pos_ref[0] % size
    for r in range(size):
        held_ref[(member + r) % size] = shifts[r][...]
    before_ref[...] = jnp.zeros_like(before_ref)
    run = held_ref[0]
    for q in range(1, size):
        @pl.when(member == q)
        def _(run=run):
            before_ref[...] = run
        run = vm(run, all_ref[q]) + held_ref[q]
    whole_ref[...] = run


def hop_kernel(got_ref, map_ref, shift_ref, out_ref):
    out_ref[...] = vm(got_ref[...], map_ref[...]) + shift_ref[...]


def final_kernel(pos_ref, levels_ref, got_ref, before_ref, init_ref, prefix_ref, table_ref, total_ref, lefts_ref, left_hbm, out_ref, left_ref, sems):
    steps, n = lefts_ref.shape
    base = steps // 4
    copies = [
        pltpu.make_async_copy(left_hbm.at[pl.ds(a, b)], left_ref.at[pl.ds(a, b)], sems.at[i])
        for i, (a, b) in enumerate([(base, base - 1), (0, base)])
    ]
    for copy in copies:
        copy.start()
    first = jnp.where(pos_ref[0] == 0, row(init_ref, 0), 0.0)
    state = vm(got_ref[...], prefix_ref[...]) + before_ref[...] + first
    out_ref[pl.ds(steps - 1, 1), :] = (vm(state, total_ref[...]) + row(lefts_ref, steps - 1))[:1]
    levels = steps.bit_length() - 1
    starts = [state]
    sizes = [steps >> (level + 1) for level in range(levels)]
    for level in reversed(range(levels)):
        if level == levels - 1:
            copies[0].wait()
        if level == 1:
            copies[1].wait()
        at, offset = sum(sizes[:level]), sum(sizes[1:level])
        later = []
        for i, x in enumerate(starts):
            mat = table_ref[levels_ref[0, 2 * i]] if level == 0 else left_ref[offset + i]
            later += [x, vm(x, mat) + row(lefts_ref, at + i)]
        starts = later
    for t in range(1, steps):
        out_ref[pl.ds(t - 1, 1), :] = starts[t][:1]


def shards(count, frames, levels, initial_state, transitions, gain, pixel_mode, pixel_weight):
    n = gain.shape[0]
    kinds = transitions.shape[0]
    pixels, length = frames.shape
    steps = length // count
    size = 1
    while count % (2 * size) == 0 and 4 * size * size <= count:
        size *= 2
    groups = count // size
    position = lax.axis_index("tm").astype(jnp.int32)[None]
    initial_state = initial_state[None]
    levels = levels[None]
    pairs = steps // 2 - 1
    turn = pixels % 128 == 0

    tables = [shape((kinds, n, 2 * n), BF16), shape((kinds, n, n), BF16)]
    trans = pltpu.VMEM(transitions.shape, F32)
    dma = pltpu.SemaphoreType.DMA
    if turn:
        table, low, turned = call(
            functools.partial(front_kernel, turn), "front", 5, 0, 6 * MIB,
            out_shape=tables + [shape((length, pixels), BF16)],
            in_specs=[HBM, HBM],
            out_specs=[VMEM, VMEM, HBM],
            scratch_shapes=[trans, pltpu.VMEM(frames.shape, BF16), pltpu.VMEM((length, pixels), BF16), dma((3,))],
        )(transitions, frames)
        turned = turned.reshape(count, steps, pixels)
        x = lax.all_to_all(turned, "tm", split_axis=0, concat_axis=0, tiled=True)
    else:
        table, low = call(
            functools.partial(front_kernel, turn), "front", 5, 0, 6 * MIB,
            out_shape=tables,
            in_specs=[HBM],
            out_specs=[VMEM, VMEM],
            scratch_shapes=[trans, dma((2,))],
        )(transitions)
        x = lax.all_to_all(frames, "tm", split_axis=1, concat_axis=0, tiled=True).T[None]
    mode = pixel_mode.reshape(x.shape[0], x.shape[2])
    weight = pixel_weight.reshape(x.shape[0], x.shape[2])

    tree = pltpu.VMEM((pairs, n, 2 * n), BF16)
    left, right, total = call(
        functools.partial(tree_kernel, steps), "tree_of_maps", 8, 2 * steps * n**3 * 6, 8 * MIB,
        out_shape=[shape((pairs, n, 2 * n), BF16), shape((pairs, n, 2 * n), BF16), shape((n, 2 * n), BF16)],
        in_specs=[SMEM, VMEM, VMEM],
        out_specs=[HBM, HBM, VMEM],
        scratch_shapes=[tree, tree, dma((4,))],
    )(levels, table, low)

    def around(x):
        return [
            lax.ppermute(x, "tm", [(j // size * size + (j + r) % size, j) for j in range(count)])
            for r in range(1, size)
        ]

    members = around(total)
    lefts, shift = call(
        local_kernel, "local_states", 6, 1 << 27, 6 * MIB,
        out_shape=[shape((steps, n), F32), shape((8, n), F32)],
        in_specs=[SMEM, SMEM] + [VMEM] * 7 + [HBM],
        out_specs=[VMEM] * 2,
        scratch_shapes=[pltpu.VMEM((steps, n), F32), tree, dma((2,))],
    )(position, levels, x, mode, weight, gain, initial_state, table, total, right)

    vector = shape((8, n), F32)
    maps, prefix, whole = call(
        functools.partial(group_kernel, size), "group_maps", 2, 1 << 24, MIB,
        out_shape=[shape((size, n, 2 * n), BF16), shape((n, 2 * n), BF16), shape((n, 2 * n), BF16)],
        in_specs=[SMEM] + [VMEM] * size,
        out_specs=[VMEM] * 3,
    )(position, total, *members)
    before, carried = call(
        functools.partial(beside_kernel, size), "group_states", 2, 1 << 20, MIB // 4,
        out_shape=[vector, vector],
        in_specs=[SMEM] + [VMEM] * (1 + size),
        out_specs=[VMEM] * 2,
        scratch_shapes=[pltpu.VMEM((size, 8, n), F32)],
    )(position, maps, shift, *around(shift))
    sent = carried
    for hop in range(groups - 1):
        got = lax.ppermute(sent, "tm", [(j, j + size) for j in range(count - size)])
        if hop < groups - 2:
            sent = call(
                hop_kernel, "next_group", 2, 1 << 18, 1 << 16,
                out_shape=vector,
                in_specs=[VMEM] * 3,
                out_specs=VMEM,
            )(got, whole, carried)

    return call(
        final_kernel, "estimates", 5, 1 << 23, 5 * MIB,
        out_shape=shape((steps, n), F32),
        in_specs=[SMEM, SMEM] + [VMEM] * 7 + [HBM],
        out_specs=VMEM,
        scratch_shapes=[tree, dma((2,))],
    )(position, levels, got, before, initial_state, prefix, table, total, lefts, left)


def solution(mesh):
    in_specs = (P("tm", "parts"), P(("parts", "tm")), P("parts"), P(), P(), P(), P())
    out_specs = P(("parts", "tm"), None)
    return jax.shard_map(
        functools.partial(shards, mesh.shape["tm"]),
        mesh=mesh,
        in_specs=in_specs,
        out_specs=out_specs,
        check_vma=False,
    )
```

```python
import functools

import jax
import jax.numpy as jnp
from jax import lax
from jax.experimental import pallas as pl
from jax.experimental.pallas import tpu as pltpu
from jax.sharding import PartitionSpec as P

F32 = jnp.float32
BF16 = jnp.bfloat16
MIB = 1 << 20
BIG, SMALL = 60, 2
NT = (((1,), (1,)), ((), ()))
VMEM = pl.BlockSpec(memory_space=pltpu.VMEM)
SMEM = pl.BlockSpec(memory_space=pltpu.SMEM)
HBM = pl.BlockSpec(memory_space=pltpu.HBM)
shape = jax.ShapeDtypeStruct


def call(kernel, name, mib, flops, moved, **kw):
    return pl.pallas_call(
        kernel,
        name=name,
        compiler_params=pltpu.CompilerParams(vmem_limit_bytes=mib * MIB),
        cost_estimate=pl.CostEstimate(flops=flops, bytes_accessed=moved, transcendentals=0),
        **kw,
    )


def pair(x):
    high = x.astype(BF16)
    mid = (x - high.astype(F32)).astype(BF16)
    return jnp.concatenate([high, mid], axis=1)


def mm(left, right):
    n = right.shape[0]
    out = jnp.dot(left, jnp.concatenate([right, right], axis=0), preferred_element_type=F32)
    return out[:, :n] + out[:, n:]


def vm(vec, mat):
    high = vec.astype(BF16).astype(F32)
    rows = jnp.concatenate([high, vec - high], axis=0).astype(BF16)
    out = jnp.dot(rows, mat, preferred_element_type=F32)
    n = vec.shape[1]
    out = out[:, :n] + out[:, n:]
    return out[:8] + out[8:]


def row(ref, t):
    return jnp.broadcast_to(ref[pl.ds(t, 1), :], (8, ref.shape[1]))


def front_kernel(frames_ref, turned_ref, frames, turned, sems):
    into = pltpu.make_async_copy(frames_ref, frames, sems.at[0])
    into.start()
    into.wait()
    turned[...] = frames[...].T
    out = pltpu.make_async_copy(turned, turned_ref, sems.at[1])
    out.start()
    out.wait()


def tree_kernel(steps, levels_ref, trans_ref, left_hbm, right_hbm, table_hbm, total_ref, trans, table_ref, left_ref, right_ref, sems):
    base = steps // 4
    kinds = trans_ref.shape[0]
    cuts = [(k, kinds // 4) for k in range(0, kinds, kinds // 4)]
    ins = [
        pltpu.make_async_copy(trans_ref.at[pl.ds(a, b)], trans.at[pl.ds(a, b)], sems.at[5 + i])
        for i, (a, b) in enumerate(cuts)
    ]
    for copy in ins:
        copy.start()

    def prepare(k, c):
        table_ref[k] = pair(trans[k].T)
        return c

    for copy, (a, b) in zip(ins, cuts):
        copy.wait()
        lax.fori_loop(a, a + b, prepare, 0)

    def first(t):
        return mm(table_ref[levels_ref[0, t]], table_ref[levels_ref[0, t + 1]])

    def node(k):
        return mm(left_ref[k], right_ref[k])

    def first_pairs(ks):
        made = [(first(4 * k), first(4 * k + 2)) for k in ks]
        for k, (a, b) in zip(ks, made):
            left_ref[k] = pair(a)
            right_ref[k] = pair(b)

    def later_pairs(ks):
        made = [(node(2 * (k - base)), node(2 * (k - base) + 1)) for k in ks]
        for k, (a, b) in zip(ks, made):
            left_ref[k] = pair(a)
            right_ref[k] = pair(b)

    def loop(fn, start, count):
        def body(i, c):
            fn([start + 2 * i, start + 2 * i + 1])
            return c

        lax.fori_loop(0, count // 2, body, 0)

    def store(start, count, k):
        copies = [
            pltpu.make_async_copy(ref.at[pl.ds(start, count)], hbm.at[pl.ds(start, count)], sems.at[k + i])
            for i, (ref, hbm) in enumerate([(left_ref, left_hbm), (right_ref, right_hbm)])
        ]
        for copy in copies:
            copy.start()
        return copies

    keep = pltpu.make_async_copy(table_ref, table_hbm, sems.at[4])
    keep.start()
    loop(first_pairs, 0, base)
    copies = store(0, base, 0)
    count, start = base // 2, base
    while count >= 2:
        loop(later_pairs, start, count)
        start += count
        count //= 2
    later_pairs([start])
    copies += store(base, base - 1, 2)
    total_ref[...] = pair(node(start))
    for copy in copies + [keep]:
        copy.wait()


def fetch(pieces, sems):
    copies = [
        pltpu.make_async_copy(hbm.at[pl.ds(a, b)], ref.at[pl.ds(a, b)], sems.at[i])
        for i, (hbm, ref, a, b) in enumerate(pieces)
    ]
    for copy in copies:
        copy.start()
    return copies


def local_kernel(pos_ref, levels_ref, x_ref, mode_ref, weight_ref, gain_ref, init_ref, total_ref, table_hbm, right_hbm, lefts_ref, own_ref, drive_ref, table_ref, right_ref, sems):
    segments, steps, width = x_ref.shape
    n = gain_ref.shape[0]
    base = steps // 4
    copies = fetch(
        [(table_hbm, table_ref, 0, table_ref.shape[0]), (right_hbm, right_ref, 0, base), (right_hbm, right_ref, base, base - 1)],
        sems,
    )
    channel = lax.broadcasted_iota(jnp.int32, (n, width), 0)
    measured = jnp.zeros((steps, n), F32)
    for k in range(segments):
        weight = jnp.broadcast_to(weight_ref[pl.ds(k, 1), :].astype(F32), (n, width))
        projector = jnp.where(mode_ref[pl.ds(k, 1), :] == channel, weight, 0.0).astype(BF16)
        measured += lax.dot_general(x_ref[k], projector, NT, preferred_element_type=F32)
    drive_ref[...] = lax.dot_general(measured.astype(BF16), gain_ref[...], NT, preferred_element_type=F32)

    states = [row(drive_ref, t) for t in range(steps)]
    at, offset = 0, 0
    for level in range(steps.bit_length() - 1):
        if level < 3:
            copies[level].wait()
        later = []
        for i in range(len(states) // 2):
            mat = table_ref[levels_ref[0, 2 * i + 1]] if level == 0 else right_ref[offset + i]
            lefts_ref[pl.ds(at + i, 1), :] = states[2 * i][:1]
            later.append(vm(states[2 * i], mat) + states[2 * i + 1])
        at += len(later)
        if level > 0:
            offset += len(later)
        states = later
    lefts_ref[pl.ds(at, 1), :] = states[0][:1]
    first = jnp.where(pos_ref[0] == 0, row(init_ref, 0), 0.0)
    total = total_ref[...]
    own_ref[pl.ds(0, n), :] = total
    own_ref[pl.ds(n, 16), :] = rows16(states[0] + vm(first, total))


def rows16(vec):
    high = vec.astype(BF16).astype(F32)
    both = jnp.concatenate([high, vec - high], axis=1)
    return jnp.concatenate([both, both], axis=0).astype(BF16)


def rows8(ref, start, n):
    both = ref[pl.ds(start, 16), :].astype(F32)
    return both[:8, :n] + both[:8, n:]


def join_kernel(bit, pos_ref, own_ref, got_ref, *refs):
    out_ref, map_ref, before_ref = refs[-3:]
    n = own_ref.shape[1] // 2
    upper = pos_ref[0] & bit != 0
    own, got = own_ref[pl.ds(0, n), :], got_ref[pl.ds(0, n), :]
    own_shift, got_shift = rows8(own_ref, n, n), rows8(got_ref, n, n)
    early, late = jnp.where(upper, got, own), jnp.where(upper, own, got)
    early_shift, late_shift = jnp.where(upper, got_shift, own_shift), jnp.where(upper, own_shift, got_shift)
    out_ref[pl.ds(0, n), :] = pair(mm(early, late))
    out_ref[pl.ds(n, 16), :] = rows16(vm(early_shift, late) + late_shift)
    if bit == 1:
        rows, cols = (lax.broadcasted_iota(jnp.int32, (n, n), d) for d in (0, 1))
        eye = pair((rows == cols).astype(F32))
        map_ref[...] = jnp.where(upper, got, eye)
        before_ref[...] = jnp.where(upper, got_shift, 0.0)
    else:
        last_map, last_before = refs[0][...], refs[1][...]
        map_ref[...] = jnp.where(upper, pair(mm(got, last_map)), last_map)
        before_ref[...] = last_before + jnp.where(upper, vm(got_shift, last_map), 0.0)


def final_kernel(bit, pos_ref, levels_ref, got_ref, before_ref, init_ref, map_ref, total_ref, lefts_ref, left_hbm, table_hbm, out_ref, left_ref, table_ref, sems):
    steps, n = lefts_ref.shape
    base = steps // 4
    copies = fetch(
        [(left_hbm, left_ref, base, base - 1), (left_hbm, left_ref, 0, base), (table_hbm, table_ref, 0, table_ref.shape[0])],
        sems,
    )
    first = jnp.where(pos_ref[0] == 0, row(init_ref, 0), 0.0)
    moved = vm(rows8(got_ref, 0, n), map_ref[...])
    state = before_ref[...] + first + jnp.where(pos_ref[0] & bit != 0, moved, 0.0)
    out_ref[pl.ds(steps - 1, 1), :] = (vm(state, total_ref[...]) + row(lefts_ref, steps - 1))[:1]
    levels = steps.bit_length() - 1
    starts = [state]
    sizes = [steps >> (level + 1) for level in range(levels)]
    for level in reversed(range(levels)):
        if level == levels - 1:
            copies[0].wait()
        if level < 2:
            copies[2 - level].wait()
        at, offset = sum(sizes[:level]), sum(sizes[1:level])
        later = []
        for i, x in enumerate(starts):
            mat = table_ref[levels_ref[0, 2 * i]] if level == 0 else left_ref[offset + i]
            later += [x, vm(x, mat) + row(lefts_ref, at + i)]
        starts = later
    for t in range(1, steps):
        out_ref[pl.ds(t - 1, 1), :] = starts[t][:1]


def shards(count, frames, levels, initial_state, transitions, gain, pixel_mode, pixel_weight):
    n = gain.shape[0]
    kinds = transitions.shape[0]
    pixels, length = frames.shape
    steps = length // count
    position = lax.axis_index("tm").astype(jnp.int32)[None]
    initial_state = initial_state[None]
    levels = levels[None]
    pairs = steps // 2 - 1
    dma = pltpu.SemaphoreType.DMA

    if pixels % 128 == 0:
        turned = call(
            front_kernel, "turn_frames", BIG, 0, MIB,
            out_shape=shape((length, pixels), BF16),
            in_specs=[HBM],
            out_specs=HBM,
            scratch_shapes=[pltpu.VMEM(frames.shape, BF16), pltpu.VMEM((length, pixels), BF16), dma((2,))],
        )(frames).reshape(count, steps, pixels)
        x = lax.all_to_all(turned, "tm", split_axis=0, concat_axis=0, tiled=True)
    else:
        x = lax.all_to_all(frames, "tm", split_axis=1, concat_axis=0, tiled=True).T[None]
    mode = pixel_mode.reshape(x.shape[0], x.shape[2])
    weight = pixel_weight.reshape(x.shape[0], x.shape[2])

    tree = pltpu.VMEM((pairs, n, 2 * n), BF16)
    table_vmem = pltpu.VMEM((kinds, n, 2 * n), BF16)
    maps = shape((pairs, n, 2 * n), BF16)
    one_map = shape((n, 2 * n), BF16)
    left, right, table, total = call(
        functools.partial(tree_kernel, steps), "tree_of_maps", BIG, 2 * steps * n**3 * 4, 8 * MIB,
        out_shape=[maps, maps, shape((kinds, n, 2 * n), BF16), one_map],
        in_specs=[SMEM, HBM],
        out_specs=[HBM, HBM, HBM, VMEM],
        scratch_shapes=[pltpu.VMEM(transitions.shape, F32), table_vmem, tree, tree, dma((9,))],
    )(levels, transitions)

    lefts, own = call(
        local_kernel, "local_states", BIG, 1 << 27, 6 * MIB,
        out_shape=[shape((steps, n), F32), shape((n + 16, 2 * n), BF16)],
        in_specs=[SMEM, SMEM] + [VMEM] * 6 + [HBM] * 2,
        out_specs=[VMEM] * 2,
        scratch_shapes=[pltpu.VMEM((steps, n), F32), table_vmem, tree, dma((3,))],
    )(position, levels, x, mode, weight, gain, initial_state, total, table, right)

    def swap(x, bit):
        return lax.ppermute(x, "tm", [(j, j ^ bit) for j in range(count)])

    bit, kept = 1, []
    while 2 * bit < count:
        own, *kept = call(
            functools.partial(join_kernel, bit), "join_halves", SMALL, 1 << 25, MIB // 2,
            out_shape=[shape((n + 16, 2 * n), BF16), one_map, shape((8, n), F32)],
            in_specs=[SMEM] + [VMEM] * (2 + len(kept)),
            out_specs=[VMEM] * 3,
        )(position, own, swap(own, bit), *kept)
        bit *= 2
    got = swap(own[n:], bit)
    prefix, before = kept

    return call(
        functools.partial(final_kernel, bit), "estimates", BIG, 1 << 23, 5 * MIB,
        out_shape=shape((steps, n), F32),
        in_specs=[SMEM, SMEM] + [VMEM] * 6 + [HBM] * 2,
        out_specs=VMEM,
        scratch_shapes=[tree, table_vmem, dma((3,))],
    )(position, levels, got, before, initial_state, prefix, total, lefts, left, table)


def solution(mesh):
    in_specs = (P("tm", "parts"), P(("parts", "tm")), P("parts"), P(), P(), P(), P())
    out_specs = P(("parts", "tm"), None)
    return jax.shard_map(
        functools.partial(shards, mesh.shape["tm"]),
        mesh=mesh,
        in_specs=in_specs,
        out_specs=out_specs,
        check_vma=False,
    )
```

```python
import functools

import jax
import jax.numpy as jnp
from jax import lax
from jax.experimental import pallas as pl
from jax.experimental.pallas import tpu as pltpu
from jax.sharding import PartitionSpec as P

F32 = jnp.float32
BF16 = jnp.bfloat16
MIB = 1 << 20
BIG, SMALL = 60, 2
NT = (((1,), (1,)), ((), ()))
VMEM = pl.BlockSpec(memory_space=pltpu.VMEM)
SMEM = pl.BlockSpec(memory_space=pltpu.SMEM)
HBM = pl.BlockSpec(memory_space=pltpu.HBM)
shape = jax.ShapeDtypeStruct


def call(kernel, name, mib, flops, moved, **kw):
    return pl.pallas_call(
        kernel,
        name=name,
        compiler_params=pltpu.CompilerParams(vmem_limit_bytes=mib * MIB),
        cost_estimate=pl.CostEstimate(flops=flops, bytes_accessed=moved, transcendentals=0),
        **kw,
    )


def pair(x):
    high = x.astype(BF16)
    mid = (x - high.astype(F32)).astype(BF16)
    return jnp.concatenate([high, mid], axis=1)


def mm(left, right):
    n = right.shape[0]
    out = jnp.dot(left, jnp.concatenate([right, right], axis=0), preferred_element_type=F32)
    return out[:, :n] + out[:, n:]


def vm(vec, mat):
    high = vec.astype(BF16).astype(F32)
    rows = jnp.concatenate([high, vec - high], axis=0).astype(BF16)
    out = jnp.dot(rows, mat, preferred_element_type=F32)
    n = vec.shape[1]
    out = out[:, :n] + out[:, n:]
    return out[:8] + out[8:]


def row(ref, t):
    return jnp.broadcast_to(ref[pl.ds(t, 1), :], (8, ref.shape[1]))


def front_kernel(frames_ref, turned_ref, frames, turned, sems):
    into = pltpu.make_async_copy(frames_ref, frames, sems.at[0])
    into.start()
    into.wait()
    turned[...] = frames[...].T
    out = pltpu.make_async_copy(turned, turned_ref, sems.at[1])
    out.start()
    out.wait()


def tree_kernel(steps, levels_ref, trans_ref, left_hbm, right_hbm, table_hbm, total_ref, trans, table_ref, left_ref, right_ref, sems):
    base = steps // 4
    kinds = trans_ref.shape[0]
    cuts = [(k, kinds // 4) for k in range(0, kinds, kinds // 4)]
    ins = [
        pltpu.make_async_copy(trans_ref.at[pl.ds(a, b)], trans.at[pl.ds(a, b)], sems.at[7 + i])
        for i, (a, b) in enumerate(cuts)
    ]
    for copy in ins:
        copy.start()

    for copy, (a, b) in zip(ins, cuts):
        copy.wait()
        for k in range(a, a + b):
            table_ref[k] = pair(trans[k].T)

    def first(t):
        return mm(table_ref[levels_ref[0, t]], table_ref[levels_ref[0, t + 1]])

    def node(k):
        return mm(left_ref[k], right_ref[k])

    def first_pairs(ks):
        made = [(first(4 * k), first(4 * k + 2)) for k in ks]
        for k, (a, b) in zip(ks, made):
            left_ref[k] = pair(a)
            right_ref[k] = pair(b)

    def later_pairs(ks):
        made = [(node(2 * (k - base)), node(2 * (k - base) + 1)) for k in ks]
        for k, (a, b) in zip(ks, made):
            left_ref[k] = pair(a)
            right_ref[k] = pair(b)

    def run(fn, start, count):
        if count <= 4:
            fn(list(range(start, start + count)))
            return

        def body(i, c):
            fn([start + 4 * i + k for k in range(4)])
            return c

        lax.fori_loop(0, count // 4, body, 0)

    copies = [pltpu.make_async_copy(table_ref, table_hbm, sems.at[0])]
    copies[0].start()

    def store(start, count):
        for ref, hbm in ((right_ref, right_hbm), (left_ref, left_hbm)):
            part = pl.ds(start, count)
            copies.append(pltpu.make_async_copy(ref.at[part], hbm.at[part], sems.at[len(copies)]))
            copies[-1].start()

    run(first_pairs, 0, base)
    store(0, base)
    run(later_pairs, base, base // 2)
    store(base, base // 2)
    count, start = base // 4, base + base // 2
    while count >= 1:
        run(later_pairs, start, count)
        start += count
        count //= 2
    store(base + base // 2, base // 2 - 1)
    total_ref[...] = pair(node(start - 1))
    for copy in copies:
        copy.wait()


def fetch(pieces, sems):
    copies = [
        pltpu.make_async_copy(hbm.at[pl.ds(a, b)], ref.at[pl.ds(a, b)], sems.at[i])
        for i, (hbm, ref, a, b) in enumerate(pieces)
    ]
    for copy in copies:
        copy.start()
    return copies


def local_kernel(pos_ref, levels_ref, *refs):
    hbm, (lefts_ref, shift_ref), (drive_ref, sems), vmem = refs[:8], refs[8:10], refs[10:12], refs[12:]
    x_ref, mode_ref, weight_ref, gain_ref, init_ref, total_ref, table_ref, right_ref = vmem
    segments, steps, width = x_ref.shape
    n = gain_ref.shape[0]
    base = steps // 4
    whole = [(a, b, 0, b.shape[0]) for a, b in zip(hbm[:7], vmem[:7])]
    copies = fetch(whole + [(hbm[7], right_ref, 0, base), (hbm[7], right_ref, base, base - 1)], sems)
    for copy in copies[:6]:
        copy.wait()
    channel = lax.broadcasted_iota(jnp.int32, (n, width), 0)
    measured = jnp.zeros((steps, n), F32)
    for k in range(segments):
        weight = jnp.broadcast_to(weight_ref[pl.ds(k, 1), :].astype(F32), (n, width))
        projector = jnp.where(mode_ref[pl.ds(k, 1), :] == channel, weight, 0.0).astype(BF16)
        measured += lax.dot_general(x_ref[k], projector, NT, preferred_element_type=F32)
    drive_ref[...] = lax.dot_general(measured.astype(BF16), gain_ref[...], NT, preferred_element_type=F32)

    states = [row(drive_ref, t) for t in range(steps)]
    at, offset = 0, 0
    for level in range(steps.bit_length() - 1):
        if level < 3:
            copies[6 + level].wait()
        later = []
        for i in range(len(states) // 2):
            mat = table_ref[levels_ref[0, 2 * i + 1]] if level == 0 else right_ref[offset + i]
            lefts_ref[pl.ds(at + i, 1), :] = states[2 * i][:1]
            later.append(vm(states[2 * i], mat) + states[2 * i + 1])
        at += len(later)
        if level > 0:
            offset += len(later)
        states = later
    lefts_ref[pl.ds(at, 1), :] = states[0][:1]
    first = jnp.where(pos_ref[0] == 0, row(init_ref, 0), 0.0)
    shift_ref[...] = states[0] + vm(first, total_ref[...])


def group_kernel(size, pos_ref, shift_ref, *refs):
    maps = refs[:size]
    prefix_ref, whole_ref, sent_ref, all_ref = refs[size:]
    n = whole_ref.shape[0]
    position = pos_ref[0]
    member = position % size
    for r in range(size):
        all_ref[(member + r) % size] = maps[r][...]
    rows, cols = (lax.broadcasted_iota(jnp.int32, (n, n), d) for d in (0, 1))
    sent_ref[...] = jnp.zeros_like(sent_ref)
    prefix = pair((rows == cols).astype(F32))
    run, vec = all_ref[0], shift_ref[...]
    for q in range(1, size):
        prefix = jnp.where(member == q, run, prefix)
        sent_ref[position - member + q] = jnp.where(member < q, vec, 0.0)[:1]
        vec = jnp.where(member < q, vm(vec, all_ref[q]), vec)
        run = pair(mm(run, all_ref[q]))
    prefix_ref[...] = prefix
    whole_ref[...] = run
    last = position - member + size
    for d in range(size, sent_ref.shape[0]):
        @pl.when(d >= last)
        def _(d=d):
            sent_ref[d] = vec[:1]


def final_kernel(size, pos_ref, levels_ref, got_ref, init_ref, prefix_ref, total_ref, lefts_ref, left_ref, table_ref, *refs):
    wholes, (out_ref, sums_ref) = refs[:-2], refs[-2:]
    steps, n = lefts_ref.shape
    groups = got_ref.shape[0] // size
    position = pos_ref[0]
    group = position // size
    for g in range(groups):
        sums_ref[g] = jnp.broadcast_to(jnp.sum(got_ref[pl.ds(g * size, size)], axis=0), (8, n))
    state = jnp.zeros((8, n), F32)
    for r in range(groups - 1, 0, -1):
        if r <= len(wholes):
            state = vm(state, wholes[r - 1][...])
        state += jnp.where(group >= r, sums_ref[jnp.maximum(group - r, 0)], 0.0)
    first = jnp.where(position == 0, row(init_ref, 0), 0.0)
    state = vm(state, prefix_ref[...]) + sums_ref[group] + first
    out_ref[pl.ds(steps - 1, 1), :] = (vm(state, total_ref[...]) + row(lefts_ref, steps - 1))[:1]
    levels = steps.bit_length() - 1
    starts = [state]
    sizes = [steps >> (level + 1) for level in range(levels)]
    for level in reversed(range(levels)):
        at, offset = sum(sizes[:level]), sum(sizes[1:level])
        later = []
        for i, x in enumerate(starts):
            mat = table_ref[levels_ref[0, 2 * i]] if level == 0 else left_ref[offset + i]
            later += [x, vm(x, mat) + row(lefts_ref, at + i)]
        starts = later
    for t in range(1, steps):
        out_ref[pl.ds(t - 1, 1), :] = starts[t][:1]


def shards(count, frames, levels, initial_state, transitions, gain, pixel_mode, pixel_weight):
    n = gain.shape[0]
    kinds = transitions.shape[0]
    pixels, length = frames.shape
    steps = length // count
    position = lax.axis_index("tm").astype(jnp.int32)[None]
    initial_state = initial_state[None]
    levels = levels[None]
    pairs = steps // 2 - 1
    dma = pltpu.SemaphoreType.DMA

    if pixels % 128 == 0:
        turned = call(
            front_kernel, "turn_frames", BIG, 0, MIB,
            out_shape=shape((length, pixels), BF16),
            in_specs=[HBM],
            out_specs=HBM,
            scratch_shapes=[pltpu.VMEM(frames.shape, BF16), pltpu.VMEM((length, pixels), BF16), dma((2,))],
        )(frames).reshape(count, steps, pixels)
        x = lax.all_to_all(turned, "tm", split_axis=0, concat_axis=0, tiled=True)
    else:
        x = lax.all_to_all(frames, "tm", split_axis=1, concat_axis=0, tiled=True).T[None]
    mode = pixel_mode.reshape(x.shape[0], x.shape[2])
    weight = pixel_weight.reshape(x.shape[0], x.shape[2])

    tree = pltpu.VMEM((pairs, n, 2 * n), BF16)
    table_vmem = pltpu.VMEM((kinds, n, 2 * n), BF16)
    maps = shape((pairs, n, 2 * n), BF16)
    one_map = shape((n, 2 * n), BF16)
    left, right, table, total = call(
        functools.partial(tree_kernel, steps), "tree_of_maps", BIG, 2 * steps * n**3 * 4, 8 * MIB,
        out_shape=[maps, maps, shape((kinds, n, 2 * n), BF16), one_map],
        in_specs=[SMEM, HBM],
        out_specs=[HBM, HBM, HBM, VMEM],
        scratch_shapes=[pltpu.VMEM(transitions.shape, F32), table_vmem, tree, tree, dma((11,))],
    )(levels, transitions)

    size = 1
    while count % (2 * size) == 0 and 4 * size * size <= count:
        size *= 2
    groups = count // size
    members = [
        lax.ppermute(total, "tm", [(j // size * size + (j + r) % size, j) for j in range(count)])
        for r in range(1, size)
    ]
    inputs = (x, mode, weight, gain, initial_state, total, table, right)
    lefts, shift = call(
        local_kernel, "local_states", BIG, 1 << 27, 6 * MIB,
        out_shape=[shape((steps, n), F32), shape((8, n), F32)],
        in_specs=[SMEM, SMEM] + [HBM] * 8,
        out_specs=[VMEM] * 2,
        scratch_shapes=[pltpu.VMEM((steps, n), F32), dma((9,))] + [pltpu.VMEM(a.shape, a.dtype) for a in inputs],
    )(position, levels, *inputs)

    prefix, whole, sent = call(
        functools.partial(group_kernel, size), "group_maps", SMALL, 1 << 24, MIB,
        out_shape=[one_map, one_map, shape((count, 1, n), F32)],
        in_specs=[SMEM] + [VMEM] * (1 + size),
        out_specs=[VMEM] * 3,
        scratch_shapes=[pltpu.VMEM((size, n, 2 * n), BF16)],
    )(position, shift, total, *members)
    wholes = [
        lax.ppermute(whole, "tm", [(j, j + r * size) for j in range(count - r * size)])
        for r in range(1, groups - 1)
    ]
    got = lax.all_to_all(sent, "tm", split_axis=0, concat_axis=0, tiled=True)

    return call(
        functools.partial(final_kernel, size), "estimates", 6, 1 << 23, 5 * MIB,
        out_shape=shape((steps, n), F32),
        in_specs=[SMEM, SMEM] + [VMEM] * (7 + len(wholes)),
        out_specs=VMEM,
        scratch_shapes=[pltpu.VMEM((groups, 8, n), F32)],
    )(position, levels, got, initial_state, prefix, total, lefts, left, table, *wholes)


def solution(mesh):
    in_specs = (P("tm", "parts"), P(("parts", "tm")), P("parts"), P(), P(), P(), P())
    out_specs = P(("parts", "tm"), None)
    return jax.shard_map(
        functools.partial(shards, mesh.shape["tm"]),
        mesh=mesh,
        in_specs=in_specs,
        out_specs=out_specs,
        check_vma=False,
    )
```

```python
import functools

import jax
import jax.numpy as jnp
from jax import lax
from jax.experimental import pallas as pl
from jax.experimental.pallas import tpu as pltpu
from jax.sharding import PartitionSpec as P

F32 = jnp.float32
BF16 = jnp.bfloat16
MIB = 1 << 20
BIG, ROOMY, SMALL = 60, 52, 2
NT = (((1,), (1,)), ((), ()))
VMEM = pl.BlockSpec(memory_space=pltpu.VMEM)
SMEM = pl.BlockSpec(memory_space=pltpu.SMEM)
HBM = pl.BlockSpec(memory_space=pltpu.HBM)
shape = jax.ShapeDtypeStruct


def call(kernel, name, mib, flops, moved, **kw):
    return pl.pallas_call(
        kernel,
        name=name,
        compiler_params=pltpu.CompilerParams(vmem_limit_bytes=mib * MIB),
        cost_estimate=pl.CostEstimate(flops=flops, bytes_accessed=moved, transcendentals=0),
        **kw,
    )


def pair(x):
    high = x.astype(BF16)
    mid = (x - high.astype(F32)).astype(BF16)
    return jnp.concatenate([high, mid], axis=1)


def mm(left, right):
    n = right.shape[0]
    out = jnp.dot(left, jnp.concatenate([right, right], axis=0), preferred_element_type=F32)
    return out[:, :n] + out[:, n:]


def vm(vec, mat):
    high = vec.astype(BF16).astype(F32)
    rows = jnp.concatenate([high, vec - high], axis=0).astype(BF16)
    out = jnp.dot(rows, mat, preferred_element_type=F32)
    n = vec.shape[1]
    out = out[:, :n] + out[:, n:]
    return out[:8] + out[8:]


def row(ref, t):
    return jnp.broadcast_to(ref[pl.ds(t, 1), :], (8, ref.shape[1]))


def front_kernel(frames_ref, turned_ref, frames, turned, sems):
    into = pltpu.make_async_copy(frames_ref, frames, sems.at[0])
    into.start()
    into.wait()
    turned[...] = frames[...].T
    out = pltpu.make_async_copy(turned, turned_ref, sems.at[1])
    out.start()
    out.wait()


def tree_kernel(steps, levels_ref, trans_ref, left_hbm, right_hbm, table_hbm, total_ref, trans, table_ref, left_ref, right_ref, sems):
    base = steps // 4
    kinds = trans_ref.shape[0]
    cuts = [(k, kinds // 4) for k in range(0, kinds, kinds // 4)]
    ins = [
        pltpu.make_async_copy(trans_ref.at[pl.ds(a, b)], trans.at[pl.ds(a, b)], sems.at[7 + i])
        for i, (a, b) in enumerate(cuts)
    ]
    for copy in ins:
        copy.start()

    for copy, (a, b) in zip(ins, cuts):
        copy.wait()
        for k in range(a, a + b):
            table_ref[k] = pair(trans[k].T)

    def first(t):
        return mm(table_ref[levels_ref[0, t]], table_ref[levels_ref[0, t + 1]])

    def node(k):
        return mm(left_ref[k], right_ref[k])

    def first_pairs(ks):
        made = [(first(4 * k), first(4 * k + 2)) for k in ks]
        for k, (a, b) in zip(ks, made):
            left_ref[k] = pair(a)
            right_ref[k] = pair(b)

    def later_pairs(ks):
        made = [(node(2 * (k - base)), node(2 * (k - base) + 1)) for k in ks]
        for k, (a, b) in zip(ks, made):
            left_ref[k] = pair(a)
            right_ref[k] = pair(b)

    def run(fn, start, count):
        if count <= 4:
            fn(list(range(start, start + count)))
            return

        def body(i, c):
            fn([start + 4 * i + k for k in range(4)])
            return c

        lax.fori_loop(0, count // 4, body, 0)

    copies = [pltpu.make_async_copy(table_ref, table_hbm, sems.at[0])]
    copies[0].start()

    def store(start, count):
        for ref, hbm in ((right_ref, right_hbm), (left_ref, left_hbm)):
            part = pl.ds(start, count)
            copies.append(pltpu.make_async_copy(ref.at[part], hbm.at[part], sems.at[len(copies)]))
            copies[-1].start()

    run(first_pairs, 0, base)
    store(0, base)
    run(later_pairs, base, base // 2)
    store(base, base // 2)
    count, start = base // 4, base + base // 2
    while count >= 1:
        run(later_pairs, start, count)
        start += count
        count //= 2
    store(base + base // 2, base // 2 - 1)
    total_ref[...] = pair(node(start - 1))
    for copy in copies:
        copy.wait()


def fetch(pieces, sems):
    copies = [
        pltpu.make_async_copy(hbm.at[pl.ds(a, b)], ref.at[pl.ds(a, b)], sems.at[i])
        for i, (hbm, ref, a, b) in enumerate(pieces)
    ]
    for copy in copies:
        copy.start()
    return copies


def local_kernel(pos_ref, levels_ref, *refs):
    hbm, (lefts_ref, own_ref), (drive_ref, sems), vmem = refs[:8], refs[8:10], refs[10:12], refs[12:]
    x_ref, mode_ref, weight_ref, gain_ref, init_ref, total_ref, table_ref, right_ref = vmem
    segments, steps, width = x_ref.shape
    n = gain_ref.shape[0]
    base = steps // 4
    whole = [(a, b, 0, b.shape[0]) for a, b in zip(hbm[:7], vmem[:7])]
    copies = fetch(whole + [(hbm[7], right_ref, 0, base), (hbm[7], right_ref, base, base - 1)], sems)
    for copy in copies[:6]:
        copy.wait()
    channel = lax.broadcasted_iota(jnp.int32, (n, width), 0)
    measured = jnp.zeros((steps, n), F32)
    for k in range(segments):
        weight = jnp.broadcast_to(weight_ref[pl.ds(k, 1), :].astype(F32), (n, width))
        projector = jnp.where(mode_ref[pl.ds(k, 1), :] == channel, weight, 0.0).astype(BF16)
        measured += lax.dot_general(x_ref[k], projector, NT, preferred_element_type=F32)
    drive_ref[...] = lax.dot_general(measured.astype(BF16), gain_ref[...], NT, preferred_element_type=F32)

    states = [row(drive_ref, t) for t in range(steps)]
    at, offset = 0, 0
    for level in range(steps.bit_length() - 1):
        if level < 3:
            copies[6 + level].wait()
        later = []
        for i in range(len(states) // 2):
            mat = table_ref[levels_ref[0, 2 * i + 1]] if level == 0 else right_ref[offset + i]
            lefts_ref[pl.ds(at + i, 1), :] = states[2 * i][:1]
            later.append(vm(states[2 * i], mat) + states[2 * i + 1])
        at += len(later)
        if level > 0:
            offset += len(later)
        states = later
    lefts_ref[pl.ds(at, 1), :] = states[0][:1]
    first = jnp.where(pos_ref[0] == 0, row(init_ref, 0), 0.0)
    total = total_ref[...]
    own_ref[pl.ds(0, n), :] = total
    own_ref[pl.ds(n, 16), :] = rows16(states[0] + vm(first, total))


def rows16(vec):
    high = vec.astype(BF16).astype(F32)
    both = jnp.concatenate([high, vec - high], axis=1)
    return jnp.concatenate([both, both], axis=0).astype(BF16)


def rows8(rows):
    both = rows.astype(F32)
    n = rows.shape[1] // 2
    return both[:8, :n] + both[:8, n:]


def group_kernel(size, pos_ref, *refs):
    blocks = refs[:size]
    prefix_ref, before_ref, mine_ref, shift_ref, all_ref = refs[size:]
    n = prefix_ref.shape[0]
    member = pos_ref[0] % size
    for r in range(size):
        all_ref[(member + r) % size] = blocks[r][...]

    def block(q):
        return all_ref[q, :n, :], rows8(all_ref[q, n:, :])

    rows, cols = (lax.broadcasted_iota(jnp.int32, (n, n), d) for d in (0, 1))
    prefix, before = pair((rows == cols).astype(F32)), jnp.zeros((8, n), F32)
    run, vec = block(0)
    for q in range(1, size):
        here = member == q
        prefix, before = jnp.where(here, run, prefix), jnp.where(here, vec, before)
        step, shift = block(q)
        vec = vm(vec, step) + shift
        run = pair(mm(run, step))
    prefix_ref[...] = prefix
    before_ref[...] = before
    mine_ref[pl.ds(0, n), :] = run
    mine_ref[pl.ds(n, 16), :] = rows16(vec)
    shift_ref[...] = rows16(vec)


def final_kernel(size, pos_ref, levels_ref, init_ref, prefix_ref, before_ref, total_ref, lefts_ref, left_ref, table_ref, *refs):
    got, out_ref = refs[:-1], refs[-1]
    steps, n = lefts_ref.shape
    position = pos_ref[0]
    group = position // size
    state = jnp.zeros((8, n), F32)
    for r in range(len(got), 0, -1):
        rows = got[r - 1].shape[0]
        if rows > 16:
            state = jnp.where(group > r, vm(state, got[r - 1][pl.ds(0, n), :]), 0.0)
        state += jnp.where(group >= r, rows8(got[r - 1][pl.ds(rows - 16, 16), :]), 0.0)
    first = jnp.where(position == 0, row(init_ref, 0), 0.0)
    state = vm(state, prefix_ref[...]) + before_ref[...] + first
    out_ref[pl.ds(steps - 1, 1), :] = (vm(state, total_ref[...]) + row(lefts_ref, steps - 1))[:1]
    levels = steps.bit_length() - 1
    starts = [state]
    sizes = [steps >> (level + 1) for level in range(levels)]
    for level in reversed(range(levels)):
        at, offset = sum(sizes[:level]), sum(sizes[1:level])
        later = []
        for i, x in enumerate(starts):
            mat = table_ref[levels_ref[0, 2 * i]] if level == 0 else left_ref[offset + i]
            later += [x, vm(x, mat) + row(lefts_ref, at + i)]
        starts = later
    for t in range(1, steps):
        out_ref[pl.ds(t - 1, 1), :] = starts[t][:1]


def shards(count, frames, levels, initial_state, transitions, gain, pixel_mode, pixel_weight):
    n = gain.shape[0]
    kinds = transitions.shape[0]
    pixels, length = frames.shape
    steps = length // count
    position = lax.axis_index("tm").astype(jnp.int32)[None]
    initial_state = initial_state[None]
    levels = levels[None]
    pairs = steps // 2 - 1
    dma = pltpu.SemaphoreType.DMA

    if pixels % 128 == 0:
        turned = call(
            front_kernel, "turn_frames", BIG, 0, MIB,
            out_shape=shape((length, pixels), BF16),
            in_specs=[HBM],
            out_specs=HBM,
            scratch_shapes=[pltpu.VMEM(frames.shape, BF16), pltpu.VMEM((length, pixels), BF16), dma((2,))],
        )(frames).reshape(count, steps, pixels)
        x = lax.all_to_all(turned, "tm", split_axis=0, concat_axis=0, tiled=True)
    else:
        x = lax.all_to_all(frames, "tm", split_axis=1, concat_axis=0, tiled=True).T[None]
    mode = pixel_mode.reshape(x.shape[0], x.shape[2])
    weight = pixel_weight.reshape(x.shape[0], x.shape[2])

    tree = pltpu.VMEM((pairs, n, 2 * n), BF16)
    table_vmem = pltpu.VMEM((kinds, n, 2 * n), BF16)
    maps = shape((pairs, n, 2 * n), BF16)
    one_map = shape((n, 2 * n), BF16)
    left, right, table, total = call(
        functools.partial(tree_kernel, steps), "tree_of_maps", ROOMY, 2 * steps * n**3 * 4, 8 * MIB,
        out_shape=[maps, maps, shape((kinds, n, 2 * n), BF16), one_map],
        in_specs=[SMEM, HBM],
        out_specs=[HBM, HBM, HBM, VMEM],
        scratch_shapes=[pltpu.VMEM(transitions.shape, F32), table_vmem, tree, tree, dma((11,))],
    )(levels, transitions)

    size = 1
    while count % (2 * size) == 0 and 4 * size * size <= count:
        size *= 2
    groups = count // size
    block = shape((n + 16, 2 * n), BF16)
    inputs = (x, mode, weight, gain, initial_state, total, table, right)
    lefts, own = call(
        local_kernel, "local_states", ROOMY, 1 << 27, 6 * MIB,
        out_shape=[shape((steps, n), F32), block],
        in_specs=[SMEM, SMEM] + [HBM] * 8,
        out_specs=[VMEM] * 2,
        scratch_shapes=[pltpu.VMEM((steps, n), F32), dma((9,))] + [pltpu.VMEM(a.shape, a.dtype) for a in inputs],
    )(position, levels, *inputs)

    others = [
        lax.ppermute(own, "tm", [(j // size * size + (j + r) % size, j) for j in range(count)])
        for r in range(1, size)
    ]
    prefix, before, mine, shift = call(
        functools.partial(group_kernel, size), "group_maps", SMALL, 1 << 24, MIB,
        out_shape=[one_map, shape((8, n), F32), block, shape((16, 2 * n), BF16)],
        in_specs=[SMEM] + [VMEM] * size,
        out_specs=[VMEM] * 4,
        scratch_shapes=[pltpu.VMEM((size, n + 16, 2 * n), BF16)],
    )(position, own, *others)
    got = [
        lax.ppermute(mine if r < groups - 1 else shift, "tm", [(j, (j + r * size) % count) for j in range(count)])
        for r in range(1, groups)
    ]

    return call(
        functools.partial(final_kernel, size), "estimates", 6, 1 << 23, 5 * MIB,
        out_shape=shape((steps, n), F32),
        in_specs=[SMEM, SMEM] + [VMEM] * (7 + len(got)),
        out_specs=VMEM,
    )(position, levels, initial_state, prefix, before, total, lefts, left, table, *got)


def solution(mesh):
    in_specs = (P("tm", "parts"), P(("parts", "tm")), P("parts"), P(), P(), P(), P())
    out_specs = P(("parts", "tm"), None)
    return jax.shard_map(
        functools.partial(shards, mesh.shape["tm"]),
        mesh=mesh,
        in_specs=in_specs,
        out_specs=out_specs,
        check_vma=False,
    )
```

```python
import functools

import jax
import jax.numpy as jnp
from jax import lax
from jax.experimental import pallas as pl
from jax.experimental.pallas import tpu as pltpu
from jax.sharding import PartitionSpec as P

F32 = jnp.float32
BF16 = jnp.bfloat16
MIB = 1 << 20
NT = (((1,), (1,)), ((), ()))
VMEM = pl.BlockSpec(memory_space=pltpu.VMEM)
SMEM = pl.BlockSpec(memory_space=pltpu.SMEM)
HBM = pl.BlockSpec(memory_space=pltpu.HBM)
shape = jax.ShapeDtypeStruct


def hbm(x):
    return pltpu.with_memory_space_constraint(x, pltpu.HBM)


def call(kernel, name, mib, flops, moved, **kw):
    return pl.pallas_call(
        kernel,
        name=name,
        compiler_params=pltpu.CompilerParams(vmem_limit_bytes=mib * MIB),
        cost_estimate=pl.CostEstimate(flops=flops, bytes_accessed=moved, transcendentals=0),
        **kw,
    )


def pair(x):
    high = x.astype(BF16)
    mid = (x - high.astype(F32)).astype(BF16)
    return jnp.concatenate([high, mid], axis=1)


def mm(left, right):
    n = right.shape[0]
    out = jnp.dot(left, jnp.concatenate([right, right], axis=0), preferred_element_type=F32)
    return out[:, :n] + out[:, n:]


def vm(vec, mat):
    high = vec.astype(BF16).astype(F32)
    rows = jnp.concatenate([high, vec - high], axis=0).astype(BF16)
    out = jnp.dot(rows, mat, preferred_element_type=F32)
    n = vec.shape[1]
    out = out[:, :n] + out[:, n:]
    return out[:8] + out[8:]


def row(ref, t):
    return jnp.broadcast_to(ref[pl.ds(t, 1), :], (8, ref.shape[1]))


def front_kernel(cuts, trans_ref, *refs):
    turn = len(refs) > 3
    if turn:
        frames_ref, table_ref, turned_ref, trans, frames, turned, sems = refs
        width = frames.shape[1] // cuts
        parts = [pl.ds(k * width, width) for k in range(cuts)]
        ins = [
            pltpu.make_async_copy(frames_ref.at[:, part], frames.at[:, part], sems.at[k])
            for k, part in enumerate(parts)
        ]
        outs = [
            pltpu.make_async_copy(turned.at[part], turned_ref.at[part], sems.at[cuts + k])
            for k, part in enumerate(parts)
        ]
        for copy in ins:
            copy.start()
    else:
        table_ref, trans, sems = refs
    kinds = trans.shape[0]
    few = kinds // 4
    maps = [
        pltpu.make_async_copy(trans_ref.at[pl.ds(k * few, few)], trans.at[pl.ds(k * few, few)], sems.at[2 * cuts + k])
        for k in range(4)
    ]
    for copy in maps:
        copy.start()
    if turn:
        for k in range(cuts):
            ins[k].wait()
            turned[parts[k], :] = frames[:, parts[k]].T
            outs[k].start()
    for k in range(4):
        maps[k].wait()
        for q in range(k * few, (k + 1) * few):
            table_ref[q] = pair(trans[q].T)
    if turn:
        for copy in outs:
            copy.wait()


def tree_kernel(steps, levels_ref, table_ref, left_hbm, right_hbm, total_ref, left_ref, right_ref, sems):
    base = steps // 4

    def first(t):
        return mm(table_ref[levels_ref[0, t]], table_ref[levels_ref[0, t + 1]])

    def node(k):
        return mm(left_ref[k], right_ref[k])

    def first_pairs(ks):
        made = [(first(4 * k), first(4 * k + 2)) for k in ks]
        for k, (a, b) in zip(ks, made):
            left_ref[k] = pair(a)
            right_ref[k] = pair(b)

    def later_pairs(ks):
        made = [(node(2 * (k - base)), node(2 * (k - base) + 1)) for k in ks]
        for k, (a, b) in zip(ks, made):
            left_ref[k] = pair(a)
            right_ref[k] = pair(b)

    def run(fn, start, count):
        if count <= 4:
            fn(list(range(start, start + count)))
            return

        def body(i, c):
            fn([start + 4 * i + k for k in range(4)])
            return c

        lax.fori_loop(0, count // 4, body, 0)

    copies = []

    def store(start, count):
        for ref, hbm in ((right_ref, right_hbm), (left_ref, left_hbm)):
            part = pl.ds(start, count)
            copies.append(pltpu.make_async_copy(ref.at[part], hbm.at[part], sems.at[len(copies)]))
            copies[-1].start()

    run(first_pairs, 0, base)
    store(0, base)
    run(later_pairs, base, base // 2)
    store(base, base // 2)
    count, start = base // 4, base + base // 2
    while count >= 1:
        run(later_pairs, start, count)
        start += count
        count //= 2
    store(base + base // 2, base // 2 - 1)
    total_ref[...] = pair(node(start - 1))
    for copy in copies:
        copy.wait()


def local_kernel(pos_ref, levels_ref, x_ref, mode_ref, weight_ref, gain_ref, init_ref, table_ref, maps_ref, right_hbm, lefts_ref, sent_ref, drive_ref, right_ref, sems):
    segments, steps, width = x_ref.shape
    n = gain_ref.shape[0]
    base = steps // 4
    copies = [
        pltpu.make_async_copy(right_hbm.at[pl.ds(a, b)], right_ref.at[pl.ds(a, b)], sems.at[i])
        for i, (a, b) in enumerate([(0, base), (base, base - 1)])
    ]
    for copy in copies:
        copy.start()
    channel = lax.broadcasted_iota(jnp.int32, (n, width), 0)
    measured = jnp.zeros((steps, n), F32)
    for k in range(segments):
        weight = jnp.broadcast_to(weight_ref[pl.ds(k, 1), :].astype(F32), (n, width))
        projector = jnp.where(mode_ref[pl.ds(k, 1), :] == channel, weight, 0.0).astype(BF16)
        measured += lax.dot_general(x_ref[k], projector, NT, preferred_element_type=F32)
    drive_ref[...] = lax.dot_general(measured.astype(BF16), gain_ref[...], NT, preferred_element_type=F32)

    states = [row(drive_ref, t) for t in range(steps)]
    at, offset = 0, 0
    for level in range(steps.bit_length() - 1):
        if level in (1, 2):
            copies[level - 1].wait()
        later = []
        for i in range(len(states) // 2):
            mat = table_ref[levels_ref[0, 2 * i + 1]] if level == 0 else right_ref[offset + i]
            lefts_ref[pl.ds(at + i, 1), :] = states[2 * i][:1]
            later.append(vm(states[2 * i], mat) + states[2 * i + 1])
        at += len(later)
        if level > 0:
            offset += len(later)
        states = later
    lefts_ref[pl.ds(at, 1), :] = states[0][:1]
    position, size = pos_ref[0], maps_ref.shape[0]
    member = position % size
    start = position - member
    first = jnp.where(position == 0, row(init_ref, 0), 0.0)
    shift = states[0] + vm(first, maps_ref[member])
    sent_ref[...] = jnp.zeros_like(sent_ref)
    for q in range(1, size):
        sent_ref[start + q] = jnp.where(member < q, shift, 0.0)[:1]
        shift = jnp.where(member < q, vm(shift, maps_ref[q]), shift)
    for d in range(size, sent_ref.shape[0]):
        sent_ref[d] = jnp.where(d >= start + size, shift[:1], sent_ref[d])


def group_kernel(size, pos_ref, *refs):
    blocks = refs[:size]
    all_ref, prefix_ref, whole_ref = refs[size:]
    n = whole_ref.shape[0]
    member = pos_ref[0] % size
    for r in range(size):
        all_ref[member ^ r] = blocks[r][...]
    rows, cols = (lax.broadcasted_iota(jnp.int32, (n, n), d) for d in (0, 1))
    prefix = pair((rows == cols).astype(F32))
    run = all_ref[0]
    for q in range(1, size):
        prefix = jnp.where(member == q, run, prefix)
        run = pair(mm(run, all_ref[q]))
    prefix_ref[...] = prefix
    whole_ref[...] = run


def final_kernel(size, pos_ref, levels_ref, got_ref, init_ref, prefix_ref, total_ref, lefts_ref, left_ref, table_ref, *refs):
    wholes, (out_ref, sums_ref) = refs[:-2], refs[-2:]
    steps, n = lefts_ref.shape
    groups = got_ref.shape[0] // size
    position = pos_ref[0]
    group = position // size
    for g in range(groups):
        sums_ref[g] = jnp.broadcast_to(jnp.sum(got_ref[pl.ds(g * size, size)], axis=0), (8, n))
    state = jnp.zeros((8, n), F32)
    for r in range(groups - 1, 0, -1):
        if r <= len(wholes):
            state = jnp.where(group > r, vm(state, wholes[r - 1][...]), 0.0)
        state += jnp.where(group >= r, sums_ref[jnp.maximum(group - r, 0)], 0.0)
    first = jnp.where(position == 0, row(init_ref, 0), 0.0)
    state = vm(state, prefix_ref[...]) + sums_ref[group] + first
    out_ref[pl.ds(steps - 1, 1), :] = (vm(state, total_ref[...]) + row(lefts_ref, steps - 1))[:1]
    levels = steps.bit_length() - 1
    starts = [state]
    sizes = [steps >> (level + 1) for level in range(levels)]
    for level in reversed(range(levels)):
        at, offset = sum(sizes[:level]), sum(sizes[1:level])
        later = []
        for i, x in enumerate(starts):
            mat = table_ref[levels_ref[0, 2 * i]] if level == 0 else left_ref[offset + i]
            later += [x, vm(x, mat) + row(lefts_ref, at + i)]
        starts = later
    for t in range(1, steps):
        out_ref[pl.ds(t - 1, 1), :] = starts[t][:1]


def shards(count, frames, levels, initial_state, transitions, gain, pixel_mode, pixel_weight):
    n = gain.shape[0]
    kinds = transitions.shape[0]
    pixels, length = frames.shape
    steps = length // count
    position = lax.axis_index("tm").astype(jnp.int32)[None]
    initial_state = initial_state[None]
    levels = levels[None]
    pairs = steps // 2 - 1
    dma = pltpu.SemaphoreType.DMA

    one_map = shape((n, 2 * n), BF16)
    table_shape = shape((kinds, n, 2 * n), BF16)
    cuts = 4
    trans_vmem = pltpu.VMEM(transitions.shape, F32)
    front = functools.partial(front_kernel, cuts)
    if pixels % 128 == 0 and length % (128 * cuts) == 0:
        table, turned = call(
            front, "front", 5, 0, 4 * MIB,
            out_shape=[table_shape, pltpu.HBM((length, pixels), BF16)],
            in_specs=[HBM, HBM],
            out_specs=[VMEM, HBM],
            scratch_shapes=[trans_vmem, pltpu.VMEM(frames.shape, BF16), pltpu.VMEM((length, pixels), BF16), dma((2 * cuts + 4,))],
        )(hbm(transitions), hbm(frames))
        turned = turned.reshape(count, steps, pixels)
        x = lax.all_to_all(turned, "tm", split_axis=0, concat_axis=0, tiled=True)
    else:
        table = call(
            front, "front", 5, 0, 4 * MIB,
            out_shape=table_shape,
            in_specs=[HBM],
            out_specs=VMEM,
            scratch_shapes=[trans_vmem, dma((2 * cuts + 4,))],
        )(hbm(transitions))
        x = lax.all_to_all(frames, "tm", split_axis=1, concat_axis=0, tiled=True).T[None]
    mode = pixel_mode.reshape(x.shape[0], x.shape[2])
    weight = pixel_weight.reshape(x.shape[0], x.shape[2])

    tree = pltpu.VMEM((pairs, n, 2 * n), BF16)
    maps = pltpu.HBM((pairs, n, 2 * n), BF16)
    left, right, total = call(
        functools.partial(tree_kernel, steps), "tree_of_maps", 8, 2 * steps * n**3 * 4, 8 * MIB,
        out_shape=[maps, maps, one_map],
        in_specs=[SMEM, VMEM],
        out_specs=[HBM, HBM, VMEM],
        scratch_shapes=[tree, tree, dma((6,))],
    )(levels, table)

    size = 1
    while count % (2 * size) == 0 and 4 * size * size <= count:
        size *= 2
    groups = count // size

    members = [lax.ppermute(total, "tm", [(j, j ^ r) for j in range(count)]) for r in range(1, size)]
    group_maps, prefix, whole = call(
        functools.partial(group_kernel, size), "group_maps", 2, 1 << 24, MIB,
        out_shape=[shape((size, n, 2 * n), BF16), one_map, one_map],
        in_specs=[SMEM] + [VMEM] * size,
        out_specs=[VMEM] * 3,
    )(position, total, *members)
    wholes = [
        lax.ppermute(whole, "tm", [(j, (j + r * size) % count) for j in range(count)]) for r in range(1, groups - 1)
    ]

    lefts, sent = call(
        local_kernel, "local_states", 8, 1 << 27, 6 * MIB,
        out_shape=[shape((steps, n), F32), shape((count, 1, n), F32)],
        in_specs=[SMEM, SMEM] + [VMEM] * 7 + [HBM],
        out_specs=[VMEM] * 2,
        scratch_shapes=[pltpu.VMEM((steps, n), F32), tree, dma((2,))],
    )(position, levels, x, mode, weight, gain, initial_state, table, group_maps, hbm(right))
    got = lax.all_to_all(sent, "tm", split_axis=0, concat_axis=0, tiled=True)

    return call(
        functools.partial(final_kernel, size), "estimates", 6, 1 << 23, 5 * MIB,
        out_shape=shape((steps, n), F32),
        in_specs=[SMEM, SMEM] + [VMEM] * (7 + len(wholes)),
        out_specs=VMEM,
        scratch_shapes=[pltpu.VMEM((groups, 8, n), F32)],
    )(position, levels, got, initial_state, prefix, total, lefts, left, table, *wholes)


def solution(mesh):
    in_specs = (P("tm", "parts"), P(("parts", "tm")), P("parts"), P(), P(), P(), P())
    out_specs = P(("parts", "tm"), None)
    return jax.shard_map(
        functools.partial(shards, mesh.shape["tm"]),
        mesh=mesh,
        in_specs=in_specs,
        out_specs=out_specs,
        check_vma=False,
    )
```

```python
import functools

import jax
import jax.numpy as jnp
from jax import lax
from jax.experimental import pallas as pl
from jax.experimental.pallas import tpu as pltpu
from jax.sharding import PartitionSpec as P

F32 = jnp.float32
BF16 = jnp.bfloat16
MIB = 1 << 20
NT = (((1,), (1,)), ((), ()))
VMEM = pl.BlockSpec(memory_space=pltpu.VMEM)
SMEM = pl.BlockSpec(memory_space=pltpu.SMEM)
HBM = pl.BlockSpec(memory_space=pltpu.HBM)
shape = jax.ShapeDtypeStruct


def hbm(x):
    return pltpu.with_memory_space_constraint(x, pltpu.HBM)


def call(kernel, name, mib, flops, moved, **kw):
    return pl.pallas_call(
        kernel,
        name=name,
        compiler_params=pltpu.CompilerParams(vmem_limit_bytes=mib * MIB),
        cost_estimate=pl.CostEstimate(flops=flops, bytes_accessed=moved, transcendentals=0),
        **kw,
    )


def pair(x):
    high = x.astype(BF16)
    mid = (x - high.astype(F32)).astype(BF16)
    return jnp.concatenate([high, mid], axis=1)


def mm(left, right):
    n = right.shape[0]
    out = jnp.dot(left, jnp.concatenate([right, right], axis=0), preferred_element_type=F32)
    return out[:, :n] + out[:, n:]


def vm(vec, mat):
    high = vec.astype(BF16).astype(F32)
    rows = jnp.concatenate([high, vec - high], axis=0).astype(BF16)
    out = jnp.dot(rows, mat, preferred_element_type=F32)
    n = vec.shape[1]
    out = out[:, :n] + out[:, n:]
    return out[:8] + out[8:]


def row(ref, t):
    return jnp.broadcast_to(ref[pl.ds(t, 1), :], (8, ref.shape[1]))


def front_kernel(cuts, extra, trans_ref, *refs):
    given, refs = refs[:extra], refs[extra:]
    turn = len(refs) > extra + 3
    if turn:
        frames_ref, table_ref, *moved, turned_ref, trans, frames, turned, sems = refs
        width = frames.shape[1] // cuts
        parts = [pl.ds(k * width, width) for k in range(cuts)]
        ins = [
            pltpu.make_async_copy(frames_ref.at[:, part], frames.at[:, part], sems.at[k])
            for k, part in enumerate(parts)
        ]
        outs = [
            pltpu.make_async_copy(turned.at[part], turned_ref.at[part], sems.at[cuts + k])
            for k, part in enumerate(parts)
        ]
        for copy in ins:
            copy.start()
    else:
        table_ref, *moved, trans, sems = refs
        outs = []
    kinds = trans.shape[0]
    few = kinds // 4
    maps = [
        pltpu.make_async_copy(trans_ref.at[pl.ds(k * few, few)], trans.at[pl.ds(k * few, few)], sems.at[2 * cuts + k])
        for k in range(4)
    ]
    moves = [
        pltpu.make_async_copy(a, b, sems.at[2 * cuts + 4 + k]) for k, (a, b) in enumerate(zip(given, moved))
    ]
    for copy in maps + moves:
        copy.start()
    if turn:
        for k in range(cuts):
            ins[k].wait()
            turned[parts[k], :] = frames[:, parts[k]].T
            outs[k].start()
    for k in range(4):
        maps[k].wait()
        for q in range(k * few, (k + 1) * few):
            table_ref[q] = pair(trans[q].T)
    for copy in moves + outs:
        copy.wait()


def tree_kernel(steps, levels_ref, table_ref, left_hbm, right_hbm, table_hbm, total_ref, left_ref, right_ref, sems):
    base = steps // 4

    def first(t):
        return mm(table_ref[levels_ref[0, t]], table_ref[levels_ref[0, t + 1]])

    def node(k):
        return mm(left_ref[k], right_ref[k])

    def first_pairs(ks):
        made = [(first(4 * k), first(4 * k + 2)) for k in ks]
        for k, (a, b) in zip(ks, made):
            left_ref[k] = pair(a)
            right_ref[k] = pair(b)

    def later_pairs(ks):
        made = [(node(2 * (k - base)), node(2 * (k - base) + 1)) for k in ks]
        for k, (a, b) in zip(ks, made):
            left_ref[k] = pair(a)
            right_ref[k] = pair(b)

    def run(fn, start, count):
        if count <= 4:
            fn(list(range(start, start + count)))
            return

        def body(i, c):
            fn([start + 4 * i + k for k in range(4)])
            return c

        lax.fori_loop(0, count // 4, body, 0)

    copies = [pltpu.make_async_copy(table_ref, table_hbm, sems.at[0])]
    copies[0].start()

    def store(start, count):
        for ref, hbm in ((right_ref, right_hbm), (left_ref, left_hbm)):
            part = pl.ds(start, count)
            copies.append(pltpu.make_async_copy(ref.at[part], hbm.at[part], sems.at[len(copies)]))
            copies[-1].start()

    run(first_pairs, 0, base)
    store(0, base)
    run(later_pairs, base, base // 2)
    store(base, base // 2)
    count, start = base // 4, base + base // 2
    while count >= 1:
        run(later_pairs, start, count)
        start += count
        count //= 2
    store(base + base // 2, base // 2 - 1)
    total_ref[...] = pair(node(start - 1))
    for copy in copies:
        copy.wait()


def local_kernel(pos_ref, levels_ref, x_ref, mode_ref, weight_ref, gain_ref, init_ref, total_ref, table_hbm, right_hbm, lefts_ref, shift_ref, drive_ref, table_ref, right_ref, sems):
    segments, steps, width = x_ref.shape
    n = gain_ref.shape[0]
    base = steps // 4
    copies = [
        pltpu.make_async_copy(table_hbm, table_ref, sems.at[0]),
        pltpu.make_async_copy(right_hbm.at[pl.ds(0, base)], right_ref.at[pl.ds(0, base)], sems.at[1]),
        pltpu.make_async_copy(right_hbm.at[pl.ds(base, base - 1)], right_ref.at[pl.ds(base, base - 1)], sems.at[2]),
    ]
    for copy in copies:
        copy.start()
    channel = lax.broadcasted_iota(jnp.int32, (n, width), 0)
    measured = jnp.zeros((steps, n), F32)
    for k in range(segments):
        weight = jnp.broadcast_to(weight_ref[pl.ds(k, 1), :].astype(F32), (n, width))
        projector = jnp.where(mode_ref[pl.ds(k, 1), :] == channel, weight, 0.0).astype(BF16)
        measured += lax.dot_general(x_ref[k], projector, NT, preferred_element_type=F32)
    drive_ref[...] = lax.dot_general(measured.astype(BF16), gain_ref[...], NT, preferred_element_type=F32)

    states = [row(drive_ref, t) for t in range(steps)]
    at, offset = 0, 0
    for level in range(steps.bit_length() - 1):
        if level < 3:
            copies[level].wait()
        later = []
        for i in range(len(states) // 2):
            mat = table_ref[levels_ref[0, 2 * i + 1]] if level == 0 else right_ref[offset + i]
            lefts_ref[pl.ds(at + i, 1), :] = states[2 * i][:1]
            later.append(vm(states[2 * i], mat) + states[2 * i + 1])
        at += len(later)
        if level > 0:
            offset += len(later)
        states = later
    lefts_ref[pl.ds(at, 1), :] = states[0][:1]
    first = jnp.where(pos_ref[0] == 0, row(init_ref, 0), 0.0)
    shift_ref[...] = states[0] + vm(first, total_ref[...])


def group_kernel(size, pos_ref, *refs):
    blocks = refs[:size]
    all_ref, prefix_ref, whole_ref = refs[size:]
    n = whole_ref.shape[0]
    member = pos_ref[0] % size
    for r in range(size):
        all_ref[member ^ r] = blocks[r][...]
    rows, cols = (lax.broadcasted_iota(jnp.int32, (n, n), d) for d in (0, 1))
    prefix = pair((rows == cols).astype(F32))
    run = all_ref[0]
    for q in range(1, size):
        prefix = jnp.where(member == q, run, prefix)
        run = pair(mm(run, all_ref[q]))
    prefix_ref[...] = prefix
    whole_ref[...] = run


def beside_kernel(size, pos_ref, all_ref, *refs):
    shifts = refs[:size]
    before_ref, whole_ref, held_ref = refs[size:]
    member = pos_ref[0] % size
    for r in range(size):
        held_ref[member ^ r] = shifts[r][...]
    run, before = held_ref[0], jnp.zeros(before_ref.shape, F32)
    for q in range(1, size):
        before = jnp.where(member == q, run, before)
        run = vm(run, all_ref[q]) + held_ref[q]
    before_ref[...] = before
    whole_ref[...] = run


def final_kernel(size, groups, pos_ref, levels_ref, init_ref, prefix_ref, before_ref, total_ref, lefts_ref, left_ref, table_hbm, *refs):
    shifts, wholes = refs[: groups - 1], refs[groups - 1 : 2 * groups - 3]
    out_ref, sums_ref, table_ref, sem = refs[2 * groups - 3 :]
    copy = pltpu.make_async_copy(table_hbm, table_ref, sem)
    copy.start()
    steps, n = lefts_ref.shape
    position = pos_ref[0]
    group = position // size
    for r in range(1, groups):
        sums_ref[group ^ r] = shifts[r - 1][...]
    state = jnp.zeros((8, n), F32)
    for r in range(groups - 1, 0, -1):
        if r < groups - 1:
            state = jnp.where(group > r, vm(state, wholes[r - 1][...]), 0.0)
        state += jnp.where(group >= r, sums_ref[jnp.maximum(group - r, 0)], 0.0)
    first = jnp.where(position == 0, row(init_ref, 0), 0.0)
    state = vm(state, prefix_ref[...]) + before_ref[...] + first
    out_ref[pl.ds(steps - 1, 1), :] = (vm(state, total_ref[...]) + row(lefts_ref, steps - 1))[:1]
    levels = steps.bit_length() - 1
    starts = [state]
    sizes = [steps >> (level + 1) for level in range(levels)]
    for level in reversed(range(levels)):
        if level == 0:
            copy.wait()
        at, offset = sum(sizes[:level]), sum(sizes[1:level])
        later = []
        for i, x in enumerate(starts):
            mat = table_ref[levels_ref[0, 2 * i]] if level == 0 else left_ref[offset + i]
            later += [x, vm(x, mat) + row(lefts_ref, at + i)]
        starts = later
    for t in range(1, steps):
        out_ref[pl.ds(t - 1, 1), :] = starts[t][:1]


def shards(count, frames, levels, initial_state, transitions, gain, pixel_mode, pixel_weight):
    n = gain.shape[0]
    kinds = transitions.shape[0]
    pixels, length = frames.shape
    steps = length // count
    position = lax.axis_index("tm").astype(jnp.int32)[None]
    pairs = steps // 2 - 1
    dma = pltpu.SemaphoreType.DMA
    one_map = shape((n, 2 * n), BF16)
    table_shape = shape((kinds, n, 2 * n), BF16)
    cuts = 4
    turn = pixels % 128 == 0 and length % (128 * cuts) == 0
    segments = count if turn else 1
    small = [
        levels[None],
        initial_state[None],
        gain,
        pixel_mode.reshape(segments, -1),
        pixel_weight.reshape(segments, -1),
    ]
    given = [hbm(a) for a in [transitions] + small + [frames] * turn]
    outs = [table_shape] + [shape(a.shape, a.dtype) for a in small]
    buffers = [pltpu.VMEM(transitions.shape, F32)]
    if turn:
        outs.append(pltpu.HBM((length, pixels), BF16))
        buffers += [pltpu.VMEM(frames.shape, BF16), pltpu.VMEM((length, pixels), BF16)]
    table, levels, initial_state, gain, mode, weight, *turned = call(
        functools.partial(front_kernel, cuts, len(small)), "front", 5, 0, 4 * MIB,
        out_shape=outs,
        in_specs=[HBM] * len(given),
        out_specs=[VMEM] * (1 + len(small)) + [HBM] * turn,
        scratch_shapes=buffers + [dma((2 * cuts + 4 + len(small),))],
    )(*given)
    if turn:
        x = lax.all_to_all(turned[0].reshape(count, steps, pixels), "tm", split_axis=0, concat_axis=0, tiled=True)
    else:
        x = lax.all_to_all(frames, "tm", split_axis=1, concat_axis=0, tiled=True).T[None]

    tree = pltpu.VMEM((pairs, n, 2 * n), BF16)
    table_vmem = pltpu.VMEM(table_shape.shape, BF16)
    maps = pltpu.HBM((pairs, n, 2 * n), BF16)
    left, right, table, total = call(
        functools.partial(tree_kernel, steps), "tree_of_maps", 8, 2 * steps * n**3 * 4, 8 * MIB,
        out_shape=[maps, maps, pltpu.HBM(table_shape.shape, BF16), one_map],
        in_specs=[SMEM, VMEM],
        out_specs=[HBM, HBM, HBM, VMEM],
        scratch_shapes=[tree, tree, dma((7,))],
    )(levels, table)
    right, table = hbm(right), hbm(table)

    size = 1
    while count % (2 * size) == 0 and 4 * size * size <= count:
        size *= 2
    groups = count // size

    vector = shape((8, n), F32)

    def swaps(x, step, times):
        return [lax.ppermute(x, "tm", [(j, j ^ (r * step)) for j in range(count)]) for r in range(1, times)]

    members = swaps(total, 1, size)
    lefts, shift = call(
        local_kernel, "local_states", 8, 1 << 27, 6 * MIB,
        out_shape=[shape((steps, n), F32), vector],
        in_specs=[SMEM, SMEM] + [VMEM] * 6 + [HBM] * 2,
        out_specs=[VMEM] * 2,
        scratch_shapes=[pltpu.VMEM((steps, n), F32), table_vmem, tree, dma((3,))],
    )(position, levels, x, mode, weight, gain, initial_state, total, table, right)
    shifts = swaps(shift, 1, size)

    group_maps, prefix, whole = call(
        functools.partial(group_kernel, size), "group_maps", 2, 1 << 24, MIB,
        out_shape=[shape((size, n, 2 * n), BF16), one_map, one_map],
        in_specs=[SMEM] + [VMEM] * size,
        out_specs=[VMEM] * 3,
    )(position, total, *members)
    wholes = [
        lax.ppermute(whole, "tm", [(j, (j + r * size) % count) for j in range(count)]) for r in range(1, groups - 1)
    ]
    before, carried = call(
        functools.partial(beside_kernel, size), "group_states", 2, 1 << 20, MIB // 4,
        out_shape=[vector, vector],
        in_specs=[SMEM] + [VMEM] * (1 + size),
        out_specs=[VMEM] * 2,
        scratch_shapes=[pltpu.VMEM((size, 8, n), F32)],
    )(position, group_maps, shift, *shifts)

    return call(
        functools.partial(final_kernel, size, groups), "estimates", 6, 1 << 23, 5 * MIB,
        out_shape=shape((steps, n), F32),
        in_specs=[SMEM, SMEM] + [VMEM] * 6 + [HBM] + [VMEM] * (2 * groups - 3),
        out_specs=VMEM,
        scratch_shapes=[pltpu.VMEM((groups, 8, n), F32), table_vmem, dma(())],
    )(position, levels, initial_state, prefix, before, total, lefts, left, table, *swaps(carried, size, groups), *wholes)


def solution(mesh):
    in_specs = (P("tm", "parts"), P(("parts", "tm")), P("parts"), P(), P(), P(), P())
    out_specs = P(("parts", "tm"), None)
    return jax.shard_map(
        functools.partial(shards, mesh.shape["tm"]),
        mesh=mesh,
        in_specs=in_specs,
        out_specs=out_specs,
        check_vma=False,
    )
```

```python
import functools

import jax
import jax.numpy as jnp
from jax import lax
from jax.experimental import pallas as pl
from jax.experimental.pallas import tpu as pltpu
from jax.sharding import PartitionSpec as P

F32 = jnp.float32
BF16 = jnp.bfloat16
MIB = 1 << 20
NT = (((1,), (1,)), ((), ()))
VMEM = pl.BlockSpec(memory_space=pltpu.VMEM)
SMEM = pl.BlockSpec(memory_space=pltpu.SMEM)
HBM = pl.BlockSpec(memory_space=pltpu.HBM)
shape = jax.ShapeDtypeStruct


def hbm(x):
    return pltpu.with_memory_space_constraint(x, pltpu.HBM)


def call(kernel, name, mib, flops, moved, **kw):
    return pl.pallas_call(
        kernel,
        name=name,
        compiler_params=pltpu.CompilerParams(vmem_limit_bytes=mib * MIB),
        cost_estimate=pl.CostEstimate(flops=flops, bytes_accessed=moved, transcendentals=0),
        **kw,
    )


def pair(x):
    high = x.astype(BF16)
    mid = (x - high.astype(F32)).astype(BF16)
    return jnp.concatenate([high, mid], axis=1)


def mm(left, right):
    n = right.shape[0]
    out = jnp.dot(left, jnp.concatenate([right, right], axis=0), preferred_element_type=F32)
    return out[:, :n] + out[:, n:]


def vm(vec, mat):
    high = vec.astype(BF16).astype(F32)
    rows = jnp.concatenate([high, vec - high], axis=0).astype(BF16)
    out = jnp.dot(rows, mat, preferred_element_type=F32)
    n = vec.shape[1]
    out = out[:, :n] + out[:, n:]
    return out[:8] + out[8:]


def row(ref, t):
    return jnp.broadcast_to(ref[pl.ds(t, 1), :], (8, ref.shape[1]))


def front_kernel(cuts, extra, trans_ref, *refs):
    given, refs = refs[:extra], refs[extra:]
    turn = len(refs) > extra + 3
    if turn:
        frames_ref, table_ref, *moved, turned_ref, trans, frames, turned, sems = refs
        width = frames.shape[1] // cuts
        parts = [pl.ds(k * width, width) for k in range(cuts)]
        ins = [
            pltpu.make_async_copy(frames_ref.at[:, part], frames.at[:, part], sems.at[k])
            for k, part in enumerate(parts)
        ]
        outs = [
            pltpu.make_async_copy(turned.at[part], turned_ref.at[part], sems.at[cuts + k])
            for k, part in enumerate(parts)
        ]
        for copy in ins:
            copy.start()
    else:
        table_ref, *moved, trans, sems = refs
        outs = []
    kinds = trans.shape[0]
    few = kinds // 4
    maps = [
        pltpu.make_async_copy(trans_ref.at[pl.ds(k * few, few)], trans.at[pl.ds(k * few, few)], sems.at[2 * cuts + k])
        for k in range(4)
    ]
    moves = [
        pltpu.make_async_copy(a, b, sems.at[2 * cuts + 4 + k]) for k, (a, b) in enumerate(zip(given, moved))
    ]
    for copy in maps + moves:
        copy.start()
    if turn:
        for k in range(cuts):
            ins[k].wait()
            turned[parts[k], :] = frames[:, parts[k]].T
            outs[k].start()
    for k in range(4):
        maps[k].wait()
        for q in range(k * few, (k + 1) * few):
            table_ref[q] = pair(trans[q].T)
    for copy in moves + outs:
        copy.wait()


def tree_kernel(steps, levels_ref, table_ref, left_hbm, right_hbm, table_hbm, total_ref, left_ref, right_ref, sems):
    base = steps // 4

    def first(t):
        return mm(table_ref[levels_ref[0, t]], table_ref[levels_ref[0, t + 1]])

    def node(k):
        return mm(left_ref[k], right_ref[k])

    def first_pairs(ks):
        made = [(first(4 * k), first(4 * k + 2)) for k in ks]
        for k, (a, b) in zip(ks, made):
            left_ref[k] = pair(a)
            right_ref[k] = pair(b)

    def later_pairs(ks):
        made = [(node(2 * (k - base)), node(2 * (k - base) + 1)) for k in ks]
        for k, (a, b) in zip(ks, made):
            left_ref[k] = pair(a)
            right_ref[k] = pair(b)

    def run(fn, start, count):
        if count <= 4:
            fn(list(range(start, start + count)))
            return

        def body(i, c):
            fn([start + 4 * i + k for k in range(4)])
            return c

        lax.fori_loop(0, count // 4, body, 0)

    copies = [pltpu.make_async_copy(table_ref, table_hbm, sems.at[0])]
    copies[0].start()

    def store(start, count):
        for ref, hbm in ((right_ref, right_hbm), (left_ref, left_hbm)):
            part = pl.ds(start, count)
            copies.append(pltpu.make_async_copy(ref.at[part], hbm.at[part], sems.at[len(copies)]))
            copies[-1].start()

    run(first_pairs, 0, base)
    store(0, base)
    run(later_pairs, base, base // 2)
    store(base, base // 2)
    count, start = base // 4, base + base // 2
    while count >= 1:
        run(later_pairs, start, count)
        start += count
        count //= 2
    store(base + base // 2, base // 2 - 1)
    total_ref[...] = pair(node(start - 1))
    for copy in copies:
        copy.wait()


def local_kernel(pos_ref, levels_ref, x_ref, mode_ref, weight_ref, gain_ref, init_ref, total_ref, table_hbm, right_hbm, lefts_ref, shift_ref, drive_ref, table_ref, right_ref, sems):
    segments, steps, width = x_ref.shape
    n = gain_ref.shape[0]
    base = steps // 4
    copies = [
        pltpu.make_async_copy(table_hbm, table_ref, sems.at[0]),
        pltpu.make_async_copy(right_hbm.at[pl.ds(0, base)], right_ref.at[pl.ds(0, base)], sems.at[1]),
        pltpu.make_async_copy(right_hbm.at[pl.ds(base, base - 1)], right_ref.at[pl.ds(base, base - 1)], sems.at[2]),
    ]
    for copy in copies:
        copy.start()
    channel = lax.broadcasted_iota(jnp.int32, (n, width), 0)
    measured = jnp.zeros((steps, n), F32)
    for k in range(segments):
        weight = jnp.broadcast_to(weight_ref[pl.ds(k, 1), :].astype(F32), (n, width))
        projector = jnp.where(mode_ref[pl.ds(k, 1), :] == channel, weight, 0.0).astype(BF16)
        measured += lax.dot_general(x_ref[k], projector, NT, preferred_element_type=F32)
    drive_ref[...] = lax.dot_general(measured.astype(BF16), gain_ref[...], NT, preferred_element_type=F32)

    states = [row(drive_ref, t) for t in range(steps)]
    at, offset = 0, 0
    for level in range(steps.bit_length() - 1):
        if level < 3:
            copies[level].wait()
        later = []
        for i in range(len(states) // 2):
            mat = table_ref[levels_ref[0, 2 * i + 1]] if level == 0 else right_ref[offset + i]
            lefts_ref[pl.ds(at + i, 1), :] = states[2 * i][:1]
            later.append(vm(states[2 * i], mat) + states[2 * i + 1])
        at += len(later)
        if level > 0:
            offset += len(later)
        states = later
    lefts_ref[pl.ds(at, 1), :] = states[0][:1]
    first = jnp.where(pos_ref[0] == 0, row(init_ref, 0), 0.0)
    shift_ref[...] = states[0] + vm(first, total_ref[...])


def group_kernel(size, pos_ref, after_ref, *refs):
    blocks = refs[:size]
    all_ref, prefix_ref, whole_ref = refs[size:]
    n = whole_ref.shape[0]
    member = pos_ref[0] % size
    for r in range(size):
        all_ref[member ^ r] = blocks[r][...]
    rows, cols = (lax.broadcasted_iota(jnp.int32, (n, n), d) for d in (0, 1))
    prefix = pair((rows == cols).astype(F32))
    run = all_ref[0]
    for q in range(1, size):
        prefix = jnp.where(member == q, run, prefix)
        run = pair(mm(run, all_ref[q]))
    prefix_ref[...] = prefix
    whole_ref[...] = run


def beside_kernel(size, pos_ref, all_ref, *refs):
    shifts = refs[:size]
    before_ref, whole_ref, held_ref = refs[size:]
    member = pos_ref[0] % size
    for r in range(size):
        held_ref[member ^ r] = shifts[r][...]
    run, before = held_ref[0], jnp.zeros(before_ref.shape, F32)
    for q in range(1, size):
        before = jnp.where(member == q, run, before)
        run = vm(run, all_ref[q]) + held_ref[q]
    before_ref[...] = before
    whole_ref[...] = run


def final_kernel(size, groups, pos_ref, levels_ref, init_ref, prefix_ref, before_ref, total_ref, lefts_ref, left_ref, table_hbm, *refs):
    shifts, wholes = refs[: groups - 1], refs[groups - 1 : 2 * groups - 3]
    out_ref, sums_ref, table_ref, sem = refs[2 * groups - 3 :]
    copy = pltpu.make_async_copy(table_hbm, table_ref, sem)
    copy.start()
    steps, n = lefts_ref.shape
    position = pos_ref[0]
    group = position // size
    for r in range(1, groups):
        sums_ref[group ^ r] = shifts[r - 1][...]
    state = jnp.zeros((8, n), F32)
    for r in range(groups - 1, 0, -1):
        if r < groups - 1:
            state = jnp.where(group > r, vm(state, wholes[r - 1][...]), 0.0)
        state += jnp.where(group >= r, sums_ref[jnp.maximum(group - r, 0)], 0.0)
    first = jnp.where(position == 0, row(init_ref, 0), 0.0)
    state = vm(state, prefix_ref[...]) + before_ref[...] + first
    out_ref[pl.ds(steps - 1, 1), :] = (vm(state, total_ref[...]) + row(lefts_ref, steps - 1))[:1]
    levels = steps.bit_length() - 1
    starts = [state]
    sizes = [steps >> (level + 1) for level in range(levels)]
    for level in reversed(range(levels)):
        if level == 0:
            copy.wait()
        at, offset = sum(sizes[:level]), sum(sizes[1:level])
        later = []
        for i, x in enumerate(starts):
            mat = table_ref[levels_ref[0, 2 * i]] if level == 0 else left_ref[offset + i]
            later += [x, vm(x, mat) + row(lefts_ref, at + i)]
        starts = later
    for t in range(1, steps):
        out_ref[pl.ds(t - 1, 1), :] = starts[t][:1]


def shards(count, frames, levels, initial_state, transitions, gain, pixel_mode, pixel_weight):
    n = gain.shape[0]
    kinds = transitions.shape[0]
    pixels, length = frames.shape
    steps = length // count
    position = lax.axis_index("tm").astype(jnp.int32)[None]
    pairs = steps // 2 - 1
    dma = pltpu.SemaphoreType.DMA
    one_map = shape((n, 2 * n), BF16)
    table_shape = shape((kinds, n, 2 * n), BF16)
    cuts = 4
    turn = pixels % 128 == 0 and length % (128 * cuts) == 0
    segments = count if turn else 1
    small = [
        levels[None],
        initial_state[None],
        gain,
        pixel_mode.reshape(segments, -1),
        pixel_weight.reshape(segments, -1),
    ]
    given = [hbm(a) for a in [transitions] + small + [frames] * turn]
    outs = [table_shape] + [shape(a.shape, a.dtype) for a in small]
    buffers = [pltpu.VMEM(transitions.shape, F32)]
    if turn:
        outs.append(pltpu.HBM((length, pixels), BF16))
        buffers += [pltpu.VMEM(frames.shape, BF16), pltpu.VMEM((length, pixels), BF16)]
    table, levels, initial_state, gain, mode, weight, *turned = call(
        functools.partial(front_kernel, cuts, len(small)), "front", 5, 0, 4 * MIB,
        out_shape=outs,
        in_specs=[HBM] * len(given),
        out_specs=[VMEM] * (1 + len(small)) + [HBM] * turn,
        scratch_shapes=buffers + [dma((2 * cuts + 4 + len(small),))],
    )(*given)
    if turn:
        x = lax.all_to_all(turned[0].reshape(count, steps, pixels), "tm", split_axis=0, concat_axis=0, tiled=True)
    else:
        x = lax.all_to_all(frames, "tm", split_axis=1, concat_axis=0, tiled=True).T[None]

    tree = pltpu.VMEM((pairs, n, 2 * n), BF16)
    table_vmem = pltpu.VMEM(table_shape.shape, BF16)
    maps = pltpu.HBM((pairs, n, 2 * n), BF16)
    left, right, table, total = call(
        functools.partial(tree_kernel, steps), "tree_of_maps", 8, 2 * steps * n**3 * 4, 8 * MIB,
        out_shape=[maps, maps, pltpu.HBM(table_shape.shape, BF16), one_map],
        in_specs=[SMEM, VMEM],
        out_specs=[HBM, HBM, HBM, VMEM],
        scratch_shapes=[tree, tree, dma((7,))],
    )(levels, table)
    right, table = hbm(right), hbm(table)

    size = 1
    while count % (2 * size) == 0 and 4 * size * size <= count:
        size *= 2
    groups = count // size

    vector = shape((8, n), F32)

    def swaps(x, step, times):
        return [lax.ppermute(x, "tm", [(j, j ^ (r * step)) for j in range(count)]) for r in range(1, times)]

    members = swaps(total, 1, size)
    lefts, shift = call(
        local_kernel, "local_states", 8, 1 << 27, 6 * MIB,
        out_shape=[shape((steps, n), F32), vector],
        in_specs=[SMEM, SMEM] + [VMEM] * 6 + [HBM] * 2,
        out_specs=[VMEM] * 2,
        scratch_shapes=[pltpu.VMEM((steps, n), F32), table_vmem, tree, dma((3,))],
    )(position, levels, x, mode, weight, gain, initial_state, total, table, right)
    shifts = swaps(shift, 1, size)

    group_maps, prefix, whole = call(
        functools.partial(group_kernel, size), "group_maps", 2, 1 << 24, MIB,
        out_shape=[shape((size, n, 2 * n), BF16), one_map, one_map],
        in_specs=[SMEM] + [VMEM] * (1 + size),
        out_specs=[VMEM] * 3,
    )(position, shift, total, *members)
    wholes = [
        lax.ppermute(whole, "tm", [(j, (j + r * size) % count) for j in range(count)]) for r in range(1, groups - 1)
    ]
    before, carried = call(
        functools.partial(beside_kernel, size), "group_states", 2, 1 << 20, MIB // 4,
        out_shape=[vector, vector],
        in_specs=[SMEM] + [VMEM] * (1 + size),
        out_specs=[VMEM] * 2,
        scratch_shapes=[pltpu.VMEM((size, 8, n), F32)],
    )(position, group_maps, shift, *shifts)

    return call(
        functools.partial(final_kernel, size, groups), "estimates", 6, 1 << 23, 5 * MIB,
        out_shape=shape((steps, n), F32),
        in_specs=[SMEM, SMEM] + [VMEM] * 6 + [HBM] + [VMEM] * (2 * groups - 3),
        out_specs=VMEM,
        scratch_shapes=[pltpu.VMEM((groups, 8, n), F32), table_vmem, dma(())],
    )(position, levels, initial_state, prefix, before, total, lefts, left, table, *swaps(carried, size, groups), *wholes)


def solution(mesh):
    in_specs = (P("tm", "parts"), P(("parts", "tm")), P("parts"), P(), P(), P(), P())
    out_specs = P(("parts", "tm"), None)
    return jax.shard_map(
        functools.partial(shards, mesh.shape["tm"]),
        mesh=mesh,
        in_specs=in_specs,
        out_specs=out_specs,
        check_vma=False,
    )
```

```python
import functools

import jax
import jax.numpy as jnp
from jax import lax
from jax.experimental import pallas as pl
from jax.experimental.pallas import tpu as pltpu
from jax.sharding import PartitionSpec as P

F32 = jnp.float32
BF16 = jnp.bfloat16
MIB = 1 << 20
NT = (((1,), (1,)), ((), ()))
VMEM = pl.BlockSpec(memory_space=pltpu.VMEM)
SMEM = pl.BlockSpec(memory_space=pltpu.SMEM)
HBM = pl.BlockSpec(memory_space=pltpu.HBM)
shape = jax.ShapeDtypeStruct


def hbm(x):
    return pltpu.with_memory_space_constraint(x, pltpu.HBM)


def call(kernel, name, mib, flops, moved, **kw):
    return pl.pallas_call(
        kernel,
        name=name,
        compiler_params=pltpu.CompilerParams(vmem_limit_bytes=mib * MIB),
        cost_estimate=pl.CostEstimate(flops=flops, bytes_accessed=moved, transcendentals=0),
        **kw,
    )


def pair(x):
    high = x.astype(BF16)
    mid = (x - high.astype(F32)).astype(BF16)
    return jnp.concatenate([high, mid], axis=1)


def mm(left, right):
    n = right.shape[0]
    out = jnp.dot(left, jnp.concatenate([right, right], axis=0), preferred_element_type=F32)
    return out[:, :n] + out[:, n:]


def vm(vec, mat):
    high = vec.astype(BF16).astype(F32)
    rows = jnp.concatenate([high, vec - high], axis=0).astype(BF16)
    out = jnp.dot(rows, mat, preferred_element_type=F32)
    n = vec.shape[1]
    out = out[:, :n] + out[:, n:]
    return out[:8] + out[8:]


def row(ref, t):
    return jnp.broadcast_to(ref[pl.ds(t, 1), :], (8, ref.shape[1]))


def front_kernel(cuts, extra, size, pos_ref, trans_ref, *refs):
    given, refs = refs[:extra], refs[extra:]
    turn = len(refs) > extra + 3
    if turn:
        frames_ref, table_ref, *moved = refs[: 2 + extra]
        slabs = refs[2 + extra : 2 + extra + size]
        trans, frames, turned, sems = refs[2 + extra + size :]
        width = frames.shape[1] // cuts
        parts = [pl.ds(k * width, width) for k in range(cuts)]
        ins = [
            pltpu.make_async_copy(frames_ref.at[:, part], frames.at[:, part], sems.at[k])
            for k, part in enumerate(parts)
        ]
        for copy in ins:
            copy.start()
    else:
        table_ref, *moved, trans, sems = refs
    kinds = trans.shape[0]
    few = kinds // 4
    maps = [
        pltpu.make_async_copy(trans_ref.at[pl.ds(k * few, few)], trans.at[pl.ds(k * few, few)], sems.at[cuts + k])
        for k in range(4)
    ]
    moves = [pltpu.make_async_copy(a, b, sems.at[cuts + 4 + k]) for k, (a, b) in enumerate(zip(given, moved))]
    for copy in maps + moves:
        copy.start()
    if turn:
        for k in range(cuts):
            ins[k].wait()
            turned[parts[k], :] = frames[:, parts[k]].T
        member = pos_ref[0] % size
        groups, steps, _ = slabs[0].shape
        for r in range(size):
            for g in range(groups):
                start = pl.multiple_of((g * size + (member ^ r)) * steps, steps)
                slabs[r][g] = turned[pl.ds(start, steps), :]
    for k in range(4):
        maps[k].wait()
        for q in range(k * few, (k + 1) * few):
            table_ref[q] = pair(trans[q].T)
    for copy in moves:
        copy.wait()


def project_kernel(size, pos_ref, mode_ref, weight_ref, *refs):
    slabs, outs, (sums, weights) = refs[:size], refs[size:-2], refs[-2:]
    weights[...] = weight_ref[...].astype(F32)
    groups, steps, width = slabs[0].shape
    n = sums.shape[2]
    position = pos_ref[0]
    channel = lax.broadcasted_iota(jnp.int32, (n, width), 0)
    total = jnp.zeros((groups * steps, n), F32)
    for r in range(size):
        here = pl.ds(position ^ r, 1)
        weight = jnp.broadcast_to(weights[here, :], (n, width))
        projector = jnp.where(mode_ref[here, :] == channel, weight, 0.0).astype(BF16)
        total += lax.dot_general(slabs[r][...].reshape(groups * steps, width), projector, NT, preferred_element_type=F32)
    sums[...] = total.reshape(groups, steps, n)
    for r in range(groups):
        outs[r][...] = sums[(position // size) ^ r]


def tree_kernel(steps, levels_ref, table_ref, left_hbm, right_hbm, table_hbm, total_ref, left_ref, right_ref, sems):
    base = steps // 4

    def first(t):
        return mm(table_ref[levels_ref[0, t]], table_ref[levels_ref[0, t + 1]])

    def node(k):
        return mm(left_ref[k], right_ref[k])

    def first_pairs(ks):
        made = [(first(4 * k), first(4 * k + 2)) for k in ks]
        for k, (a, b) in zip(ks, made):
            left_ref[k] = pair(a)
            right_ref[k] = pair(b)

    def later_pairs(ks):
        made = [(node(2 * (k - base)), node(2 * (k - base) + 1)) for k in ks]
        for k, (a, b) in zip(ks, made):
            left_ref[k] = pair(a)
            right_ref[k] = pair(b)

    def run(fn, start, count):
        if count <= 4:
            fn(list(range(start, start + count)))
            return

        def body(i, c):
            fn([start + 4 * i + k for k in range(4)])
            return c

        lax.fori_loop(0, count // 4, body, 0)

    copies = [pltpu.make_async_copy(table_ref, table_hbm, sems.at[0])]
    copies[0].start()

    def store(start, count):
        for ref, hbm in ((right_ref, right_hbm), (left_ref, left_hbm)):
            part = pl.ds(start, count)
            copies.append(pltpu.make_async_copy(ref.at[part], hbm.at[part], sems.at[len(copies)]))
            copies[-1].start()

    run(first_pairs, 0, base)
    store(0, base)
    run(later_pairs, base, base // 2)
    store(base, base // 2)
    count, start = base // 4, base + base // 2
    while count >= 1:
        run(later_pairs, start, count)
        start += count
        count //= 2
    store(base + base // 2, base // 2 - 1)
    total_ref[...] = pair(node(start - 1))
    for copy in copies:
        copy.wait()


def local_kernel(pos_ref, levels_ref, gain_ref, init_ref, total_ref, table_hbm, right_hbm, *refs):
    parts, (lefts_ref, shift_ref, drive_ref, table_ref, right_ref, sems) = refs[:-6], refs[-6:]
    steps, n = drive_ref.shape
    base = steps // 4
    copies = [
        pltpu.make_async_copy(table_hbm, table_ref, sems.at[0]),
        pltpu.make_async_copy(right_hbm.at[pl.ds(0, base)], right_ref.at[pl.ds(0, base)], sems.at[1]),
        pltpu.make_async_copy(right_hbm.at[pl.ds(base, base - 1)], right_ref.at[pl.ds(base, base - 1)], sems.at[2]),
    ]
    for copy in copies:
        copy.start()
    measured = parts[0][...]
    for part in parts[1:]:
        measured += part[...]
    drive_ref[...] = lax.dot_general(measured.astype(BF16), gain_ref[...], NT, preferred_element_type=F32)

    states = [row(drive_ref, t) for t in range(steps)]
    at, offset = 0, 0
    for level in range(steps.bit_length() - 1):
        if level < 3:
            copies[level].wait()
        later = []
        for i in range(len(states) // 2):
            mat = table_ref[levels_ref[0, 2 * i + 1]] if level == 0 else right_ref[offset + i]
            lefts_ref[pl.ds(at + i, 1), :] = states[2 * i][:1]
            later.append(vm(states[2 * i], mat) + states[2 * i + 1])
        at += len(later)
        if level > 0:
            offset += len(later)
        states = later
    lefts_ref[pl.ds(at, 1), :] = states[0][:1]
    first = jnp.where(pos_ref[0] == 0, row(init_ref, 0), 0.0)
    shift_ref[...] = states[0] + vm(first, total_ref[...])


def group_kernel(size, pos_ref, after_ref, *refs):
    blocks = refs[:size]
    all_ref, prefix_ref, whole_ref = refs[size:]
    n = whole_ref.shape[0]
    member = pos_ref[0] % size
    for r in range(size):
        all_ref[member ^ r] = blocks[r][...]
    rows, cols = (lax.broadcasted_iota(jnp.int32, (n, n), d) for d in (0, 1))
    prefix = pair((rows == cols).astype(F32))
    run = all_ref[0]
    for q in range(1, size):
        prefix = jnp.where(member == q, run, prefix)
        run = pair(mm(run, all_ref[q]))
    prefix_ref[...] = prefix
    whole_ref[...] = run


def beside_kernel(size, pos_ref, all_ref, *refs):
    shifts = refs[:size]
    before_ref, whole_ref, held_ref = refs[size:]
    member = pos_ref[0] % size
    for r in range(size):
        held_ref[member ^ r] = shifts[r][...]
    run, before = held_ref[0], jnp.zeros(before_ref.shape, F32)
    for q in range(1, size):
        before = jnp.where(member == q, run, before)
        run = vm(run, all_ref[q]) + held_ref[q]
    before_ref[...] = before
    whole_ref[...] = run


def final_kernel(size, groups, pos_ref, levels_ref, init_ref, prefix_ref, before_ref, total_ref, lefts_ref, left_ref, table_hbm, *refs):
    shifts, wholes = refs[: groups - 1], refs[groups - 1 : 2 * groups - 3]
    out_ref, sums_ref, table_ref, sem = refs[2 * groups - 3 :]
    copy = pltpu.make_async_copy(table_hbm, table_ref, sem)
    copy.start()
    steps, n = lefts_ref.shape
    position = pos_ref[0]
    group = position // size
    for r in range(1, groups):
        sums_ref[group ^ r] = shifts[r - 1][...]
    state = jnp.zeros((8, n), F32)
    for r in range(groups - 1, 0, -1):
        if r < groups - 1:
            state = jnp.where(group > r, vm(state, wholes[r - 1][...]), 0.0)
        state += jnp.where(group >= r, sums_ref[jnp.maximum(group - r, 0)], 0.0)
    first = jnp.where(position == 0, row(init_ref, 0), 0.0)
    state = vm(state, prefix_ref[...]) + before_ref[...] + first
    out_ref[pl.ds(steps - 1, 1), :] = (vm(state, total_ref[...]) + row(lefts_ref, steps - 1))[:1]
    levels = steps.bit_length() - 1
    starts = [state]
    sizes = [steps >> (level + 1) for level in range(levels)]
    for level in reversed(range(levels)):
        if level == 0:
            copy.wait()
        at, offset = sum(sizes[:level]), sum(sizes[1:level])
        later = []
        for i, x in enumerate(starts):
            mat = table_ref[levels_ref[0, 2 * i]] if level == 0 else left_ref[offset + i]
            later += [x, vm(x, mat) + row(lefts_ref, at + i)]
        starts = later
    for t in range(1, steps):
        out_ref[pl.ds(t - 1, 1), :] = starts[t][:1]


def shards(count, frames, levels, initial_state, transitions, gain, pixel_mode, pixel_weight):
    n = gain.shape[0]
    kinds = transitions.shape[0]
    pixels, length = frames.shape
    steps = length // count
    position = lax.axis_index("tm").astype(jnp.int32)[None]
    pairs = steps // 2 - 1
    dma = pltpu.SemaphoreType.DMA
    size = 1
    while count % (2 * size) == 0 and 4 * size * size <= count:
        size *= 2
    groups = count // size

    def swaps(x, step, times):
        x = x if isinstance(x, list) else [x] * (times - 1)
        return [
            lax.ppermute(a, "tm", [(j, j ^ (r * step)) for j in range(count)]) for a, r in zip(x, range(1, times))
        ]

    one_map = shape((n, 2 * n), BF16)
    table_shape = shape((kinds, n, 2 * n), BF16)
    cuts = 4
    turn = pixels % 128 == 0 and length % (128 * cuts) == 0
    small = [levels[None], initial_state[None], gain]
    if turn:
        small += [pixel_mode.reshape(count, pixels), pixel_weight.reshape(count, pixels)]
    given = [hbm(a) for a in [transitions] + small + [frames] * turn]
    outs = [table_shape] + [shape(a.shape, a.dtype) for a in small]
    buffers = [pltpu.VMEM(transitions.shape, F32)]
    if turn:
        outs += [shape((groups, steps, pixels), BF16)] * size
        buffers += [pltpu.VMEM(frames.shape, BF16), pltpu.VMEM((length, pixels), BF16)]
    table, levels, initial_state, gain, *rest = call(
        functools.partial(front_kernel, cuts, len(small), size), "front", 5, 0, 4 * MIB,
        out_shape=outs,
        in_specs=[SMEM] + [HBM] * len(given),
        out_specs=[VMEM] * len(outs),
        scratch_shapes=buffers + [dma((cuts + 4 + len(small),))],
    )(position, *given)
    if turn:
        mode, weight, slab, *slabs = rest
        first, *parts = call(
            functools.partial(project_kernel, size), "project", 4, 1 << 25, MIB,
            out_shape=[shape((steps, n), F32)] * groups,
            in_specs=[SMEM] + [VMEM] * (2 + size),
            out_specs=[VMEM] * groups,
            scratch_shapes=[pltpu.VMEM((groups, steps, n), F32), pltpu.VMEM((count, pixels), F32)],
        )(position, mode, weight, slab, *swaps(slabs, 1, size))
        parts = [first] + swaps(parts, size, groups)
    else:
        x = lax.all_to_all(frames, "tm", split_axis=1, concat_axis=0, tiled=True)
        channels = jnp.arange(n, dtype=jnp.int32)
        projector = jnp.where(pixel_mode[None, :] == channels[:, None], pixel_weight[None, :], jnp.zeros((), BF16))
        parts = [lax.dot_general(x, projector, (((0,), (1,)), ((), ())), preferred_element_type=F32)]

    tree = pltpu.VMEM((pairs, n, 2 * n), BF16)
    table_vmem = pltpu.VMEM(table_shape.shape, BF16)
    maps = pltpu.HBM((pairs, n, 2 * n), BF16)
    left, right, table, total = call(
        functools.partial(tree_kernel, steps), "tree_of_maps", 8, 2 * steps * n**3 * 4, 8 * MIB,
        out_shape=[maps, maps, pltpu.HBM(table_shape.shape, BF16), one_map],
        in_specs=[SMEM, VMEM],
        out_specs=[HBM, HBM, HBM, VMEM],
        scratch_shapes=[tree, tree, dma((7,))],
    )(levels, table)
    right, table = hbm(right), hbm(table)

    vector = shape((8, n), F32)

    members = swaps(total, 1, size)
    lefts, shift = call(
        local_kernel, "local_states", 8, 1 << 27, 6 * MIB,
        out_shape=[shape((steps, n), F32), vector],
        in_specs=[SMEM, SMEM] + [VMEM] * 3 + [HBM] * 2 + [VMEM] * len(parts),
        out_specs=[VMEM] * 2,
        scratch_shapes=[pltpu.VMEM((steps, n), F32), table_vmem, tree, dma((3,))],
    )(position, levels, gain, initial_state, total, table, right, *parts)
    shifts = swaps(shift, 1, size)

    group_maps, prefix, whole = call(
        functools.partial(group_kernel, size), "group_maps", 2, 1 << 24, MIB,
        out_shape=[shape((size, n, 2 * n), BF16), one_map, one_map],
        in_specs=[SMEM] + [VMEM] * (1 + size),
        out_specs=[VMEM] * 3,
    )(position, shifts[0], total, *members)
    wholes = [
        lax.ppermute(whole, "tm", [(j, (j + r * size) % count) for j in range(count)]) for r in range(1, groups - 1)
    ]
    before, carried = call(
        functools.partial(beside_kernel, size), "group_states", 2, 1 << 20, MIB // 4,
        out_shape=[vector, vector],
        in_specs=[SMEM] + [VMEM] * (1 + size),
        out_specs=[VMEM] * 2,
        scratch_shapes=[pltpu.VMEM((size, 8, n), F32)],
    )(position, group_maps, shift, *shifts)

    return call(
        functools.partial(final_kernel, size, groups), "estimates", 6, 1 << 23, 5 * MIB,
        out_shape=shape((steps, n), F32),
        in_specs=[SMEM, SMEM] + [VMEM] * 6 + [HBM] + [VMEM] * (2 * groups - 3),
        out_specs=VMEM,
        scratch_shapes=[pltpu.VMEM((groups, 8, n), F32), table_vmem, dma(())],
    )(position, levels, initial_state, prefix, before, total, lefts, left, table, *swaps(carried, size, groups), *wholes)


def solution(mesh):
    in_specs = (P("tm", "parts"), P(("parts", "tm")), P("parts"), P(), P(), P(), P())
    out_specs = P(("parts", "tm"), None)
    return jax.shard_map(
        functools.partial(shards, mesh.shape["tm"]),
        mesh=mesh,
        in_specs=in_specs,
        out_specs=out_specs,
        check_vma=False,
    )
```

```python
import functools

import jax
import jax.numpy as jnp
from jax import lax
from jax.experimental import pallas as pl
from jax.experimental.pallas import tpu as pltpu
from jax.sharding import PartitionSpec as P

F32 = jnp.float32
BF16 = jnp.bfloat16
MIB = 1 << 20
NT = (((1,), (1,)), ((), ()))
VMEM = pl.BlockSpec(memory_space=pltpu.VMEM)
SMEM = pl.BlockSpec(memory_space=pltpu.SMEM)
HBM = pl.BlockSpec(memory_space=pltpu.HBM)
shape = jax.ShapeDtypeStruct


def hbm(x):
    return pltpu.with_memory_space_constraint(x, pltpu.HBM)


def call(kernel, name, mib, **kw):
    return pl.pallas_call(
        kernel,
        name=name,
        compiler_params=pltpu.CompilerParams(vmem_limit_bytes=mib * MIB),
        cost_estimate=pl.CostEstimate(flops=1, bytes_accessed=1, transcendentals=0),
        **kw,
    )


def pair(x):
    high = x.astype(BF16)
    mid = (x - high.astype(F32)).astype(BF16)
    return jnp.concatenate([high, mid], axis=1)


def mm(left, right):
    n = right.shape[0]
    out = jnp.dot(left, jnp.concatenate([right, right], axis=0), preferred_element_type=F32)
    return out[:, :n] + out[:, n:]


def vm(vec, mat):
    high = vec.astype(BF16).astype(F32)
    rows = jnp.concatenate([high, vec - high], axis=0).astype(BF16)
    out = jnp.dot(rows, mat, preferred_element_type=F32)
    n = vec.shape[1]
    out = out[:, :n] + out[:, n:]
    return out[:8] + out[8:]


def row(ref, t):
    return jnp.broadcast_to(ref[pl.ds(t, 1), :], (8, ref.shape[1]))


def front_kernel(cuts, extra, size, pos_ref, trans_ref, *refs):
    given, refs = refs[:extra], refs[extra:]
    turn = len(refs) > extra + 3
    if turn:
        frames_ref, table_ref, *moved = refs[: 2 + extra]
        slabs = refs[2 + extra : 2 + extra + size]
        trans, frames, turned, sems = refs[2 + extra + size :]
        width = frames.shape[1] // cuts
        parts = [pl.ds(k * width, width) for k in range(cuts)]
        ins = [
            pltpu.make_async_copy(frames_ref.at[:, part], frames.at[:, part], sems.at[k])
            for k, part in enumerate(parts)
        ]
        for copy in ins:
            copy.start()
    else:
        table_ref, *moved, trans, sems = refs
    kinds = trans.shape[0]
    few = kinds // 4
    maps = [
        pltpu.make_async_copy(trans_ref.at[pl.ds(k * few, few)], trans.at[pl.ds(k * few, few)], sems.at[cuts + k])
        for k in range(4)
    ]
    moves = [pltpu.make_async_copy(a, b, sems.at[cuts + 4 + k]) for k, (a, b) in enumerate(zip(given, moved))]
    for copy in maps + moves:
        copy.start()
    if turn:
        for k in range(cuts):
            ins[k].wait()
            turned[parts[k], :] = frames[:, parts[k]].T
        member = pos_ref[0] % size
        groups, steps, _ = slabs[0].shape
        for r in range(size):
            for g in range(groups):
                start = pl.multiple_of((g * size + (member ^ r)) * steps, steps)
                slabs[r][g] = turned[pl.ds(start, steps), :]
    for k in range(4):
        maps[k].wait()
        for q in range(k * few, (k + 1) * few):
            table_ref[q] = pair(trans[q].T)
    for copy in moves:
        copy.wait()


def project_kernel(size, pos_ref, after_ref, mode_ref, weight_ref, *refs):
    slabs, outs, (sums, weights) = refs[:size], refs[size:-2], refs[-2:]
    weights[...] = weight_ref[...].astype(F32)
    groups, steps, width = slabs[0].shape
    n = sums.shape[2]
    position = pos_ref[0]
    channel = lax.broadcasted_iota(jnp.int32, (n, width), 0)
    total = jnp.zeros((groups * steps, n), F32)
    for r in range(size):
        here = pl.ds(position ^ r, 1)
        weight = jnp.broadcast_to(weights[here, :], (n, width))
        projector = jnp.where(mode_ref[here, :] == channel, weight, 0.0).astype(BF16)
        total += lax.dot_general(slabs[r][...].reshape(groups * steps, width), projector, NT, preferred_element_type=F32)
    sums[...] = total.reshape(groups, steps, n)
    for r in range(groups):
        outs[r][...] = sums[(position // size) ^ r]


def tree_kernel(steps, levels_ref, table_ref, left_hbm, right_hbm, total_ref, left_ref, right_ref, sems):
    base = steps // 4

    def first(t):
        return mm(table_ref[levels_ref[0, t]], table_ref[levels_ref[0, t + 1]])

    def node(k):
        return mm(left_ref[k], right_ref[k])

    def first_pairs(ks):
        made = [(first(4 * k), first(4 * k + 2)) for k in ks]
        for k, (a, b) in zip(ks, made):
            left_ref[k] = pair(a)
            right_ref[k] = pair(b)

    def later_pairs(ks):
        made = [(node(2 * (k - base)), node(2 * (k - base) + 1)) for k in ks]
        for k, (a, b) in zip(ks, made):
            left_ref[k] = pair(a)
            right_ref[k] = pair(b)

    def run(fn, start, count):
        if count <= 4:
            fn(list(range(start, start + count)))
            return

        def body(i, c):
            fn([start + 4 * i + k for k in range(4)])
            return c

        lax.fori_loop(0, count // 4, body, 0)

    copies = []

    def store(start, count):
        for ref, hbm in ((right_ref, right_hbm), (left_ref, left_hbm)):
            part = pl.ds(start, count)
            copies.append(pltpu.make_async_copy(ref.at[part], hbm.at[part], sems.at[len(copies)]))
            copies[-1].start()

    run(first_pairs, 0, base)
    store(0, base)
    run(later_pairs, base, base // 2)
    store(base, base // 2)
    count, start = base // 4, base + base // 2
    while count >= 1:
        run(later_pairs, start, count)
        start += count
        count //= 2
    store(base + base // 2, base // 2 - 1)
    total_ref[...] = pair(node(start - 1))
    for copy in copies:
        copy.wait()


def local_kernel(pos_ref, levels_ref, gain_ref, init_ref, total_ref, table_ref, right_hbm, *refs):
    parts, (lefts_ref, own_ref, drive_ref, right_ref, sems) = refs[:-5], refs[-5:]
    steps, n = drive_ref.shape
    base = steps // 4
    copies = [
        pltpu.make_async_copy(right_hbm.at[pl.ds(0, base)], right_ref.at[pl.ds(0, base)], sems.at[0]),
        pltpu.make_async_copy(right_hbm.at[pl.ds(base, base - 1)], right_ref.at[pl.ds(base, base - 1)], sems.at[1]),
    ]
    for copy in copies:
        copy.start()
    measured = parts[0][...]
    for part in parts[1:]:
        measured += part[...]
    drive_ref[...] = lax.dot_general(measured.astype(BF16), gain_ref[...], NT, preferred_element_type=F32)

    states = [row(drive_ref, t) for t in range(steps)]
    at, offset = 0, 0
    for level in range(steps.bit_length() - 1):
        if level in (1, 2):
            copies[level - 1].wait()
        later = []
        for i in range(len(states) // 2):
            mat = table_ref[levels_ref[0, 2 * i + 1]] if level == 0 else right_ref[offset + i]
            lefts_ref[pl.ds(at + i, 1), :] = states[2 * i][:1]
            later.append(vm(states[2 * i], mat) + states[2 * i + 1])
        at += len(later)
        if level > 0:
            offset += len(later)
        states = later
    lefts_ref[pl.ds(at, 1), :] = states[0][:1]
    first = jnp.where(pos_ref[0] == 0, row(init_ref, 0), 0.0)
    total = total_ref[...]
    own_ref[pl.ds(0, n), :] = total
    own_ref[pl.ds(n, 16), :] = rows16(states[0] + vm(first, total))


def rows16(vec):
    high = vec.astype(BF16).astype(F32)
    both = jnp.concatenate([high, vec - high], axis=1)
    return jnp.concatenate([both, both], axis=0).astype(BF16)


def rows8(rows):
    both = rows.astype(F32)
    n = rows.shape[1] // 2
    return both[:8, :n] + both[:8, n:]


def group_kernel(size, pos_ref, *refs):
    blocks = refs[:size]
    prefix_ref, before_ref, mine_ref, shift_ref, all_ref = refs[size:]
    n = prefix_ref.shape[0]
    member = pos_ref[0] % size
    for r in range(size):
        all_ref[member ^ r] = blocks[r][...]

    def block(q):
        return all_ref[q, :n, :], rows8(all_ref[q, n:, :])

    rows, cols = (lax.broadcasted_iota(jnp.int32, (n, n), d) for d in (0, 1))
    prefix, before = pair((rows == cols).astype(F32)), jnp.zeros((8, n), F32)
    run, vec = block(0)
    for q in range(1, size):
        here = member == q
        prefix, before = jnp.where(here, run, prefix), jnp.where(here, vec, before)
        step, shift = block(q)
        vec = vm(vec, step) + shift
        run = pair(mm(run, step))
    prefix_ref[...] = prefix
    before_ref[...] = before
    mine_ref[pl.ds(0, n), :] = run
    mine_ref[pl.ds(n, 16), :] = rows16(vec)
    shift_ref[...] = rows16(vec)


def final_kernel(size, pos_ref, levels_ref, init_ref, prefix_ref, before_ref, total_ref, lefts_ref, left_ref, table_ref, *refs):
    got, out_ref = refs[:-1], refs[-1]
    steps, n = lefts_ref.shape
    position = pos_ref[0]
    group = position // size
    state = jnp.zeros((8, n), F32)
    for r in range(len(got), 0, -1):
        rows = got[r - 1].shape[0]
        if rows > 16:
            state = jnp.where(group > r, vm(state, got[r - 1][pl.ds(0, n), :]), 0.0)
        state += jnp.where(group >= r, rows8(got[r - 1][pl.ds(rows - 16, 16), :]), 0.0)
    first = jnp.where(position == 0, row(init_ref, 0), 0.0)
    state = vm(state, prefix_ref[...]) + before_ref[...] + first
    out_ref[pl.ds(steps - 1, 1), :] = (vm(state, total_ref[...]) + row(lefts_ref, steps - 1))[:1]
    levels = steps.bit_length() - 1
    starts = [state]
    sizes = [steps >> (level + 1) for level in range(levels)]
    for level in reversed(range(levels)):
        at, offset = sum(sizes[:level]), sum(sizes[1:level])
        later = []
        for i, x in enumerate(starts):
            mat = table_ref[levels_ref[0, 2 * i]] if level == 0 else left_ref[offset + i]
            later += [x, vm(x, mat) + row(lefts_ref, at + i)]
        starts = later
    for t in range(1, steps):
        out_ref[pl.ds(t - 1, 1), :] = starts[t][:1]


def shards(count, frames, levels, initial_state, transitions, gain, pixel_mode, pixel_weight):
    n = gain.shape[0]
    kinds = transitions.shape[0]
    pixels, length = frames.shape
    steps = length // count
    position = lax.axis_index("tm").astype(jnp.int32)[None]
    pairs = steps // 2 - 1
    dma = pltpu.SemaphoreType.DMA
    size = 1
    while count % (2 * size) == 0 and 4 * size * size <= count:
        size *= 2
    groups = count // size

    def swaps(x, step, times):
        x = x if isinstance(x, list) else [x] * (times - 1)
        return [
            lax.ppermute(a, "tm", [(j, j ^ (r * step)) for j in range(count)]) for a, r in zip(x, range(1, times))
        ]

    one_map = shape((n, 2 * n), BF16)
    table_shape = shape((kinds, n, 2 * n), BF16)
    cuts = 4
    turn = pixels % 128 == 0 and length % (128 * cuts) == 0
    small = [levels[None], initial_state[None], gain]
    if turn:
        small += [pixel_mode.reshape(count, pixels), pixel_weight.reshape(count, pixels)]
    given = [hbm(a) for a in [transitions] + small + [frames] * turn]
    outs = [table_shape] + [shape(a.shape, a.dtype) for a in small]
    buffers = [pltpu.VMEM(transitions.shape, F32)]
    if turn:
        outs += [shape((groups, steps, pixels), BF16)] * size
        buffers += [pltpu.VMEM(frames.shape, BF16), pltpu.VMEM((length, pixels), BF16)]
    table, levels, initial_state, gain, *rest = call(
        functools.partial(front_kernel, cuts, len(small), size), "front", 5,
        out_shape=outs,
        in_specs=[SMEM] + [HBM] * len(given),
        out_specs=[VMEM] * len(outs),
        scratch_shapes=buffers + [dma((cuts + 4 + len(small),))],
    )(position, *given)
    tree = pltpu.VMEM((pairs, n, 2 * n), BF16)
    maps = pltpu.HBM((pairs, n, 2 * n), BF16)
    left, right, total = call(
        functools.partial(tree_kernel, steps), "tree_of_maps", 8,
        out_shape=[maps, maps, one_map],
        in_specs=[SMEM, VMEM],
        out_specs=[HBM, HBM, VMEM],
        scratch_shapes=[tree, tree, dma((6,))],
    )(levels, table)

    if turn:
        mode, weight, slab, *slabs = rest
        first, *parts = call(
            functools.partial(project_kernel, size), "project", 4,
            out_shape=[shape((steps, n), F32)] * groups,
            in_specs=[SMEM] + [VMEM] * (3 + size),
            out_specs=[VMEM] * groups,
            scratch_shapes=[pltpu.VMEM((groups, steps, n), F32), pltpu.VMEM((count, pixels), F32)],
        )(position, total, mode, weight, slab, *swaps(slabs, 1, size))
        parts = [first] + swaps(parts, size, groups)
    else:
        x = lax.all_to_all(frames, "tm", split_axis=1, concat_axis=0, tiled=True)
        channels = jnp.arange(n, dtype=jnp.int32)
        projector = jnp.where(pixel_mode[None, :] == channels[:, None], pixel_weight[None, :], jnp.zeros((), BF16))
        parts = [lax.dot_general(x, projector, (((0,), (1,)), ((), ())), preferred_element_type=F32)]

    block = shape((n + 16, 2 * n), BF16)
    lefts, own = call(
        local_kernel, "local_states", 8,
        out_shape=[shape((steps, n), F32), block],
        in_specs=[SMEM, SMEM] + [VMEM] * 4 + [HBM] + [VMEM] * len(parts),
        out_specs=[VMEM] * 2,
        scratch_shapes=[pltpu.VMEM((steps, n), F32), tree, dma((2,))],
    )(position, levels, gain, initial_state, total, table, hbm(right), *parts)
    prefix, before, mine, carried = call(
        functools.partial(group_kernel, size), "group_maps", 2,
        out_shape=[one_map, shape((8, n), F32), block, shape((16, 2 * n), BF16)],
        in_specs=[SMEM] + [VMEM] * size,
        out_specs=[VMEM] * 4,
        scratch_shapes=[pltpu.VMEM((size, n + 16, 2 * n), BF16)],
    )(position, own, *swaps(own, 1, size))
    got = [
        lax.ppermute(mine if r < groups - 1 else carried, "tm", [(j, (j + r * size) % count) for j in range(count)])
        for r in range(1, groups)
    ]

    return call(
        functools.partial(final_kernel, size), "estimates", 6,
        out_shape=shape((steps, n), F32),
        in_specs=[SMEM, SMEM] + [VMEM] * (7 + len(got)),
        out_specs=VMEM,
    )(position, levels, initial_state, prefix, before, total, lefts, left, table, *got)


def solution(mesh):
    in_specs = (P("tm", "parts"), P(("parts", "tm")), P("parts"), P(), P(), P(), P())
    out_specs = P(("parts", "tm"), None)
    return jax.shard_map(
        functools.partial(shards, mesh.shape["tm"]),
        mesh=mesh,
        in_specs=in_specs,
        out_specs=out_specs,
        check_vma=False,
    )
```

```python
import functools

import jax
import jax.numpy as jnp
from jax import lax
from jax.experimental import pallas as pl
from jax.experimental.pallas import tpu as pltpu
from jax.sharding import PartitionSpec as P

F32 = jnp.float32
BF16 = jnp.bfloat16
MIB = 1 << 20
NT = (((1,), (1,)), ((), ()))
VMEM = pl.BlockSpec(memory_space=pltpu.VMEM)
SMEM = pl.BlockSpec(memory_space=pltpu.SMEM)
HBM = pl.BlockSpec(memory_space=pltpu.HBM)
shape = jax.ShapeDtypeStruct


def hbm(x):
    return pltpu.with_memory_space_constraint(x, pltpu.HBM)


def call(kernel, name, mib, **kw):
    return pl.pallas_call(
        kernel,
        name=name,
        compiler_params=pltpu.CompilerParams(vmem_limit_bytes=mib * MIB),
        cost_estimate=pl.CostEstimate(flops=1, bytes_accessed=1, transcendentals=0),
        **kw,
    )


def pair(x):
    high = x.astype(BF16)
    mid = (x - high.astype(F32)).astype(BF16)
    return jnp.concatenate([high, mid], axis=1)


def mm(left, right):
    n = right.shape[0]
    out = jnp.dot(left, jnp.concatenate([right, right], axis=0), preferred_element_type=F32)
    return out[:, :n] + out[:, n:]


def vm(vec, mat):
    high = vec.astype(BF16).astype(F32)
    rows = jnp.concatenate([high, vec - high], axis=0).astype(BF16)
    out = jnp.dot(rows, mat, preferred_element_type=F32)
    n = vec.shape[1]
    out = out[:, :n] + out[:, n:]
    return out[:8] + out[8:]


def row(ref, t):
    return jnp.broadcast_to(ref[pl.ds(t, 1), :], (8, ref.shape[1]))


def front_kernel(cuts, extra, size, pos_ref, trans_ref, *refs):
    given, refs = refs[:extra], refs[extra:]
    turn = len(refs) > extra + 3
    if turn:
        frames_ref, table_ref, *moved = refs[: 2 + extra]
        slabs = refs[2 + extra : 2 + extra + size]
        trans, frames, turned, sems = refs[2 + extra + size :]
        width = frames.shape[1] // cuts
        parts = [pl.ds(k * width, width) for k in range(cuts)]
        ins = [
            pltpu.make_async_copy(frames_ref.at[:, part], frames.at[:, part], sems.at[k])
            for k, part in enumerate(parts)
        ]
        for copy in ins:
            copy.start()
    else:
        table_ref, *moved, trans, sems = refs
    kinds = trans.shape[0]
    few = kinds // 4
    maps = [
        pltpu.make_async_copy(trans_ref.at[pl.ds(k * few, few)], trans.at[pl.ds(k * few, few)], sems.at[cuts + k])
        for k in range(4)
    ]
    moves = [pltpu.make_async_copy(a, b, sems.at[cuts + 4 + k]) for k, (a, b) in enumerate(zip(given, moved))]
    for copy in maps + moves:
        copy.start()
    if turn:
        for k in range(cuts):
            ins[k].wait()
            turned[parts[k], :] = frames[:, parts[k]].T
        member = pos_ref[0] % size
        groups, steps, _ = slabs[0].shape
        for r in range(size):
            for g in range(groups):
                start = pl.multiple_of((g * size + (member ^ r)) * steps, steps)
                slabs[r][g] = turned[pl.ds(start, steps), :]
    for k in range(4):
        maps[k].wait()
        for q in range(k * few, (k + 1) * few):
            table_ref[q] = pair(trans[q].T)
    for copy in moves:
        copy.wait()


def project_kernel(size, pos_ref, after_ref, mode_ref, weight_ref, *refs):
    slabs, outs, (sums, weights) = refs[:size], refs[size:-2], refs[-2:]
    weights[...] = weight_ref[...].astype(F32)
    groups, steps, width = slabs[0].shape
    n = sums.shape[2]
    position = pos_ref[0]
    channel = lax.broadcasted_iota(jnp.int32, (n, width), 0)
    total = jnp.zeros((groups * steps, n), F32)
    for r in range(size):
        here = pl.ds(position ^ r, 1)
        weight = jnp.broadcast_to(weights[here, :], (n, width))
        projector = jnp.where(mode_ref[here, :] == channel, weight, 0.0).astype(BF16)
        total += lax.dot_general(slabs[r][...].reshape(groups * steps, width), projector, NT, preferred_element_type=F32)
    sums[...] = total.reshape(groups, steps, n)
    for r in range(groups):
        outs[r][...] = sums[(position // size) ^ r]


def each(fn, start, count):
    if count <= 4:
        fn(list(range(start, start + count)))
        return

    def body(i, c):
        fn([start + 4 * i + k for k in range(4)])
        return c

    lax.fori_loop(0, count // 4, body, 0)


def keep(left_ref, right_ref, ks, made):
    for k, (a, b) in zip(ks, made):
        left_ref[k] = pair(a)
        right_ref[k] = pair(b)


def low_tree_kernel(steps, levels_ref, table_ref, left_hbm, right_hbm, mark_ref, left_ref, right_ref, sems):
    base = steps // 4
    copies = []

    def first(t):
        return mm(table_ref[levels_ref[0, t]], table_ref[levels_ref[0, t + 1]])

    def first_pairs(ks):
        keep(left_ref, right_ref, ks, [(first(4 * k), first(4 * k + 2)) for k in ks])

    def node(k):
        return mm(left_ref[k], right_ref[k])

    def later_pairs(ks):
        keep(left_ref, right_ref, ks, [(node(2 * (k - base)), node(2 * (k - base) + 1)) for k in ks])

    def store(start, count):
        for ref, hbm_ref in ((right_ref, right_hbm), (left_ref, left_hbm)):
            part = pl.ds(start, count)
            copies.append(pltpu.make_async_copy(ref.at[part], hbm_ref.at[part], sems.at[len(copies)]))
            copies[-1].start()

    each(first_pairs, 0, base)
    store(0, base)
    each(later_pairs, base, base // 2)
    store(base, base // 2)
    mark_ref[...] = jnp.zeros_like(mark_ref)
    for copy in copies:
        copy.wait()


def high_tree_kernel(base, after_ref, low_left, low_right, left_out, right_out, total_ref, left_ref, right_ref, sems):
    half = base // 2
    part = pl.ds(base, half)
    copies = [
        pltpu.make_async_copy(low_left.at[part], left_ref.at[pl.ds(0, half)], sems.at[0]),
        pltpu.make_async_copy(low_right.at[part], right_ref.at[pl.ds(0, half)], sems.at[1]),
    ]
    for copy in copies:
        copy.start()
    for copy in copies:
        copy.wait()

    def node(k):
        return mm(left_ref[k], right_ref[k])

    count, start = half // 2, half
    while count >= 1:
        ks = list(range(start, start + count))
        keep(left_ref, right_ref, ks, [(node(2 * (k - half)), node(2 * (k - half) + 1)) for k in ks])
        start += count
        count //= 2
    total_ref[...] = pair(node(start - 1))
    left_out[...] = left_ref[pl.ds(half, half - 1)]
    right_out[...] = right_ref[pl.ds(half, half - 1)]


def local_kernel(pos_ref, levels_ref, gain_ref, init_ref, total_ref, table_ref, high_ref, right_hbm, *refs):
    parts, (lefts_ref, own_ref, drive_ref, right_ref, sems) = refs[:-5], refs[-5:]
    steps, n = drive_ref.shape
    base = steps // 4
    copies = [
        pltpu.make_async_copy(right_hbm.at[pl.ds(0, base)], right_ref.at[pl.ds(0, base)], sems.at[0]),
        pltpu.make_async_copy(right_hbm.at[pl.ds(base, base // 2)], right_ref.at[pl.ds(base, base // 2)], sems.at[1]),
    ]
    for copy in copies:
        copy.start()
    measured = parts[0][...]
    for part in parts[1:]:
        measured += part[...]
    drive_ref[...] = lax.dot_general(measured.astype(BF16), gain_ref[...], NT, preferred_element_type=F32)

    states = [row(drive_ref, t) for t in range(steps)]
    at, offset = 0, 0
    for level in range(steps.bit_length() - 1):
        if level in (1, 2):
            copies[level - 1].wait()
        later = []
        for i in range(len(states) // 2):
            if level == 0:
                mat = table_ref[levels_ref[0, 2 * i + 1]]
            elif level < 3:
                mat = right_ref[offset + i]
            else:
                mat = high_ref[offset + i - base - base // 2]
            lefts_ref[pl.ds(at + i, 1), :] = states[2 * i][:1]
            later.append(vm(states[2 * i], mat) + states[2 * i + 1])
        at += len(later)
        if level > 0:
            offset += len(later)
        states = later
    lefts_ref[pl.ds(at, 1), :] = states[0][:1]
    first = jnp.where(pos_ref[0] == 0, row(init_ref, 0), 0.0)
    total = total_ref[...]
    own_ref[pl.ds(0, n), :] = total
    own_ref[pl.ds(n, 16), :] = rows16(states[0] + vm(first, total))


def rows16(vec):
    high = vec.astype(BF16).astype(F32)
    both = jnp.concatenate([high, vec - high], axis=1)
    return jnp.concatenate([both, both], axis=0).astype(BF16)


def rows8(rows):
    both = rows.astype(F32)
    n = rows.shape[1] // 2
    return both[:8, :n] + both[:8, n:]


def group_kernel(size, pos_ref, *refs):
    blocks = refs[:size]
    prefix_ref, before_ref, mine_ref, shift_ref, all_ref = refs[size:]
    n = prefix_ref.shape[0]
    member = pos_ref[0] % size
    for r in range(size):
        all_ref[member ^ r] = blocks[r][...]

    def block(q):
        return all_ref[q, :n, :], rows8(all_ref[q, n:, :])

    rows, cols = (lax.broadcasted_iota(jnp.int32, (n, n), d) for d in (0, 1))
    prefix, before = pair((rows == cols).astype(F32)), jnp.zeros((8, n), F32)
    run, vec = block(0)
    for q in range(1, size):
        here = member == q
        prefix, before = jnp.where(here, run, prefix), jnp.where(here, vec, before)
        step, shift = block(q)
        vec = vm(vec, step) + shift
        run = pair(mm(run, step))
    prefix_ref[...] = prefix
    before_ref[...] = before
    mine_ref[pl.ds(0, n), :] = run
    mine_ref[pl.ds(n, 16), :] = rows16(vec)
    shift_ref[...] = rows16(vec)


def final_kernel(size, pos_ref, levels_ref, init_ref, prefix_ref, before_ref, total_ref, lefts_ref, left_ref, high_ref, table_ref, *refs):
    got, out_ref = refs[:-1], refs[-1]
    steps, n = lefts_ref.shape
    position = pos_ref[0]
    group = position // size
    state = jnp.zeros((8, n), F32)
    for r in range(len(got), 0, -1):
        rows = got[r - 1].shape[0]
        if rows > 16:
            state = jnp.where(group > r, vm(state, got[r - 1][pl.ds(0, n), :]), 0.0)
        state += jnp.where(group >= r, rows8(got[r - 1][pl.ds(rows - 16, 16), :]), 0.0)
    first = jnp.where(position == 0, row(init_ref, 0), 0.0)
    state = vm(state, prefix_ref[...]) + before_ref[...] + first
    out_ref[pl.ds(steps - 1, 1), :] = (vm(state, total_ref[...]) + row(lefts_ref, steps - 1))[:1]
    levels = steps.bit_length() - 1
    starts = [state]
    sizes = [steps >> (level + 1) for level in range(levels)]
    low = sizes[1] + sizes[2]
    for level in reversed(range(levels)):
        at, offset = sum(sizes[:level]), sum(sizes[1:level])
        later = []
        for i, x in enumerate(starts):
            if level == 0:
                mat = table_ref[levels_ref[0, 2 * i]]
            elif level < 3:
                mat = left_ref[offset + i]
            else:
                mat = high_ref[offset + i - low]
            later += [x, vm(x, mat) + row(lefts_ref, at + i)]
        starts = later
    for t in range(1, steps):
        out_ref[pl.ds(t - 1, 1), :] = starts[t][:1]


def shards(count, frames, levels, initial_state, transitions, gain, pixel_mode, pixel_weight):
    n = gain.shape[0]
    kinds = transitions.shape[0]
    pixels, length = frames.shape
    steps = length // count
    position = lax.axis_index("tm").astype(jnp.int32)[None]
    dma = pltpu.SemaphoreType.DMA
    size = 1
    while count % (2 * size) == 0 and 4 * size * size <= count:
        size *= 2
    groups = count // size

    def swaps(x, step, times):
        x = x if isinstance(x, list) else [x] * (times - 1)
        return [
            lax.ppermute(a, "tm", [(j, j ^ (r * step)) for j in range(count)]) for a, r in zip(x, range(1, times))
        ]

    one_map = shape((n, 2 * n), BF16)
    table_shape = shape((kinds, n, 2 * n), BF16)
    cuts = 4
    turn = pixels % 128 == 0 and length % (128 * cuts) == 0
    small = [levels[None], initial_state[None], gain]
    if turn:
        small += [pixel_mode.reshape(count, pixels), pixel_weight.reshape(count, pixels)]
    given = [hbm(a) for a in [transitions] + small + [frames] * turn]
    outs = [table_shape] + [shape(a.shape, a.dtype) for a in small]
    buffers = [pltpu.VMEM(transitions.shape, F32)]
    if turn:
        outs += [shape((groups, steps, pixels), BF16)] * size
        buffers += [pltpu.VMEM(frames.shape, BF16), pltpu.VMEM((length, pixels), BF16)]
    table, levels, initial_state, gain, *rest = call(
        functools.partial(front_kernel, cuts, len(small), size), "front", 5,
        out_shape=outs,
        in_specs=[SMEM] + [HBM] * len(given),
        out_specs=[VMEM] * len(outs),
        scratch_shapes=buffers + [dma((cuts + 4 + len(small),))],
    )(position, *given)
    base = steps // 4
    low = (base + base // 2, n, 2 * n)
    high = shape((base // 2 - 1, n, 2 * n), BF16)
    low_left, low_right, mark = call(
        functools.partial(low_tree_kernel, steps), "low_tree", 8,
        out_shape=[pltpu.HBM(low, BF16)] * 2 + [shape((8, n), F32)],
        in_specs=[SMEM, VMEM],
        out_specs=[HBM, HBM, VMEM],
        scratch_shapes=[pltpu.VMEM(low, BF16)] * 2 + [dma((4,))],
    )(levels, table)

    if turn:
        mode, weight, slab, *slabs = rest
        first, *parts = call(
            functools.partial(project_kernel, size), "project", 4,
            out_shape=[shape((steps, n), F32)] * groups,
            in_specs=[SMEM] + [VMEM] * (3 + size),
            out_specs=[VMEM] * groups,
            scratch_shapes=[pltpu.VMEM((groups, steps, n), F32), pltpu.VMEM((count, pixels), F32)],
        )(position, mark, mode, weight, slab, *swaps(slabs, 1, size))
        far = swaps(parts, size, groups)
        first, parts = far[0], [first] + far[::-1]
    else:
        x = lax.all_to_all(frames, "tm", split_axis=1, concat_axis=0, tiled=True)
        channels = jnp.arange(n, dtype=jnp.int32)
        projector = jnp.where(pixel_mode[None, :] == channels[:, None], pixel_weight[None, :], jnp.zeros((), BF16))
        parts = [lax.dot_general(x, projector, (((0,), (1,)), ((), ())), preferred_element_type=F32)]
        first = mark

    high_left, high_right, total = call(
        functools.partial(high_tree_kernel, base), "high_tree", 5,
        out_shape=[high, high, one_map],
        in_specs=[VMEM, HBM, HBM],
        out_specs=[VMEM] * 3,
        scratch_shapes=[pltpu.VMEM((base, n, 2 * n), BF16)] * 2 + [dma((2,))],
    )(first, hbm(low_left), hbm(low_right))
    block = shape((n + 16, 2 * n), BF16)
    lefts, own = call(
        local_kernel, "local_states", 8,
        out_shape=[shape((steps, n), F32), block],
        in_specs=[SMEM, SMEM] + [VMEM] * 5 + [HBM] + [VMEM] * len(parts),
        out_specs=[VMEM] * 2,
        scratch_shapes=[pltpu.VMEM((steps, n), F32), pltpu.VMEM(low, BF16), dma((2,))],
    )(position, levels, gain, initial_state, total, table, high_right, hbm(low_right), *parts)
    prefix, before, mine, carried = call(
        functools.partial(group_kernel, size), "group_maps", 2,
        out_shape=[one_map, shape((8, n), F32), block, shape((16, 2 * n), BF16)],
        in_specs=[SMEM] + [VMEM] * size,
        out_specs=[VMEM] * 4,
        scratch_shapes=[pltpu.VMEM((size, n + 16, 2 * n), BF16)],
    )(position, own, *swaps(own, 1, size))
    got = [
        lax.ppermute(mine if r < groups - 1 else carried, "tm", [(j, (j + r * size) % count) for j in range(count)])
        for r in range(1, groups)
    ]

    return call(
        functools.partial(final_kernel, size), "estimates", 6,
        out_shape=shape((steps, n), F32),
        in_specs=[SMEM, SMEM] + [VMEM] * (8 + len(got)),
        out_specs=VMEM,
    )(position, levels, initial_state, prefix, before, total, lefts, low_left, high_left, table, *got)


def solution(mesh):
    in_specs = (P("tm", "parts"), P(("parts", "tm")), P("parts"), P(), P(), P(), P())
    out_specs = P(("parts", "tm"), None)
    return jax.shard_map(
        functools.partial(shards, mesh.shape["tm"]),
        mesh=mesh,
        in_specs=in_specs,
        out_specs=out_specs,
        check_vma=False,
    )
```

```python
import functools

import jax
import jax.numpy as jnp
from jax import lax
from jax.experimental import pallas as pl
from jax.experimental.pallas import tpu as pltpu
from jax.sharding import PartitionSpec as P

F32 = jnp.float32
BF16 = jnp.bfloat16
MIB = 1 << 20
NT = (((1,), (1,)), ((), ()))
VMEM = pl.BlockSpec(memory_space=pltpu.VMEM)
SMEM = pl.BlockSpec(memory_space=pltpu.SMEM)
HBM = pl.BlockSpec(memory_space=pltpu.HBM)
shape = jax.ShapeDtypeStruct


def hbm(x):
    return pltpu.with_memory_space_constraint(x, pltpu.HBM)


def call(kernel, name, mib, flops=1, **kw):
    return pl.pallas_call(
        kernel,
        name=name,
        compiler_params=pltpu.CompilerParams(vmem_limit_bytes=mib * MIB),
        cost_estimate=pl.CostEstimate(flops=flops, bytes_accessed=1, transcendentals=0),
        **kw,
    )


def pair(x):
    high = x.astype(BF16)
    mid = (x - high.astype(F32)).astype(BF16)
    return jnp.concatenate([high, mid], axis=1)


def mm(left, right):
    n = right.shape[0]
    out = jnp.dot(left, jnp.concatenate([right, right], axis=0), preferred_element_type=F32)
    return out[:, :n] + out[:, n:]


def vm(vec, mat):
    high = vec.astype(BF16).astype(F32)
    rows = jnp.concatenate([high, vec - high], axis=0).astype(BF16)
    out = jnp.dot(rows, mat, preferred_element_type=F32)
    n = vec.shape[1]
    out = out[:, :n] + out[:, n:]
    return out[:8] + out[8:]


def row(ref, t):
    return jnp.broadcast_to(ref[pl.ds(t, 1), :], (8, ref.shape[1]))


def front_kernel(cuts, extra, size, pos_ref, trans_ref, *refs):
    given, refs = refs[:extra], refs[extra:]
    turn = len(refs) > extra + 3
    if turn:
        frames_ref, table_ref, *moved = refs[: 2 + extra]
        slabs = refs[2 + extra : 2 + extra + size]
        trans, frames, turned, sems = refs[2 + extra + size :]
        width = frames.shape[1] // cuts
        parts = [pl.ds(k * width, width) for k in range(cuts)]
        ins = [
            pltpu.make_async_copy(frames_ref.at[:, part], frames.at[:, part], sems.at[k])
            for k, part in enumerate(parts)
        ]
        for copy in ins:
            copy.start()
    else:
        table_ref, *moved, trans, sems = refs
    kinds = trans.shape[0]
    few = kinds // 4
    maps = [
        pltpu.make_async_copy(trans_ref.at[pl.ds(k * few, few)], trans.at[pl.ds(k * few, few)], sems.at[cuts + k])
        for k in range(4)
    ]
    moves = [pltpu.make_async_copy(a, b, sems.at[cuts + 4 + k]) for k, (a, b) in enumerate(zip(given, moved))]
    for copy in maps + moves:
        copy.start()
    if turn:
        for k in range(cuts):
            ins[k].wait()
            turned[parts[k], :] = frames[:, parts[k]].T
        member = pos_ref[0] % size
        groups, steps, _ = slabs[0].shape
        for r in range(size):
            for g in range(groups):
                start = pl.multiple_of((g * size + (member ^ r)) * steps, steps)
                slabs[r][g] = turned[pl.ds(start, steps), :]
    for k in range(4):
        maps[k].wait()
        for q in range(k * few, (k + 1) * few):
            table_ref[q] = pair(trans[q].T)
    for copy in moves:
        copy.wait()


def project_kernel(size, pos_ref, total_ref, mode_ref, weight_ref, *refs):
    slabs, (same_ref, *outs), (sums, weights) = refs[:size], refs[size:-2], refs[-2:]
    same_ref[...] = total_ref[...]
    weights[...] = weight_ref[...].astype(F32)
    groups, steps, width = slabs[0].shape
    n = sums.shape[2]
    position = pos_ref[0]
    channel = lax.broadcasted_iota(jnp.int32, (n, width), 0)
    total = jnp.zeros((groups * steps, n), F32)
    for r in range(size):
        here = pl.ds(position ^ r, 1)
        weight = jnp.broadcast_to(weights[here, :], (n, width))
        projector = jnp.where(mode_ref[here, :] == channel, weight, 0.0).astype(BF16)
        total += lax.dot_general(slabs[r][...].reshape(groups * steps, width), projector, NT, preferred_element_type=F32)
    sums[...] = total.reshape(groups, steps, n)
    for r in range(groups):
        outs[r][...] = sums[(position // size) ^ r]


def tree_kernel(steps, levels_ref, table_ref, left_hbm, right_hbm, total_ref, left_ref, right_ref, sems):
    base = steps // 4

    def first(t):
        return mm(table_ref[levels_ref[0, t]], table_ref[levels_ref[0, t + 1]])

    def node(k):
        return mm(left_ref[k], right_ref[k])

    def first_pairs(ks):
        made = [(first(4 * k), first(4 * k + 2)) for k in ks]
        for k, (a, b) in zip(ks, made):
            left_ref[k] = pair(a)
            right_ref[k] = pair(b)

    def later_pairs(ks):
        made = [(node(2 * (k - base)), node(2 * (k - base) + 1)) for k in ks]
        for k, (a, b) in zip(ks, made):
            left_ref[k] = pair(a)
            right_ref[k] = pair(b)

    def run(fn, start, count):
        if count <= 4:
            fn(list(range(start, start + count)))
            return

        def body(i, c):
            fn([start + 4 * i + k for k in range(4)])
            return c

        lax.fori_loop(0, count // 4, body, 0)

    copies = []

    def store(start, count):
        for ref, hbm in ((right_ref, right_hbm), (left_ref, left_hbm)):
            part = pl.ds(start, count)
            copies.append(pltpu.make_async_copy(ref.at[part], hbm.at[part], sems.at[len(copies)]))
            copies[-1].start()

    run(first_pairs, 0, base)
    store(0, base)
    run(later_pairs, base, base // 2)
    store(base, base // 2)
    count, start = base // 4, base + base // 2
    while count >= 1:
        run(later_pairs, start, count)
        start += count
        count //= 2
    store(base + base // 2, base // 2 - 1)
    total_ref[...] = pair(node(start - 1))
    for copy in copies:
        copy.wait()


def local_kernel(pos_ref, levels_ref, gain_ref, init_ref, total_ref, table_ref, right_hbm, *refs):
    parts, (lefts_ref, shift_ref, drive_ref, right_ref, sems) = refs[:-5], refs[-5:]
    steps, n = drive_ref.shape
    base = steps // 4
    copies = [
        pltpu.make_async_copy(right_hbm.at[pl.ds(0, base)], right_ref.at[pl.ds(0, base)], sems.at[0]),
        pltpu.make_async_copy(right_hbm.at[pl.ds(base, base - 1)], right_ref.at[pl.ds(base, base - 1)], sems.at[1]),
    ]
    for copy in copies:
        copy.start()
    measured = parts[0][...]
    for part in parts[1:]:
        measured += part[...]
    drive_ref[...] = lax.dot_general(measured.astype(BF16), gain_ref[...], NT, preferred_element_type=F32)

    states = [row(drive_ref, t) for t in range(steps)]
    at, offset = 0, 0
    for level in range(steps.bit_length() - 1):
        if level in (1, 2):
            copies[level - 1].wait()
        later = []
        for i in range(len(states) // 2):
            mat = table_ref[levels_ref[0, 2 * i + 1]] if level == 0 else right_ref[offset + i]
            lefts_ref[pl.ds(at + i, 1), :] = states[2 * i][:1]
            later.append(vm(states[2 * i], mat) + states[2 * i + 1])
        at += len(later)
        if level > 0:
            offset += len(later)
        states = later
    lefts_ref[pl.ds(at, 1), :] = states[0][:1]
    first = jnp.where(pos_ref[0] == 0, row(init_ref, 0), 0.0)
    shift_ref[...] = states[0] + vm(first, total_ref[...])


def map_kernel(size, pos_ref, *refs):
    blocks = refs[:size]
    all_ref, prefix_ref, whole_ref = refs[size:]
    n = whole_ref.shape[0]
    member = pos_ref[0] % size
    for r in range(size):
        all_ref[member ^ r] = blocks[r][...]
    rows, cols = (lax.broadcasted_iota(jnp.int32, (n, n), d) for d in (0, 1))
    prefix = pair((rows == cols).astype(F32))
    run = all_ref[0]
    for q in range(1, size):
        prefix = jnp.where(member == q, run, prefix)
        run = pair(mm(run, all_ref[q]))
    prefix_ref[...] = prefix
    whole_ref[...] = run


def shift_kernel(size, pos_ref, all_ref, near_ref, *refs):
    shifts = refs[:size]
    before_ref, whole_ref, far_ref, held_ref = refs[size:]
    member = pos_ref[0] % size
    for r in range(size):
        held_ref[member ^ r] = shifts[r][...]
    run, before = held_ref[0], jnp.zeros(before_ref.shape, F32)
    for q in range(1, size):
        before = jnp.where(member == q, run, before)
        run = vm(run, all_ref[q]) + held_ref[q]
    before_ref[...] = before
    whole_ref[...] = run
    far_ref[...] = jnp.where((pos_ref[0] // size) % 2 == 0, vm(run, near_ref[...]), run)


def four_groups(group, near_ref, shift_ref, *far):
    state = jnp.where(group >= 2, far[0][...] + far[1][...], 0.0)
    return jnp.where(group % 2 == 1, vm(state, near_ref[...]) + shift_ref[...], state)


def any_groups(group, *got):
    many = (len(got) + 1) // 2
    state = jnp.zeros(got[0].shape, F32)
    for r in range(many, 0, -1):
        if r < many:
            state = jnp.where(group > r, vm(state, got[many + r - 1][...]), 0.0)
        state += jnp.where(group >= r, got[r - 1][...], 0.0)
    return state


def final_kernel(size, gather, pos_ref, levels_ref, init_ref, prefix_ref, before_ref, total_ref, lefts_ref, left_ref, table_ref, *refs):
    got, out_ref = refs[:-1], refs[-1]
    steps, n = lefts_ref.shape
    position = pos_ref[0]
    state = gather(position // size, *got)
    first = jnp.where(position == 0, row(init_ref, 0), 0.0)
    state = vm(state, prefix_ref[...]) + before_ref[...] + first
    out_ref[pl.ds(steps - 1, 1), :] = (vm(state, total_ref[...]) + row(lefts_ref, steps - 1))[:1]
    levels = steps.bit_length() - 1
    starts = [state]
    sizes = [steps >> (level + 1) for level in range(levels)]
    for level in reversed(range(levels)):
        at, offset = sum(sizes[:level]), sum(sizes[1:level])
        later = []
        for i, x in enumerate(starts):
            mat = table_ref[levels_ref[0, 2 * i]] if level == 0 else left_ref[offset + i]
            later += [x, vm(x, mat) + row(lefts_ref, at + i)]
        starts = later
    for t in range(1, steps):
        out_ref[pl.ds(t - 1, 1), :] = starts[t][:1]


def shards(count, frames, levels, initial_state, transitions, gain, pixel_mode, pixel_weight):
    n = gain.shape[0]
    kinds = transitions.shape[0]
    pixels, length = frames.shape
    steps = length // count
    position = lax.axis_index("tm").astype(jnp.int32)[None]
    dma = pltpu.SemaphoreType.DMA
    size = 1
    while count % (2 * size) == 0 and 4 * size * size <= count:
        size *= 2
    groups = count // size

    def swaps(x, step, times):
        x = x if isinstance(x, list) else [x] * (times - 1)
        return [
            lax.ppermute(a, "tm", [(j, j ^ (r * step)) for j in range(count)]) for a, r in zip(x, range(1, times))
        ]

    one_map = shape((n, 2 * n), BF16)
    table_shape = shape((kinds, n, 2 * n), BF16)
    cuts = 4
    turn = pixels % 128 == 0 and length % (128 * cuts) == 0
    small = [levels[None], initial_state[None], gain]
    if turn:
        small += [pixel_mode.reshape(count, pixels), pixel_weight.reshape(count, pixels)]
    given = [hbm(a) for a in [transitions] + small + [frames] * turn]
    outs = [table_shape] + [shape(a.shape, a.dtype) for a in small]
    buffers = [pltpu.VMEM(transitions.shape, F32)]
    if turn:
        outs += [shape((groups, steps, pixels), BF16)] * size
        buffers += [pltpu.VMEM(frames.shape, BF16), pltpu.VMEM((length, pixels), BF16)]
    table, levels, initial_state, gain, *rest = call(
        functools.partial(front_kernel, cuts, len(small), size), "front", 5,
        out_shape=outs,
        in_specs=[SMEM] + [HBM] * len(given),
        out_specs=[VMEM] * len(outs),
        scratch_shapes=buffers + [dma((cuts + 4 + len(small),))],
    )(position, *given)
    pairs = steps // 2 - 1
    tree = pltpu.VMEM((pairs, n, 2 * n), BF16)
    maps = pltpu.HBM((pairs, n, 2 * n), BF16)
    left, right, total = call(
        functools.partial(tree_kernel, steps), "tree_of_maps", 8,
        out_shape=[maps, maps, one_map],
        in_specs=[SMEM, VMEM],
        out_specs=[HBM, HBM, VMEM],
        scratch_shapes=[tree, tree, dma((6,))],
    )(levels, table)

    if turn:
        mode, weight, slab, *slabs = rest
        total, first, *parts = call(
            functools.partial(project_kernel, size), "project", 4,
            out_shape=[one_map] + [shape((steps, n), F32)] * groups,
            in_specs=[SMEM] + [VMEM] * (3 + size),
            out_specs=[VMEM] * (1 + groups),
            scratch_shapes=[pltpu.VMEM((groups, steps, n), F32), pltpu.VMEM((count, pixels), F32)],
        )(position, total, mode, weight, slab, *swaps(slabs, 1, size))
        far = swaps(parts, size, groups)
        parts = [first] + far[::-1]
    else:
        x = lax.all_to_all(frames, "tm", split_axis=1, concat_axis=0, tiled=True)
        channels = jnp.arange(n, dtype=jnp.int32)
        projector = jnp.where(pixel_mode[None, :] == channels[:, None], pixel_weight[None, :], jnp.zeros((), BF16))
        parts = [lax.dot_general(x, projector, (((0,), (1,)), ((), ())), preferred_element_type=F32)]
    members = swaps(total, 1, size)
    vector = shape((8, n), F32)
    lefts, shift = call(
        local_kernel, "local_states", 8, 1 << 40,
        out_shape=[shape((steps, n), F32), vector],
        in_specs=[SMEM, SMEM] + [VMEM] * 4 + [HBM] + [VMEM] * len(parts),
        out_specs=[VMEM] * 2,
        scratch_shapes=[pltpu.VMEM((steps, n), F32), tree, dma((2,))],
    )(position, levels, gain, initial_state, total, table, hbm(right), *parts)
    shifts = swaps(shift, 1, size)
    group_maps, prefix, whole = call(
        functools.partial(map_kernel, size), "group_maps", 2,
        out_shape=[shape((size, n, 2 * n), BF16), one_map, one_map],
        in_specs=[SMEM] + [VMEM] * size,
        out_specs=[VMEM] * 3,
    )(position, total, *members)
    near = swaps(whole, size, 2)[0]
    before, carried, sent = call(
        functools.partial(shift_kernel, size), "group_shifts", 2,
        out_shape=[vector] * 3,
        in_specs=[SMEM] + [VMEM] * (2 + size),
        out_specs=[VMEM] * 3,
        scratch_shapes=[pltpu.VMEM((size, 8, n), F32)],
    )(position, group_maps, near, shift, *shifts)

    def back(x, r):
        return lax.ppermute(x, "tm", [(j, (j + r * size) % count) for j in range(count)])

    if groups == 4:
        gather = four_groups
        got = [near] + swaps([carried, sent, sent], size, groups)
    else:
        gather = any_groups
        got = [back(carried, r) for r in range(1, groups)] + [back(whole, r) for r in range(1, groups - 1)]

    return call(
        functools.partial(final_kernel, size, gather), "estimates", 6,
        out_shape=shape((steps, n), F32),
        in_specs=[SMEM, SMEM] + [VMEM] * (7 + len(got)),
        out_specs=VMEM,
    )(position, levels, initial_state, prefix, before, total, lefts, left, table, *got)


def solution(mesh):
    in_specs = (P("tm", "parts"), P(("parts", "tm")), P("parts"), P(), P(), P(), P())
    out_specs = P(("parts", "tm"), None)
    return jax.shard_map(
        functools.partial(shards, mesh.shape["tm"]),
        mesh=mesh,
        in_specs=in_specs,
        out_specs=out_specs,
        check_vma=False,
    )
```

```python
import functools

import jax
import jax.numpy as jnp
from jax import lax
from jax.experimental import pallas as pl
from jax.experimental.pallas import tpu as pltpu
from jax.sharding import PartitionSpec as P

F32 = jnp.float32
BF16 = jnp.bfloat16
MIB = 1 << 20
NT = (((1,), (1,)), ((), ()))
VMEM = pl.BlockSpec(memory_space=pltpu.VMEM)
SMEM = pl.BlockSpec(memory_space=pltpu.SMEM)
HBM = pl.BlockSpec(memory_space=pltpu.HBM)
shape = jax.ShapeDtypeStruct


def hbm(x):
    return pltpu.with_memory_space_constraint(x, pltpu.HBM)


def call(kernel, name, mib, flops=1, **kw):
    return pl.pallas_call(
        kernel,
        name=name,
        compiler_params=pltpu.CompilerParams(vmem_limit_bytes=mib * MIB),
        cost_estimate=pl.CostEstimate(flops=flops, bytes_accessed=1, transcendentals=0),
        **kw,
    )


def pair(x):
    high = x.astype(BF16)
    mid = (x - high.astype(F32)).astype(BF16)
    return jnp.concatenate([high, mid], axis=1)


def mm(left, right):
    n = right.shape[0]
    out = jnp.dot(left, jnp.concatenate([right, right], axis=0), preferred_element_type=F32)
    return out[:, :n] + out[:, n:]


def vm(vec, mat):
    high = vec.astype(BF16).astype(F32)
    rows = jnp.concatenate([high, vec - high], axis=0).astype(BF16)
    out = jnp.dot(rows, mat, preferred_element_type=F32)
    n = vec.shape[1]
    out = out[:, :n] + out[:, n:]
    return out[:8] + out[8:]


def row(ref, t):
    return jnp.broadcast_to(ref[pl.ds(t, 1), :], (8, ref.shape[1]))


def front_kernel(cuts, extra, size, pos_ref, trans_ref, *refs):
    given, refs = refs[:extra], refs[extra:]
    turn = len(refs) > extra + 3
    if turn:
        frames_ref, table_ref, *moved = refs[: 2 + extra]
        slabs = refs[2 + extra : 2 + extra + size]
        trans, frames, turned, sems = refs[2 + extra + size :]
        width = frames.shape[1] // cuts
        parts = [pl.ds(k * width, width) for k in range(cuts)]
        ins = [
            pltpu.make_async_copy(frames_ref.at[:, part], frames.at[:, part], sems.at[k])
            for k, part in enumerate(parts)
        ]
        for copy in ins:
            copy.start()
    else:
        table_ref, *moved, trans, sems = refs
    kinds = trans.shape[0]
    few = kinds // 4
    maps = [
        pltpu.make_async_copy(trans_ref.at[pl.ds(k * few, few)], trans.at[pl.ds(k * few, few)], sems.at[cuts + k])
        for k in range(4)
    ]
    moves = [pltpu.make_async_copy(a, b, sems.at[cuts + 4 + k]) for k, (a, b) in enumerate(zip(given, moved))]
    for copy in maps + moves:
        copy.start()
    if turn:
        for k in range(cuts):
            ins[k].wait()
            turned[parts[k], :] = frames[:, parts[k]].T
        member = pos_ref[0] % size
        groups, steps, _ = slabs[0].shape
        for r in range(size):
            for g in range(groups):
                start = pl.multiple_of((g * size + (member ^ r)) * steps, steps)
                slabs[r][g] = turned[pl.ds(start, steps), :]
    for k in range(4):
        maps[k].wait()
        for q in range(k * few, (k + 1) * few):
            table_ref[q] = pair(trans[q].T)
    for copy in moves:
        copy.wait()


def project_kernel(size, pos_ref, total_ref, mode_ref, weight_ref, *refs):
    slabs, (same_ref, *outs), (sums, weights) = refs[:size], refs[size:-2], refs[-2:]
    same_ref[...] = total_ref[...]
    weights[...] = weight_ref[...].astype(F32)
    groups, steps, width = slabs[0].shape
    n = sums.shape[2]
    position = pos_ref[0]
    channel = lax.broadcasted_iota(jnp.int32, (n, width), 0)
    total = jnp.zeros((groups * steps, n), F32)
    for r in range(size):
        here = pl.ds(position ^ r, 1)
        weight = jnp.broadcast_to(weights[here, :], (n, width))
        projector = jnp.where(mode_ref[here, :] == channel, weight, 0.0).astype(BF16)
        total += lax.dot_general(slabs[r][...].reshape(groups * steps, width), projector, NT, preferred_element_type=F32)
    sums[...] = total.reshape(groups, steps, n)
    for r in range(groups):
        outs[r][...] = sums[(position // size) ^ r]


def tree_kernel(steps, levels_ref, table_ref, left_hbm, right_hbm, table_hbm, total_ref, left_ref, right_ref, sems):
    base = steps // 4

    def first(t):
        return mm(table_ref[levels_ref[0, t]], table_ref[levels_ref[0, t + 1]])

    def node(k):
        return mm(left_ref[k], right_ref[k])

    def first_pairs(ks):
        made = [(first(4 * k), first(4 * k + 2)) for k in ks]
        for k, (a, b) in zip(ks, made):
            left_ref[k] = pair(a)
            right_ref[k] = pair(b)

    def later_pairs(ks):
        made = [(node(2 * (k - base)), node(2 * (k - base) + 1)) for k in ks]
        for k, (a, b) in zip(ks, made):
            left_ref[k] = pair(a)
            right_ref[k] = pair(b)

    def run(fn, start, count):
        if count <= 4:
            fn(list(range(start, start + count)))
            return

        def body(i, c):
            fn([start + 4 * i + k for k in range(4)])
            return c

        lax.fori_loop(0, count // 4, body, 0)

    copies = [pltpu.make_async_copy(table_ref, table_hbm, sems.at[0])]
    copies[0].start()

    def store(start, count):
        for ref, hbm in ((right_ref, right_hbm), (left_ref, left_hbm)):
            part = pl.ds(start, count)
            copies.append(pltpu.make_async_copy(ref.at[part], hbm.at[part], sems.at[len(copies)]))
            copies[-1].start()

    run(first_pairs, 0, base)
    store(0, base)
    run(later_pairs, base, base // 2)
    store(base, base // 2)
    count, start = base // 4, base + base // 2
    while count >= 1:
        run(later_pairs, start, count)
        start += count
        count //= 2
    store(base + base // 2, base // 2 - 1)
    total_ref[...] = pair(node(start - 1))
    for copy in copies:
        copy.wait()


def local_kernel(pos_ref, levels_ref, gain_ref, init_ref, total_ref, table_hbm, right_hbm, *refs):
    parts, (lefts_ref, shift_ref, drive_ref, table_ref, right_ref, sems) = refs[:-6], refs[-6:]
    steps, n = drive_ref.shape
    base = steps // 4
    copies = [
        pltpu.make_async_copy(table_hbm, table_ref, sems.at[0]),
        pltpu.make_async_copy(right_hbm.at[pl.ds(0, base)], right_ref.at[pl.ds(0, base)], sems.at[1]),
        pltpu.make_async_copy(right_hbm.at[pl.ds(base, base - 1)], right_ref.at[pl.ds(base, base - 1)], sems.at[2]),
    ]
    for copy in copies:
        copy.start()
    measured = parts[0][...]
    for part in parts[1:]:
        measured += part[...]
    drive_ref[...] = lax.dot_general(measured.astype(BF16), gain_ref[...], NT, preferred_element_type=F32)

    states = [row(drive_ref, t) for t in range(steps)]
    at, offset = 0, 0
    for level in range(steps.bit_length() - 1):
        if level < 3:
            copies[level].wait()
        later = []
        for i in range(len(states) // 2):
            mat = table_ref[levels_ref[0, 2 * i + 1]] if level == 0 else right_ref[offset + i]
            lefts_ref[pl.ds(at + i, 1), :] = states[2 * i][:1]
            later.append(vm(states[2 * i], mat) + states[2 * i + 1])
        at += len(later)
        if level > 0:
            offset += len(later)
        states = later
    lefts_ref[pl.ds(at, 1), :] = states[0][:1]
    first = jnp.where(pos_ref[0] == 0, row(init_ref, 0), 0.0)
    shift_ref[...] = states[0] + vm(first, total_ref[...])


def map_kernel(size, pos_ref, *refs):
    blocks = refs[:size]
    all_ref, prefix_ref, whole_ref = refs[size:]
    n = whole_ref.shape[0]
    member = pos_ref[0] % size
    for r in range(size):
        all_ref[member ^ r] = blocks[r][...]
    rows, cols = (lax.broadcasted_iota(jnp.int32, (n, n), d) for d in (0, 1))
    prefix = pair((rows == cols).astype(F32))
    run = all_ref[0]
    for q in range(1, size):
        prefix = jnp.where(member == q, run, prefix)
        run = pair(mm(run, all_ref[q]))
    prefix_ref[...] = prefix
    whole_ref[...] = run


def shift_kernel(size, pos_ref, all_ref, near_ref, *refs):
    shifts = refs[:size]
    before_ref, whole_ref, far_ref, held_ref = refs[size:]
    member = pos_ref[0] % size
    for r in range(size):
        held_ref[member ^ r] = shifts[r][...]
    run, before = held_ref[0], jnp.zeros(before_ref.shape, F32)
    for q in range(1, size):
        before = jnp.where(member == q, run, before)
        run = vm(run, all_ref[q]) + held_ref[q]
    before_ref[...] = before
    whole_ref[...] = run
    far_ref[...] = jnp.where((pos_ref[0] // size) % 2 == 0, vm(run, near_ref[...]), run)


def four_groups(group, near_ref, shift_ref, *far):
    state = jnp.where(group >= 2, far[0][...] + far[1][...], 0.0)
    return jnp.where(group % 2 == 1, vm(state, near_ref[...]) + shift_ref[...], state)


def any_groups(group, *got):
    many = (len(got) + 1) // 2
    state = jnp.zeros(got[0].shape, F32)
    for r in range(many, 0, -1):
        if r < many:
            state = jnp.where(group > r, vm(state, got[many + r - 1][...]), 0.0)
        state += jnp.where(group >= r, got[r - 1][...], 0.0)
    return state


def final_kernel(size, gather, pos_ref, levels_ref, init_ref, prefix_ref, before_ref, total_ref, lefts_ref, left_ref, table_ref, *refs):
    got, out_ref = refs[:-1], refs[-1]
    steps, n = lefts_ref.shape
    position = pos_ref[0]
    state = gather(position // size, *got)
    first = jnp.where(position == 0, row(init_ref, 0), 0.0)
    state = vm(state, prefix_ref[...]) + before_ref[...] + first
    out_ref[pl.ds(steps - 1, 1), :] = (vm(state, total_ref[...]) + row(lefts_ref, steps - 1))[:1]
    levels = steps.bit_length() - 1
    starts = [state]
    sizes = [steps >> (level + 1) for level in range(levels)]
    for level in reversed(range(levels)):
        at, offset = sum(sizes[:level]), sum(sizes[1:level])
        later = []
        for i, x in enumerate(starts):
            mat = table_ref[levels_ref[0, 2 * i]] if level == 0 else left_ref[offset + i]
            later += [x, vm(x, mat) + row(lefts_ref, at + i)]
        starts = later
    for t in range(1, steps):
        out_ref[pl.ds(t - 1, 1), :] = starts[t][:1]


def shards(count, frames, levels, initial_state, transitions, gain, pixel_mode, pixel_weight):
    n = gain.shape[0]
    kinds = transitions.shape[0]
    pixels, length = frames.shape
    steps = length // count
    position = lax.axis_index("tm").astype(jnp.int32)[None]
    dma = pltpu.SemaphoreType.DMA
    size = 1
    while count % (2 * size) == 0 and 4 * size * size <= count:
        size *= 2
    groups = count // size

    def swaps(x, step, times):
        x = x if isinstance(x, list) else [x] * (times - 1)
        return [
            lax.ppermute(a, "tm", [(j, j ^ (r * step)) for j in range(count)]) for a, r in zip(x, range(1, times))
        ]

    one_map = shape((n, 2 * n), BF16)
    table_shape = shape((kinds, n, 2 * n), BF16)
    cuts = 4
    turn = pixels % 128 == 0 and length % (128 * cuts) == 0
    small = [levels[None], initial_state[None], gain]
    if turn:
        small += [pixel_mode.reshape(count, pixels), pixel_weight.reshape(count, pixels)]
    given = [hbm(a) for a in [transitions] + small + [frames] * turn]
    outs = [table_shape] + [shape(a.shape, a.dtype) for a in small]
    buffers = [pltpu.VMEM(transitions.shape, F32)]
    if turn:
        outs += [shape((groups, steps, pixels), BF16)] * size
        buffers += [pltpu.VMEM(frames.shape, BF16), pltpu.VMEM((length, pixels), BF16)]
    table, levels, initial_state, gain, *rest = call(
        functools.partial(front_kernel, cuts, len(small), size), "front", 5,
        out_shape=outs,
        in_specs=[SMEM] + [HBM] * len(given),
        out_specs=[VMEM] * len(outs),
        scratch_shapes=buffers + [dma((cuts + 4 + len(small),))],
    )(position, *given)
    pairs = steps // 2 - 1
    tree = pltpu.VMEM((pairs, n, 2 * n), BF16)
    maps = pltpu.HBM((pairs, n, 2 * n), BF16)
    left, right, table, total = call(
        functools.partial(tree_kernel, steps), "tree_of_maps", 8,
        out_shape=[maps, maps, pltpu.HBM(table_shape.shape, BF16), one_map],
        in_specs=[SMEM, VMEM],
        out_specs=[HBM, HBM, HBM, VMEM],
        scratch_shapes=[tree, tree, dma((7,))],
    )(levels, table)

    if turn:
        mode, weight, slab, *slabs = rest
        total, first, *parts = call(
            functools.partial(project_kernel, size), "project", 4,
            out_shape=[one_map] + [shape((steps, n), F32)] * groups,
            in_specs=[SMEM] + [VMEM] * (3 + size),
            out_specs=[VMEM] * (1 + groups),
            scratch_shapes=[pltpu.VMEM((groups, steps, n), F32), pltpu.VMEM((count, pixels), F32)],
        )(position, total, mode, weight, slab, *swaps(slabs, 1, size))
        far = swaps(parts, size, groups)
        parts = [first] + far[::-1]
    else:
        x = lax.all_to_all(frames, "tm", split_axis=1, concat_axis=0, tiled=True)
        channels = jnp.arange(n, dtype=jnp.int32)
        projector = jnp.where(pixel_mode[None, :] == channels[:, None], pixel_weight[None, :], jnp.zeros((), BF16))
        parts = [lax.dot_general(x, projector, (((0,), (1,)), ((), ())), preferred_element_type=F32)]
    members = swaps(total, 1, size)
    vector = shape((8, n), F32)
    lefts, shift = call(
        local_kernel, "local_states", 8, 1 << 40,
        out_shape=[shape((steps, n), F32), vector],
        in_specs=[SMEM, SMEM] + [VMEM] * 3 + [HBM] * 2 + [VMEM] * len(parts),
        out_specs=[VMEM] * 2,
        scratch_shapes=[pltpu.VMEM((steps, n), F32), pltpu.VMEM(table.shape, BF16), tree, dma((3,))],
    )(position, levels, gain, initial_state, total, hbm(table), hbm(right), *parts)
    shifts = swaps(shift, 1, size)
    group_maps, prefix, whole = call(
        functools.partial(map_kernel, size), "group_maps", 2,
        out_shape=[shape((size, n, 2 * n), BF16), one_map, one_map],
        in_specs=[SMEM] + [VMEM] * size,
        out_specs=[VMEM] * 3,
    )(position, total, *members)
    near = swaps(whole, size, 2)[0]
    before, carried, sent = call(
        functools.partial(shift_kernel, size), "group_shifts", 2,
        out_shape=[vector] * 3,
        in_specs=[SMEM] + [VMEM] * (2 + size),
        out_specs=[VMEM] * 3,
        scratch_shapes=[pltpu.VMEM((size, 8, n), F32)],
    )(position, group_maps, near, shift, *shifts)

    def back(x, r):
        return lax.ppermute(x, "tm", [(j, (j + r * size) % count) for j in range(count)])

    if groups == 4:
        gather = four_groups
        got = [near] + swaps([carried, sent, sent], size, groups)
    else:
        gather = any_groups
        got = [back(carried, r) for r in range(1, groups)] + [back(whole, r) for r in range(1, groups - 1)]

    return call(
        functools.partial(final_kernel, size, gather), "estimates", 6,
        out_shape=shape((steps, n), F32),
        in_specs=[SMEM, SMEM] + [VMEM] * (7 + len(got)),
        out_specs=VMEM,
    )(position, levels, initial_state, prefix, before, total, lefts, left, table, *got)


def solution(mesh):
    in_specs = (P("tm", "parts"), P(("parts", "tm")), P("parts"), P(), P(), P(), P())
    out_specs = P(("parts", "tm"), None)
    return jax.shard_map(
        functools.partial(shards, mesh.shape["tm"]),
        mesh=mesh,
        in_specs=in_specs,
        out_specs=out_specs,
        check_vma=False,
    )
```

```python
import functools

import jax
import jax.numpy as jnp
from jax import lax
from jax.experimental import pallas as pl
from jax.experimental.pallas import tpu as pltpu
from jax.sharding import PartitionSpec as P

F32 = jnp.float32
BF16 = jnp.bfloat16
MIB = 1 << 20
NT = (((1,), (1,)), ((), ()))
VMEM = pl.BlockSpec(memory_space=pltpu.VMEM)
SMEM = pl.BlockSpec(memory_space=pltpu.SMEM)
HBM = pl.BlockSpec(memory_space=pltpu.HBM)
ANY = pl.BlockSpec(memory_space=pl.ANY)
shape = jax.ShapeDtypeStruct


def hbm(x):
    return pltpu.with_memory_space_constraint(x, pltpu.HBM)


def call(kernel, name, mib, flops=1, **kw):
    return pl.pallas_call(
        kernel,
        name=name,
        compiler_params=pltpu.CompilerParams(vmem_limit_bytes=mib * MIB),
        cost_estimate=pl.CostEstimate(flops=flops, bytes_accessed=1, transcendentals=0),
        **kw,
    )


def pair(x):
    high = x.astype(BF16)
    mid = (x - high.astype(F32)).astype(BF16)
    return jnp.concatenate([high, mid], axis=1)


def mm(left, right):
    n = right.shape[0]
    out = jnp.dot(left, jnp.concatenate([right, right], axis=0), preferred_element_type=F32)
    return out[:, :n] + out[:, n:]


def vm(vec, mat):
    high = vec.astype(BF16).astype(F32)
    rows = jnp.concatenate([high, vec - high], axis=0).astype(BF16)
    out = jnp.dot(rows, mat, preferred_element_type=F32)
    n = vec.shape[1]
    out = out[:, :n] + out[:, n:]
    return out[:8] + out[8:]


def row(ref, t):
    return jnp.broadcast_to(ref[pl.ds(t, 1), :], (8, ref.shape[1]))


def front_kernel(cuts, extra, size, pos_ref, trans_ref, *refs):
    given, refs = refs[:extra], refs[extra:]
    turn = len(refs) > extra + 3
    if turn:
        frames_ref, table_ref, *moved = refs[: 2 + extra]
        slabs = refs[2 + extra : 2 + extra + size]
        trans, frames, turned, sems = refs[2 + extra + size :]
        width = frames.shape[1] // cuts
        parts = [pl.ds(k * width, width) for k in range(cuts)]
        ins = [
            pltpu.make_async_copy(frames_ref.at[:, part], frames.at[:, part], sems.at[k])
            for k, part in enumerate(parts)
        ]
        for copy in ins:
            copy.start()
    else:
        table_ref, *moved, trans, sems = refs
    kinds = trans.shape[0]
    few = kinds // 4
    maps = [
        pltpu.make_async_copy(trans_ref.at[pl.ds(k * few, few)], trans.at[pl.ds(k * few, few)], sems.at[cuts + k])
        for k in range(4)
    ]
    moves = [pltpu.make_async_copy(a, b, sems.at[cuts + 4 + k]) for k, (a, b) in enumerate(zip(given, moved))]
    for copy in maps + moves:
        copy.start()
    if turn:
        for k in range(cuts):
            ins[k].wait()
            turned[parts[k], :] = frames[:, parts[k]].T
        member = pos_ref[0] % size
        groups, steps, _ = slabs[0].shape
        for r in range(size):
            for g in range(groups):
                start = pl.multiple_of((g * size + (member ^ r)) * steps, steps)
                slabs[r][g] = turned[pl.ds(start, steps), :]
    for k in range(4):
        maps[k].wait()
        for q in range(k * few, (k + 1) * few):
            table_ref[q] = pair(trans[q].T)
    for copy in moves:
        copy.wait()


def project_kernel(size, pos_ref, total_ref, mode_ref, weight_ref, *refs):
    slabs, (same_ref, *outs), (sums, weights) = refs[:size], refs[size:-2], refs[-2:]
    same_ref[...] = total_ref[...]
    weights[...] = weight_ref[...].astype(F32)
    groups, steps, width = slabs[0].shape
    n = sums.shape[2]
    position = pos_ref[0]
    channel = lax.broadcasted_iota(jnp.int32, (n, width), 0)
    total = jnp.zeros((groups * steps, n), F32)
    for r in range(size):
        here = pl.ds(position ^ r, 1)
        weight = jnp.broadcast_to(weights[here, :], (n, width))
        projector = jnp.where(mode_ref[here, :] == channel, weight, 0.0).astype(BF16)
        total += lax.dot_general(slabs[r][...].reshape(groups * steps, width), projector, NT, preferred_element_type=F32)
    sums[...] = total.reshape(groups, steps, n)
    for r in range(groups):
        outs[r][...] = sums[(position // size) ^ r]


def tree_kernel(steps, levels_ref, table_ref, left_hbm, right_hbm, total_ref, left_ref, right_ref, sems):
    base = steps // 4

    def first(t):
        return mm(table_ref[levels_ref[0, t]], table_ref[levels_ref[0, t + 1]])

    def node(k):
        return mm(left_ref[k], right_ref[k])

    def first_pairs(ks):
        made = [(first(4 * k), first(4 * k + 2)) for k in ks]
        for k, (a, b) in zip(ks, made):
            left_ref[k] = pair(a)
            right_ref[k] = pair(b)

    def later_pairs(ks):
        made = [(node(2 * (k - base)), node(2 * (k - base) + 1)) for k in ks]
        for k, (a, b) in zip(ks, made):
            left_ref[k] = pair(a)
            right_ref[k] = pair(b)

    def run(fn, start, count):
        if count <= 4:
            fn(list(range(start, start + count)))
            return

        def body(i, c):
            fn([start + 4 * i + k for k in range(4)])
            return c

        lax.fori_loop(0, count // 4, body, 0)

    copies = []

    def store(start, count):
        for ref, hbm in ((right_ref, right_hbm), (left_ref, left_hbm)):
            part = pl.ds(start, count)
            copies.append(pltpu.make_async_copy(ref.at[part], hbm.at[part], sems.at[len(copies)]))
            copies[-1].start()

    run(first_pairs, 0, base)
    store(0, base)
    run(later_pairs, base, base // 2)
    store(base, base // 2)
    count, start = base // 4, base + base // 2
    while count >= 1:
        run(later_pairs, start, count)
        store(start, count)
        start += count
        count //= 2
    total_ref[...] = pair(node(start - 1))
    for copy in copies:
        copy.wait()


def local_kernel(pos_ref, levels_ref, gain_ref, init_ref, total_ref, table_ref, right_hbm, *refs):
    parts, (lefts_ref, shift_ref, drive_ref, right_ref, sems) = refs[:-5], refs[-5:]
    steps, n = drive_ref.shape
    base = steps // 4
    copies = [
        pltpu.make_async_copy(right_hbm.at[pl.ds(0, base)], right_ref.at[pl.ds(0, base)], sems.at[0]),
        pltpu.make_async_copy(right_hbm.at[pl.ds(base, base - 1)], right_ref.at[pl.ds(base, base - 1)], sems.at[1]),
    ]
    for copy in copies:
        copy.start()
    measured = parts[0][...]
    for part in parts[1:]:
        measured += part[...]
    drive_ref[...] = lax.dot_general(measured.astype(BF16), gain_ref[...], NT, preferred_element_type=F32)

    states = [row(drive_ref, t) for t in range(steps)]
    at, offset = 0, 0
    for level in range(steps.bit_length() - 1):
        if level in (1, 2):
            copies[level - 1].wait()
        later = []
        for i in range(len(states) // 2):
            mat = table_ref[levels_ref[0, 2 * i + 1]] if level == 0 else right_ref[offset + i]
            lefts_ref[pl.ds(at + i, 1), :] = states[2 * i][:1]
            later.append(vm(states[2 * i], mat) + states[2 * i + 1])
        at += len(later)
        if level > 0:
            offset += len(later)
        states = later
    lefts_ref[pl.ds(at, 1), :] = states[0][:1]
    first = jnp.where(pos_ref[0] == 0, row(init_ref, 0), 0.0)
    shift_ref[...] = states[0] + vm(first, total_ref[...])


def map_kernel(size, pos_ref, *refs):
    blocks = refs[:size]
    all_ref, prefix_ref, whole_ref = refs[size:]
    n = whole_ref.shape[0]
    member = pos_ref[0] % size
    for r in range(size):
        all_ref[member ^ r] = blocks[r][...]
    rows, cols = (lax.broadcasted_iota(jnp.int32, (n, n), d) for d in (0, 1))
    prefix = pair((rows == cols).astype(F32))
    run = all_ref[0]
    for q in range(1, size):
        prefix = jnp.where(member == q, run, prefix)
        run = pair(mm(run, all_ref[q]))
    prefix_ref[...] = prefix
    whole_ref[...] = run


def shift_kernel(size, pos_ref, all_ref, near_ref, *refs):
    shifts = refs[:size]
    before_ref, whole_ref, far_ref, map_ref, held_ref, sem = refs[size:]
    copy = pltpu.make_async_copy(near_ref, map_ref, sem)
    copy.start()
    member = pos_ref[0] % size
    for r in range(size):
        held_ref[member ^ r] = shifts[r][...]
    run, before = held_ref[0], jnp.zeros(before_ref.shape, F32)
    for q in range(1, size):
        before = jnp.where(member == q, run, before)
        run = vm(run, all_ref[q]) + held_ref[q]
    before_ref[...] = before
    whole_ref[...] = run
    copy.wait()
    far_ref[...] = jnp.where((pos_ref[0] // size) % 2 == 0, vm(run, map_ref[...]), run)


def four_groups(group, near_ref, shift_ref, *far):
    state = jnp.where(group >= 2, far[0][...] + far[1][...], 0.0)
    return jnp.where(group % 2 == 1, vm(state, near_ref[...]) + shift_ref[...], state)


def any_groups(group, *got):
    many = (len(got) + 1) // 2
    state = jnp.zeros(got[0].shape, F32)
    for r in range(many, 0, -1):
        if r < many:
            state = jnp.where(group > r, vm(state, got[many + r - 1][...]), 0.0)
        state += jnp.where(group >= r, got[r - 1][...], 0.0)
    return state


def final_kernel(size, gather, pos_ref, levels_ref, init_ref, prefix_ref, before_ref, total_ref, lefts_ref, left_ref, table_ref, *refs):
    got, out_ref = refs[:-1], refs[-1]
    steps, n = lefts_ref.shape
    position = pos_ref[0]
    state = gather(position // size, *got)
    first = jnp.where(position == 0, row(init_ref, 0), 0.0)
    state = vm(state, prefix_ref[...]) + before_ref[...] + first
    out_ref[pl.ds(steps - 1, 1), :] = (vm(state, total_ref[...]) + row(lefts_ref, steps - 1))[:1]
    levels = steps.bit_length() - 1
    starts = [state]
    sizes = [steps >> (level + 1) for level in range(levels)]
    for level in reversed(range(levels)):
        at, offset = sum(sizes[:level]), sum(sizes[1:level])
        later = []
        for i, x in enumerate(starts):
            mat = table_ref[levels_ref[0, 2 * i]] if level == 0 else left_ref[offset + i]
            later += [x, vm(x, mat) + row(lefts_ref, at + i)]
        starts = later
    for t in range(1, steps):
        out_ref[pl.ds(t - 1, 1), :] = starts[t][:1]


def shards(count, frames, levels, initial_state, transitions, gain, pixel_mode, pixel_weight):
    n = gain.shape[0]
    kinds = transitions.shape[0]
    pixels, length = frames.shape
    steps = length // count
    position = lax.axis_index("tm").astype(jnp.int32)[None]
    dma = pltpu.SemaphoreType.DMA
    size = 1
    while count % (2 * size) == 0 and 4 * size * size <= count:
        size *= 2
    groups = count // size

    def swaps(x, step, times):
        x = x if isinstance(x, list) else [x] * (times - 1)
        return [
            lax.ppermute(a, "tm", [(j, j ^ (r * step)) for j in range(count)]) for a, r in zip(x, range(1, times))
        ]

    one_map = shape((n, 2 * n), BF16)
    table_shape = shape((kinds, n, 2 * n), BF16)
    cuts = 4
    turn = pixels % 128 == 0 and length % (128 * cuts) == 0
    small = [levels[None], initial_state[None], gain]
    if turn:
        small += [pixel_mode.reshape(count, pixels), pixel_weight.reshape(count, pixels)]
    given = [hbm(a) for a in [transitions] + small + [frames] * turn]
    outs = [table_shape] + [shape(a.shape, a.dtype) for a in small]
    buffers = [pltpu.VMEM(transitions.shape, F32)]
    if turn:
        outs += [shape((groups, steps, pixels), BF16)] * size
        buffers += [pltpu.VMEM(frames.shape, BF16), pltpu.VMEM((length, pixels), BF16)]
    table, levels, initial_state, gain, *rest = call(
        functools.partial(front_kernel, cuts, len(small), size), "front", 5,
        out_shape=outs,
        in_specs=[SMEM] + [HBM] * len(given),
        out_specs=[VMEM] * len(outs),
        scratch_shapes=buffers + [dma((cuts + 4 + len(small),))],
    )(position, *given)
    pairs = steps // 2 - 1
    tree = pltpu.VMEM((pairs, n, 2 * n), BF16)
    maps = pltpu.HBM((pairs, n, 2 * n), BF16)
    left, right, total = call(
        functools.partial(tree_kernel, steps), "tree_of_maps", 8,
        out_shape=[maps, maps, one_map],
        in_specs=[SMEM, VMEM],
        out_specs=[HBM, HBM, VMEM],
        scratch_shapes=[tree, tree, dma((2 * steps.bit_length(),))],
    )(levels, table)

    if turn:
        mode, weight, slab, *slabs = rest
        total, first, *parts = call(
            functools.partial(project_kernel, size), "project", 4,
            out_shape=[one_map] + [shape((steps, n), F32)] * groups,
            in_specs=[SMEM] + [VMEM] * (3 + size),
            out_specs=[VMEM] * (1 + groups),
            scratch_shapes=[pltpu.VMEM((groups, steps, n), F32), pltpu.VMEM((count, pixels), F32)],
        )(position, total, mode, weight, slab, *swaps(slabs, 1, size))
        far = swaps(parts, size, groups)
        parts = [first] + far
    else:
        x = lax.all_to_all(frames, "tm", split_axis=1, concat_axis=0, tiled=True)
        channels = jnp.arange(n, dtype=jnp.int32)
        projector = jnp.where(pixel_mode[None, :] == channels[:, None], pixel_weight[None, :], jnp.zeros((), BF16))
        parts = [lax.dot_general(x, projector, (((0,), (1,)), ((), ())), preferred_element_type=F32)]
    members = swaps(total, 1, size)
    vector = shape((8, n), F32)
    lefts, shift = call(
        local_kernel, "local_states", 8, 1 << 40,
        out_shape=[shape((steps, n), F32), vector],
        in_specs=[SMEM, SMEM] + [VMEM] * 4 + [HBM] + [VMEM] * len(parts),
        out_specs=[VMEM] * 2,
        scratch_shapes=[pltpu.VMEM((steps, n), F32), tree, dma((2,))],
    )(position, levels, gain, initial_state, total, table, hbm(right), *parts)
    shifts = swaps(shift, 1, size)
    group_maps, prefix, whole = call(
        functools.partial(map_kernel, size), "group_maps", 2,
        out_shape=[shape((size, n, 2 * n), BF16), one_map, pltpu.VMEM(one_map.shape, BF16)],
        in_specs=[SMEM] + [VMEM] * size,
        out_specs=[VMEM] * 3,
    )(position, total, *members)
    near = swaps(whole, size, 2)[0]
    before, carried, sent, near = call(
        functools.partial(shift_kernel, size), "group_shifts", 2,
        out_shape=[vector] * 3 + [one_map],
        in_specs=[SMEM, VMEM, ANY] + [VMEM] * size,
        out_specs=[VMEM] * 4,
        scratch_shapes=[pltpu.VMEM((size, 8, n), F32), dma(())],
    )(position, group_maps, near, shift, *shifts)

    def back(x, r):
        return lax.ppermute(x, "tm", [(j, (j + r * size) % count) for j in range(count)])

    if groups == 4:
        gather = four_groups
        got = [near] + swaps([carried, sent, sent], size, groups)
    else:
        gather = any_groups
        got = [back(carried, r) for r in range(1, groups)] + [back(whole, r) for r in range(1, groups - 1)]

    return call(
        functools.partial(final_kernel, size, gather), "estimates", 6,
        out_shape=shape((steps, n), F32),
        in_specs=[SMEM, SMEM] + [VMEM] * (7 + len(got)),
        out_specs=VMEM,
    )(position, levels, initial_state, prefix, before, total, lefts, left, table, *got)


def solution(mesh):
    in_specs = (P("tm", "parts"), P(("parts", "tm")), P("parts"), P(), P(), P(), P())
    out_specs = P(("parts", "tm"), None)
    return jax.shard_map(
        functools.partial(shards, mesh.shape["tm"]),
        mesh=mesh,
        in_specs=in_specs,
        out_specs=out_specs,
        check_vma=False,
    )
```

```python
import functools

import jax
import jax.numpy as jnp
from jax import lax
from jax.experimental import pallas as pl
from jax.experimental.pallas import tpu as pltpu
from jax.sharding import PartitionSpec as P

F32 = jnp.float32
BF16 = jnp.bfloat16
MIB = 1 << 20
NT = (((1,), (1,)), ((), ()))
VMEM = pl.BlockSpec(memory_space=pltpu.VMEM)
SMEM = pl.BlockSpec(memory_space=pltpu.SMEM)
HBM = pl.BlockSpec(memory_space=pltpu.HBM)
ANY = pl.BlockSpec(memory_space=pl.ANY)
shape = jax.ShapeDtypeStruct


def hbm(x):
    return pltpu.with_memory_space_constraint(x, pltpu.HBM)


def call(kernel, name, mib, flops=1, **kw):
    return pl.pallas_call(
        kernel,
        name=name,
        compiler_params=pltpu.CompilerParams(vmem_limit_bytes=mib * MIB),
        cost_estimate=pl.CostEstimate(flops=flops, bytes_accessed=1, transcendentals=0),
        **kw,
    )


def pair(x):
    high = x.astype(BF16)
    mid = (x - high.astype(F32)).astype(BF16)
    return jnp.concatenate([high, mid], axis=1)


def mm(left, right):
    n = right.shape[0]
    out = jnp.dot(left, jnp.concatenate([right, right], axis=0), preferred_element_type=F32)
    return out[:, :n] + out[:, n:]


def vm(vec, mat):
    high = vec.astype(BF16).astype(F32)
    rows = jnp.concatenate([high, vec - high], axis=0).astype(BF16)
    out = jnp.dot(rows, mat, preferred_element_type=F32)
    n = vec.shape[1]
    out = out[:, :n] + out[:, n:]
    return out[:8] + out[8:]


def row(ref, t):
    return jnp.broadcast_to(ref[pl.ds(t, 1), :], (8, ref.shape[1]))


def front_kernel(cuts, extra, size, pos_ref, trans_ref, *refs):
    given, refs = refs[:extra], refs[extra:]
    turn = len(refs) > extra + 3
    if turn:
        frames_ref, table_ref, *moved = refs[: 2 + extra]
        slabs = refs[2 + extra : 2 + extra + size]
        trans, frames, turned, sems = refs[2 + extra + size :]
        width = frames.shape[1] // cuts
        parts = [pl.ds(k * width, width) for k in range(cuts)]
        ins = [
            pltpu.make_async_copy(frames_ref.at[:, part], frames.at[:, part], sems.at[k])
            for k, part in enumerate(parts)
        ]
        for copy in ins:
            copy.start()
    else:
        table_ref, *moved, trans, sems = refs
    kinds = trans.shape[0]
    few = kinds // 4
    maps = [
        pltpu.make_async_copy(trans_ref.at[pl.ds(k * few, few)], trans.at[pl.ds(k * few, few)], sems.at[cuts + k])
        for k in range(4)
    ]
    moves = [pltpu.make_async_copy(a, b, sems.at[cuts + 4 + k]) for k, (a, b) in enumerate(zip(given, moved))]
    for copy in maps + moves:
        copy.start()
    if turn:
        for k in range(cuts):
            ins[k].wait()
            turned[parts[k], :] = frames[:, parts[k]].T
        member = pos_ref[0] % size
        groups, steps, _ = slabs[0].shape
        for r in range(size):
            for g in range(groups):
                start = pl.multiple_of((g * size + (member ^ r)) * steps, steps)
                slabs[r][g] = turned[pl.ds(start, steps), :]
    for k in range(4):
        maps[k].wait()
        for q in range(k * few, (k + 1) * few):
            table_ref[q] = pair(trans[q].T)
    for copy in moves:
        copy.wait()


def project_kernel(size, pos_ref, total_ref, mode_ref, weight_ref, *refs):
    slabs, (same_ref, *outs), (sums, weights) = refs[:size], refs[size:-2], refs[-2:]
    same_ref[...] = total_ref[...]
    weights[...] = weight_ref[...].astype(F32)
    groups, steps, width = slabs[0].shape
    n = sums.shape[2]
    position = pos_ref[0]
    channel = lax.broadcasted_iota(jnp.int32, (n, width), 0)
    total = jnp.zeros((groups * steps, n), F32)
    for r in range(size):
        here = pl.ds(position ^ r, 1)
        weight = jnp.broadcast_to(weights[here, :], (n, width))
        projector = jnp.where(mode_ref[here, :] == channel, weight, 0.0).astype(BF16)
        total += lax.dot_general(slabs[r][...].reshape(groups * steps, width), projector, NT, preferred_element_type=F32)
    sums[...] = total.reshape(groups, steps, n)
    for r in range(groups):
        outs[r][...] = sums[(position // size) ^ r]


def tree_kernel(steps, levels_ref, table_ref, left_hbm, right_hbm, total_ref, left_ref, right_ref, sems):
    base = steps // 4

    def first(t):
        return mm(table_ref[levels_ref[0, t]], table_ref[levels_ref[0, t + 1]])

    def node(k):
        return mm(left_ref[k], right_ref[k])

    def first_pairs(ks):
        made = [(first(4 * k), first(4 * k + 2)) for k in ks]
        for k, (a, b) in zip(ks, made):
            left_ref[k] = pair(a)
            right_ref[k] = pair(b)

    def later_pairs(ks):
        made = [(node(2 * (k - base)), node(2 * (k - base) + 1)) for k in ks]
        for k, (a, b) in zip(ks, made):
            left_ref[k] = pair(a)
            right_ref[k] = pair(b)

    def run(fn, start, count):
        if count <= 4:
            fn(list(range(start, start + count)))
            return

        def body(i, c):
            fn([start + 4 * i + k for k in range(4)])
            return c

        lax.fori_loop(0, count // 4, body, 0)

    copies = []

    def store(start, count):
        for ref, hbm in ((right_ref, right_hbm), (left_ref, left_hbm)):
            part = pl.ds(start, count)
            copies.append(pltpu.make_async_copy(ref.at[part], hbm.at[part], sems.at[len(copies)]))
            copies[-1].start()

    run(first_pairs, 0, base)
    store(0, base)
    run(later_pairs, base, base // 2)
    store(base, base // 2)
    count, start = base // 4, base + base // 2
    while count >= 1:
        run(later_pairs, start, count)
        store(start, count)
        start += count
        count //= 2
    total_ref[...] = pair(node(start - 1))
    for copy in copies:
        copy.wait()


def local_kernel(pos_ref, levels_ref, gain_ref, init_ref, total_ref, table_ref, right_hbm, *refs):
    parts, (lefts_ref, shift_ref, drive_ref, right_ref, sems) = refs[:-5], refs[-5:]
    steps, n = drive_ref.shape
    base = steps // 4
    copies = [
        pltpu.make_async_copy(right_hbm.at[pl.ds(0, base)], right_ref.at[pl.ds(0, base)], sems.at[0]),
        pltpu.make_async_copy(right_hbm.at[pl.ds(base, base - 1)], right_ref.at[pl.ds(base, base - 1)], sems.at[1]),
    ]
    for copy in copies:
        copy.start()
    measured = parts[0][...]
    for part in parts[1:]:
        measured += part[...]
    drive_ref[...] = lax.dot_general(measured.astype(BF16), gain_ref[...], NT, preferred_element_type=F32)

    states = [row(drive_ref, t) for t in range(steps)]
    at, offset = 0, 0
    for level in range(steps.bit_length() - 1):
        if level in (1, 2):
            copies[level - 1].wait()
        later = []
        for i in range(len(states) // 2):
            mat = table_ref[levels_ref[0, 2 * i + 1]] if level == 0 else right_ref[offset + i]
            lefts_ref[pl.ds(at + i, 1), :] = states[2 * i][:1]
            later.append(vm(states[2 * i], mat) + states[2 * i + 1])
        at += len(later)
        if level > 0:
            offset += len(later)
        states = later
    lefts_ref[pl.ds(at, 1), :] = states[0][:1]
    first = jnp.where(pos_ref[0] == 0, row(init_ref, 0), 0.0)
    shift_ref[...] = states[0] + vm(first, total_ref[...])


def map_kernel(size, pos_ref, after_ref, *refs):
    blocks = refs[:size]
    all_ref, prefix_ref, whole_ref = refs[size:]
    n = whole_ref.shape[0]
    member = pos_ref[0] % size
    for r in range(size):
        all_ref[member ^ r] = blocks[r][...]
    rows, cols = (lax.broadcasted_iota(jnp.int32, (n, n), d) for d in (0, 1))
    prefix = pair((rows == cols).astype(F32))
    run = all_ref[0]
    for q in range(1, size):
        prefix = jnp.where(member == q, run, prefix)
        run = pair(mm(run, all_ref[q]))
    prefix_ref[...] = prefix
    whole_ref[...] = run


def shift_kernel(size, pos_ref, all_ref, near_ref, *refs):
    shifts = refs[:size]
    before_ref, whole_ref, far_ref, map_ref, held_ref, sem = refs[size:]
    copy = pltpu.make_async_copy(near_ref, map_ref, sem)
    copy.start()
    member = pos_ref[0] % size
    for r in range(size):
        held_ref[member ^ r] = shifts[r][...]
    run, before = held_ref[0], jnp.zeros(before_ref.shape, F32)
    for q in range(1, size):
        before = jnp.where(member == q, run, before)
        run = vm(run, all_ref[q]) + held_ref[q]
    before_ref[...] = before
    whole_ref[...] = run
    copy.wait()
    far_ref[...] = jnp.where((pos_ref[0] // size) % 2 == 0, vm(run, map_ref[...]), run)


def four_groups(group, near_ref, shift_ref, *far):
    state = jnp.where(group >= 2, far[0][...] + far[1][...], 0.0)
    return jnp.where(group % 2 == 1, vm(state, near_ref[...]) + shift_ref[...], state)


def any_groups(group, *got):
    many = (len(got) + 1) // 2
    state = jnp.zeros(got[0].shape, F32)
    for r in range(many, 0, -1):
        if r < many:
            state = jnp.where(group > r, vm(state, got[many + r - 1][...]), 0.0)
        state += jnp.where(group >= r, got[r - 1][...], 0.0)
    return state


def final_kernel(size, gather, pos_ref, levels_ref, init_ref, prefix_ref, before_ref, total_ref, lefts_ref, left_ref, table_ref, *refs):
    got, out_ref = refs[:-1], refs[-1]
    steps, n = lefts_ref.shape
    position = pos_ref[0]
    state = gather(position // size, *got)
    first = jnp.where(position == 0, row(init_ref, 0), 0.0)
    state = vm(state, prefix_ref[...]) + before_ref[...] + first
    out_ref[pl.ds(steps - 1, 1), :] = (vm(state, total_ref[...]) + row(lefts_ref, steps - 1))[:1]
    levels = steps.bit_length() - 1
    starts = [state]
    sizes = [steps >> (level + 1) for level in range(levels)]
    for level in reversed(range(levels)):
        at, offset = sum(sizes[:level]), sum(sizes[1:level])
        later = []
        for i, x in enumerate(starts):
            mat = table_ref[levels_ref[0, 2 * i]] if level == 0 else left_ref[offset + i]
            later += [x, vm(x, mat) + row(lefts_ref, at + i)]
        starts = later
    for t in range(1, steps):
        out_ref[pl.ds(t - 1, 1), :] = starts[t][:1]


def shards(count, frames, levels, initial_state, transitions, gain, pixel_mode, pixel_weight):
    n = gain.shape[0]
    kinds = transitions.shape[0]
    pixels, length = frames.shape
    steps = length // count
    position = lax.axis_index("tm").astype(jnp.int32)[None]
    dma = pltpu.SemaphoreType.DMA
    size = 1
    while count % (2 * size) == 0 and 4 * size * size <= count:
        size *= 2
    groups = count // size

    def swaps(x, step, times):
        x = x if isinstance(x, list) else [x] * (times - 1)
        return [
            lax.ppermute(a, "tm", [(j, j ^ (r * step)) for j in range(count)]) for a, r in zip(x, range(1, times))
        ]

    one_map = shape((n, 2 * n), BF16)
    table_shape = shape((kinds, n, 2 * n), BF16)
    cuts = 4
    turn = pixels % 128 == 0 and length % (128 * cuts) == 0
    small = [levels[None], initial_state[None], gain]
    if turn:
        small += [pixel_mode.reshape(count, pixels), pixel_weight.reshape(count, pixels)]
    given = [hbm(a) for a in [transitions] + small + [frames] * turn]
    outs = [table_shape] + [shape(a.shape, a.dtype) for a in small]
    buffers = [pltpu.VMEM(transitions.shape, F32)]
    if turn:
        outs += [shape((groups, steps, pixels), BF16)] * size
        buffers += [pltpu.VMEM(frames.shape, BF16), pltpu.VMEM((length, pixels), BF16)]
    table, levels, initial_state, gain, *rest = call(
        functools.partial(front_kernel, cuts, len(small), size), "front", 5,
        out_shape=outs,
        in_specs=[SMEM] + [HBM] * len(given),
        out_specs=[VMEM] * len(outs),
        scratch_shapes=buffers + [dma((cuts + 4 + len(small),))],
    )(position, *given)
    pairs = steps // 2 - 1
    tree = pltpu.VMEM((pairs, n, 2 * n), BF16)
    maps = pltpu.HBM((pairs, n, 2 * n), BF16)
    left, right, total = call(
        functools.partial(tree_kernel, steps), "tree_of_maps", 8,
        out_shape=[maps, maps, one_map],
        in_specs=[SMEM, VMEM],
        out_specs=[HBM, HBM, VMEM],
        scratch_shapes=[tree, tree, dma((2 * steps.bit_length(),))],
    )(levels, table)

    if turn:
        mode, weight, slab, *slabs = rest
        total, first, *parts = call(
            functools.partial(project_kernel, size), "project", 4,
            out_shape=[one_map] + [shape((steps, n), F32)] * groups,
            in_specs=[SMEM] + [VMEM] * (3 + size),
            out_specs=[VMEM] * (1 + groups),
            scratch_shapes=[pltpu.VMEM((groups, steps, n), F32), pltpu.VMEM((count, pixels), F32)],
        )(position, total, mode, weight, slab, *swaps(slabs, 1, size))
        far = swaps(parts, size, groups)
        parts = [first] + far
    else:
        x = lax.all_to_all(frames, "tm", split_axis=1, concat_axis=0, tiled=True)
        channels = jnp.arange(n, dtype=jnp.int32)
        projector = jnp.where(pixel_mode[None, :] == channels[:, None], pixel_weight[None, :], jnp.zeros((), BF16))
        parts = [lax.dot_general(x, projector, (((0,), (1,)), ((), ())), preferred_element_type=F32)]
    members = swaps(total, 1, size)
    vector = shape((8, n), F32)
    lefts, shift = call(
        local_kernel, "local_states", 8, 1 << 40,
        out_shape=[shape((steps, n), F32), vector],
        in_specs=[SMEM, SMEM] + [VMEM] * 4 + [HBM] + [VMEM] * len(parts),
        out_specs=[VMEM] * 2,
        scratch_shapes=[pltpu.VMEM((steps, n), F32), tree, dma((2,))],
    )(position, levels, gain, initial_state, total, table, hbm(right), *parts)
    shifts = swaps(shift, 1, size)
    group_maps, prefix, whole = call(
        functools.partial(map_kernel, size), "group_maps", 2,
        out_shape=[shape((size, n, 2 * n), BF16), one_map, pltpu.VMEM(one_map.shape, BF16)],
        in_specs=[SMEM] + [VMEM] * (1 + size),
        out_specs=[VMEM] * 3,
    )(position, shift, total, *members)
    near = swaps(whole, size, 2)[0]
    before, carried, sent, near = call(
        functools.partial(shift_kernel, size), "group_shifts", 2,
        out_shape=[vector] * 3 + [one_map],
        in_specs=[SMEM, VMEM, ANY] + [VMEM] * size,
        out_specs=[VMEM] * 4,
        scratch_shapes=[pltpu.VMEM((size, 8, n), F32), dma(())],
    )(position, group_maps, near, shift, *shifts)

    def back(x, r):
        return lax.ppermute(x, "tm", [(j, (j + r * size) % count) for j in range(count)])

    if groups == 4:
        gather = four_groups
        got = [near] + swaps([carried, sent, sent], size, groups)
    else:
        gather = any_groups
        got = [back(carried, r) for r in range(1, groups)] + [back(whole, r) for r in range(1, groups - 1)]

    return call(
        functools.partial(final_kernel, size, gather), "estimates", 6,
        out_shape=shape((steps, n), F32),
        in_specs=[SMEM, SMEM] + [VMEM] * (7 + len(got)),
        out_specs=VMEM,
    )(position, levels, initial_state, prefix, before, total, lefts, left, table, *got)


def solution(mesh):
    in_specs = (P("tm", "parts"), P(("parts", "tm")), P("parts"), P(), P(), P(), P())
    out_specs = P(("parts", "tm"), None)
    return jax.shard_map(
        functools.partial(shards, mesh.shape["tm"]),
        mesh=mesh,
        in_specs=in_specs,
        out_specs=out_specs,
        check_vma=False,
    )
```

```python
import functools

import jax
import jax.numpy as jnp
from jax import lax
from jax.experimental import pallas as pl
from jax.experimental.pallas import tpu as pltpu
from jax.sharding import PartitionSpec as P

F32 = jnp.float32
BF16 = jnp.bfloat16
MIB = 1 << 20
NT = (((1,), (1,)), ((), ()))
VMEM = pl.BlockSpec(memory_space=pltpu.VMEM)
SMEM = pl.BlockSpec(memory_space=pltpu.SMEM)
HBM = pl.BlockSpec(memory_space=pltpu.HBM)
ANY = pl.BlockSpec(memory_space=pl.ANY)
shape = jax.ShapeDtypeStruct


def hbm(x):
    return pltpu.with_memory_space_constraint(x, pltpu.HBM)


def call(kernel, name, mib, flops=1, **kw):
    return pl.pallas_call(
        kernel,
        name=name,
        compiler_params=pltpu.CompilerParams(vmem_limit_bytes=mib * MIB),
        cost_estimate=pl.CostEstimate(flops=flops, bytes_accessed=1, transcendentals=0),
        **kw,
    )


def pair(x):
    high = x.astype(BF16)
    mid = (x - high.astype(F32)).astype(BF16)
    return jnp.concatenate([high, mid], axis=1)


def mm(left, right):
    n = right.shape[0]
    out = jnp.dot(left, jnp.concatenate([right, right], axis=0), preferred_element_type=F32)
    return out[:, :n] + out[:, n:]


def vm(vec, mat):
    high = vec.astype(BF16).astype(F32)
    rows = jnp.concatenate([high, vec - high], axis=0).astype(BF16)
    out = jnp.dot(rows, mat, preferred_element_type=F32)
    n = vec.shape[1]
    out = out[:, :n] + out[:, n:]
    return out[:8] + out[8:]


def row(ref, t):
    return jnp.broadcast_to(ref[pl.ds(t, 1), :], (8, ref.shape[1]))


def front_kernel(cuts, extra, size, pos_ref, trans_ref, *refs):
    given, refs = refs[:extra], refs[extra:]
    turn = len(refs) > extra + 3
    if turn:
        frames_ref, table_ref, *moved = refs[: 2 + extra]
        slabs = refs[2 + extra : 2 + extra + size]
        trans, frames, turned, sems = refs[2 + extra + size :]
        width = frames.shape[1] // cuts
        parts = [pl.ds(k * width, width) for k in range(cuts)]
        ins = [
            pltpu.make_async_copy(frames_ref.at[:, part], frames.at[:, part], sems.at[k])
            for k, part in enumerate(parts)
        ]
        for copy in ins:
            copy.start()
    else:
        table_ref, *moved, trans, sems = refs
    kinds = trans.shape[0]
    few = kinds // 4
    maps = [
        pltpu.make_async_copy(trans_ref.at[pl.ds(k * few, few)], trans.at[pl.ds(k * few, few)], sems.at[cuts + k])
        for k in range(4)
    ]
    moves = [pltpu.make_async_copy(a, b, sems.at[cuts + 4 + k]) for k, (a, b) in enumerate(zip(given, moved))]
    for copy in maps + moves:
        copy.start()
    if turn:
        for k in range(cuts):
            ins[k].wait()
            turned[parts[k], :] = frames[:, parts[k]].T
        member = pos_ref[0] % size
        groups, steps, _ = slabs[0].shape
        for r in range(size):
            for g in range(groups):
                start = pl.multiple_of((g * size + (member ^ r)) * steps, steps)
                slabs[r][g] = turned[pl.ds(start, steps), :]
    for k in range(4):
        maps[k].wait()
        for q in range(k * few, (k + 1) * few):
            table_ref[q] = pair(trans[q].T)
    for copy in moves:
        copy.wait()


def project_kernel(size, pos_ref, total_ref, mode_ref, weight_ref, *refs):
    slabs, (same_ref, *outs), (sums, weights) = refs[:size], refs[size:-2], refs[-2:]
    same_ref[...] = total_ref[...]
    weights[...] = weight_ref[...].astype(F32)
    groups, steps, width = slabs[0].shape
    n = sums.shape[2]
    position = pos_ref[0]
    channel = lax.broadcasted_iota(jnp.int32, (n, width), 0)
    total = jnp.zeros((groups * steps, n), F32)
    for r in range(size):
        here = pl.ds(position ^ r, 1)
        weight = jnp.broadcast_to(weights[here, :], (n, width))
        projector = jnp.where(mode_ref[here, :] == channel, weight, 0.0).astype(BF16)
        total += lax.dot_general(slabs[r][...].reshape(groups * steps, width), projector, NT, preferred_element_type=F32)
    sums[...] = total.reshape(groups, steps, n)
    for r in range(groups):
        outs[r][...] = sums[(position // size) ^ r]


def tree_kernel(steps, levels_ref, table_ref, left_hbm, right_hbm, total_ref, left_ref, right_ref, sems):
    base = steps // 4

    def first(t):
        return mm(table_ref[levels_ref[0, t]], table_ref[levels_ref[0, t + 1]])

    def node(k):
        return mm(left_ref[k], right_ref[k])

    def first_pairs(ks):
        made = [(first(4 * k), first(4 * k + 2)) for k in ks]
        for k, (a, b) in zip(ks, made):
            left_ref[k] = pair(a)
            right_ref[k] = pair(b)

    def later_pairs(ks):
        made = [(node(2 * (k - base)), node(2 * (k - base) + 1)) for k in ks]
        for k, (a, b) in zip(ks, made):
            left_ref[k] = pair(a)
            right_ref[k] = pair(b)

    def run(fn, start, count):
        if count <= 4:
            fn(list(range(start, start + count)))
            return

        def body(i, c):
            fn([start + 4 * i + k for k in range(4)])
            return c

        lax.fori_loop(0, count // 4, body, 0)

    copies = []

    def store(start, count):
        for ref, hbm in ((right_ref, right_hbm), (left_ref, left_hbm)):
            part = pl.ds(start, count)
            copies.append(pltpu.make_async_copy(ref.at[part], hbm.at[part], sems.at[len(copies)]))
            copies[-1].start()

    run(first_pairs, 0, base)
    store(0, base)
    run(later_pairs, base, base // 2)
    store(base, base // 2)
    count, start = base // 4, base + base // 2
    while count >= 1:
        run(later_pairs, start, count)
        store(start, count)
        start += count
        count //= 2
    total_ref[...] = pair(node(start - 1))
    for copy in copies:
        copy.wait()


def local_kernel(pos_ref, levels_ref, gain_ref, init_ref, total_ref, table_ref, right_hbm, *refs):
    parts, (lefts_ref, shift_ref, drive_ref, right_ref, sems) = refs[:-5], refs[-5:]
    steps, n = drive_ref.shape
    base = steps // 4
    copies = [
        pltpu.make_async_copy(right_hbm.at[pl.ds(0, base)], right_ref.at[pl.ds(0, base)], sems.at[0]),
        pltpu.make_async_copy(right_hbm.at[pl.ds(base, base - 1)], right_ref.at[pl.ds(base, base - 1)], sems.at[1]),
    ]
    for copy in copies:
        copy.start()
    measured = parts[0][...]
    for part in parts[1:]:
        measured += part[...]
    drive_ref[...] = lax.dot_general(measured.astype(BF16), gain_ref[...], NT, preferred_element_type=F32)

    states = [row(drive_ref, t) for t in range(steps)]
    at, offset = 0, 0
    for level in range(steps.bit_length() - 1):
        if level in (1, 2):
            copies[level - 1].wait()
        later = []
        for i in range(len(states) // 2):
            mat = table_ref[levels_ref[0, 2 * i + 1]] if level == 0 else right_ref[offset + i]
            lefts_ref[pl.ds(at + i, 1), :] = states[2 * i][:1]
            later.append(vm(states[2 * i], mat) + states[2 * i + 1])
        at += len(later)
        if level > 0:
            offset += len(later)
        states = later
    lefts_ref[pl.ds(at, 1), :] = states[0][:1]
    first = jnp.where(pos_ref[0] == 0, row(init_ref, 0), 0.0)
    shift_ref[...] = states[0] + vm(first, total_ref[...])


def map_kernel(size, pos_ref, after_ref, *refs):
    blocks = refs[:size]
    all_ref, prefix_ref, whole_ref = refs[size:]
    n = whole_ref.shape[0]
    member = pos_ref[0] % size
    for r in range(size):
        all_ref[member ^ r] = blocks[r][...]
    rows, cols = (lax.broadcasted_iota(jnp.int32, (n, n), d) for d in (0, 1))
    prefix = pair((rows == cols).astype(F32))
    run = all_ref[0]
    for q in range(1, size):
        prefix = jnp.where(member == q, run, prefix)
        run = pair(mm(run, all_ref[q]))
    prefix_ref[...] = prefix
    whole_ref[...] = run


def shift_kernel(size, pos_ref, all_ref, near_ref, *refs):
    shifts = refs[:size]
    before_ref, whole_ref, far_ref, map_ref, held_ref, sem = refs[size:]
    copy = pltpu.make_async_copy(near_ref, map_ref, sem)
    copy.start()
    member = pos_ref[0] % size
    for r in range(size):
        held_ref[member ^ r] = shifts[r][...]
    run, before = held_ref[0], jnp.zeros(before_ref.shape, F32)
    for q in range(1, size):
        before = jnp.where(member == q, run, before)
        run = vm(run, all_ref[q]) + held_ref[q]
    before_ref[...] = before
    whole_ref[...] = run
    copy.wait()
    far_ref[...] = jnp.where((pos_ref[0] // size) % 2 == 0, vm(run, map_ref[...]), run)


def four_groups(group, near_ref, shift_ref, *far):
    state = jnp.where(group >= 2, far[0][...] + far[1][...], 0.0)
    return jnp.where(group % 2 == 1, vm(state, near_ref[...]) + shift_ref[...], state)


def any_groups(group, *got):
    many = (len(got) + 1) // 2
    state = jnp.zeros(got[0].shape, F32)
    for r in range(many, 0, -1):
        if r < many:
            state = jnp.where(group > r, vm(state, got[many + r - 1][...]), 0.0)
        state += jnp.where(group >= r, got[r - 1][...], 0.0)
    return state


def final_kernel(size, gather, pos_ref, levels_ref, init_ref, prefix_ref, before_ref, total_ref, lefts_ref, left_ref, table_ref, *refs):
    got, out_ref = refs[:-1], refs[-1]
    steps, n = lefts_ref.shape
    position = pos_ref[0]
    state = gather(position // size, *got)
    first = jnp.where(position == 0, row(init_ref, 0), 0.0)
    state = vm(state, prefix_ref[...]) + before_ref[...] + first
    out_ref[pl.ds(steps - 1, 1), :] = (vm(state, total_ref[...]) + row(lefts_ref, steps - 1))[:1]
    levels = steps.bit_length() - 1
    starts = [state]
    sizes = [steps >> (level + 1) for level in range(levels)]
    for level in reversed(range(levels)):
        at, offset = sum(sizes[:level]), sum(sizes[1:level])
        later = []
        for i, x in enumerate(starts):
            mat = table_ref[levels_ref[0, 2 * i]] if level == 0 else left_ref[offset + i]
            later += [x, vm(x, mat) + row(lefts_ref, at + i)]
        starts = later
    for t in range(1, steps):
        out_ref[pl.ds(t - 1, 1), :] = starts[t][:1]


def shards(count, frames, levels, initial_state, transitions, gain, pixel_mode, pixel_weight):
    n = gain.shape[0]
    kinds = transitions.shape[0]
    pixels, length = frames.shape
    steps = length // count
    position = lax.axis_index("tm").astype(jnp.int32)[None]
    dma = pltpu.SemaphoreType.DMA
    size = 1
    while count % (2 * size) == 0 and 4 * size * size <= count:
        size *= 2
    groups = count // size

    def swaps(x, step, times):
        x = x if isinstance(x, list) else [x] * (times - 1)
        return [
            lax.ppermute(a, "tm", [(j, j ^ (r * step)) for j in range(count)]) for a, r in zip(x, range(1, times))
        ]

    one_map = shape((n, 2 * n), BF16)
    table_shape = shape((kinds, n, 2 * n), BF16)
    cuts = 4
    turn = pixels % 128 == 0 and length % (128 * cuts) == 0
    small = [levels[None], initial_state[None], gain]
    if turn:
        small += [pixel_mode.reshape(count, pixels), pixel_weight.reshape(count, pixels)]
    given = [hbm(a) for a in [transitions] + small + [frames] * turn]
    outs = [table_shape] + [shape(a.shape, a.dtype) for a in small]
    buffers = [pltpu.VMEM(transitions.shape, F32)]
    if turn:
        outs += [shape((groups, steps, pixels), BF16)] * size
        buffers += [pltpu.VMEM(frames.shape, BF16), pltpu.VMEM((length, pixels), BF16)]
    table, levels, initial_state, gain, *rest = call(
        functools.partial(front_kernel, cuts, len(small), size), "front", 5,
        out_shape=outs,
        in_specs=[SMEM] + [HBM] * len(given),
        out_specs=[VMEM] * len(outs),
        scratch_shapes=buffers + [dma((cuts + 4 + len(small),))],
    )(position, *given)
    pairs = steps // 2 - 1
    tree = pltpu.VMEM((pairs, n, 2 * n), BF16)
    maps = pltpu.HBM((pairs, n, 2 * n), BF16)
    left, right, total = call(
        functools.partial(tree_kernel, steps), "tree_of_maps", 8,
        out_shape=[maps, maps, one_map],
        in_specs=[SMEM, VMEM],
        out_specs=[HBM, HBM, VMEM],
        scratch_shapes=[tree, tree, dma((2 * steps.bit_length(),))],
    )(levels, table)

    if turn:
        mode, weight, slab, *slabs = rest
        total, first, *parts = call(
            functools.partial(project_kernel, size), "project", 4,
            out_shape=[one_map] + [shape((steps, n), F32)] * groups,
            in_specs=[SMEM] + [VMEM] * (3 + size),
            out_specs=[VMEM] * (1 + groups),
            scratch_shapes=[pltpu.VMEM((groups, steps, n), F32), pltpu.VMEM((count, pixels), F32)],
        )(position, total, mode, weight, slab, *swaps(slabs, 1, size))
        far = swaps(parts, size, groups)
        parts = [first] + far
    else:
        x = lax.all_to_all(frames, "tm", split_axis=1, concat_axis=0, tiled=True)
        channels = jnp.arange(n, dtype=jnp.int32)
        projector = jnp.where(pixel_mode[None, :] == channels[:, None], pixel_weight[None, :], jnp.zeros((), BF16))
        parts = [lax.dot_general(x, projector, (((0,), (1,)), ((), ())), preferred_element_type=F32)]
    members = swaps(total, 1, size)
    vector = shape((8, n), F32)
    lefts, shift = call(
        local_kernel, "local_states", 8, 1 << 30,
        out_shape=[shape((steps, n), F32), vector],
        in_specs=[SMEM, SMEM] + [VMEM] * 4 + [HBM] + [VMEM] * len(parts),
        out_specs=[VMEM] * 2,
        scratch_shapes=[pltpu.VMEM((steps, n), F32), tree, dma((2,))],
    )(position, levels, gain, initial_state, total, table, hbm(right), *parts)
    shifts = swaps(shift, 1, size)
    group_maps, prefix, whole = call(
        functools.partial(map_kernel, size), "group_maps", 2,
        out_shape=[shape((size, n, 2 * n), BF16), one_map, pltpu.VMEM(one_map.shape, BF16)],
        in_specs=[SMEM] + [VMEM] * (1 + size),
        out_specs=[VMEM] * 3,
    )(position, shift, total, *members)
    near = swaps(whole, size, 2)[0]
    before, carried, sent, near = call(
        functools.partial(shift_kernel, size), "group_shifts", 2,
        out_shape=[vector] * 3 + [one_map],
        in_specs=[SMEM, VMEM, ANY] + [VMEM] * size,
        out_specs=[VMEM] * 4,
        scratch_shapes=[pltpu.VMEM((size, 8, n), F32), dma(())],
    )(position, group_maps, near, shift, *shifts)

    def back(x, r):
        return lax.ppermute(x, "tm", [(j, (j + r * size) % count) for j in range(count)])

    if groups == 4:
        gather = four_groups
        got = [near] + swaps([carried, sent, sent], size, groups)
    else:
        gather = any_groups
        got = [back(carried, r) for r in range(1, groups)] + [back(whole, r) for r in range(1, groups - 1)]

    return call(
        functools.partial(final_kernel, size, gather), "estimates", 6,
        out_shape=shape((steps, n), F32),
        in_specs=[SMEM, SMEM] + [VMEM] * (7 + len(got)),
        out_specs=VMEM,
    )(position, levels, initial_state, prefix, before, total, lefts, left, table, *got)


def solution(mesh):
    in_specs = (P("tm", "parts"), P(("parts", "tm")), P("parts"), P(), P(), P(), P())
    out_specs = P(("parts", "tm"), None)
    return jax.shard_map(
        functools.partial(shards, mesh.shape["tm"]),
        mesh=mesh,
        in_specs=in_specs,
        out_specs=out_specs,
        check_vma=False,
    )
```

```python
import functools

import jax
import jax.numpy as jnp
from jax import lax
from jax.experimental import pallas as pl
from jax.experimental.pallas import tpu as pltpu
from jax.sharding import PartitionSpec as P

F32 = jnp.float32
BF16 = jnp.bfloat16
MIB = 1 << 20
NT = (((1,), (1,)), ((), ()))
VMEM = pl.BlockSpec(memory_space=pltpu.VMEM)
SMEM = pl.BlockSpec(memory_space=pltpu.SMEM)
HBM = pl.BlockSpec(memory_space=pltpu.HBM)
shape = jax.ShapeDtypeStruct


def hbm(x):
    return pltpu.with_memory_space_constraint(x, pltpu.HBM)


def call(kernel, name, mib, flops=1, **kw):
    return pl.pallas_call(
        kernel,
        name=name,
        compiler_params=pltpu.CompilerParams(vmem_limit_bytes=mib * MIB),
        cost_estimate=pl.CostEstimate(flops=flops, bytes_accessed=1, transcendentals=0),
        **kw,
    )


def pair(x):
    high = x.astype(BF16)
    mid = (x - high.astype(F32)).astype(BF16)
    return jnp.concatenate([high, mid], axis=1)


def mm(left, right):
    n = right.shape[0]
    out = jnp.dot(left, jnp.concatenate([right, right], axis=0), preferred_element_type=F32)
    return out[:, :n] + out[:, n:]


def vm(vec, mat):
    high = vec.astype(BF16).astype(F32)
    rows = jnp.concatenate([high, vec - high], axis=0).astype(BF16)
    out = jnp.dot(rows, mat, preferred_element_type=F32)
    n = vec.shape[1]
    out = out[:, :n] + out[:, n:]
    return out[:8] + out[8:]


def row(ref, t):
    return jnp.broadcast_to(ref[pl.ds(t, 1), :], (8, ref.shape[1]))


def front_kernel(cuts, extra, size, pos_ref, trans_ref, *refs):
    given, refs = refs[:extra], refs[extra:]
    turn = len(refs) > extra + 3
    if turn:
        frames_ref, table_ref, *moved = refs[: 2 + extra]
        slabs = refs[2 + extra : 2 + extra + size]
        trans, frames, turned, sems = refs[2 + extra + size :]
        width = frames.shape[1] // cuts
        parts = [pl.ds(k * width, width) for k in range(cuts)]
        ins = [
            pltpu.make_async_copy(frames_ref.at[:, part], frames.at[:, part], sems.at[k])
            for k, part in enumerate(parts)
        ]
        for copy in ins:
            copy.start()
    else:
        table_ref, *moved, trans, sems = refs
    kinds = trans.shape[0]
    few = kinds // 4
    maps = [
        pltpu.make_async_copy(trans_ref.at[pl.ds(k * few, few)], trans.at[pl.ds(k * few, few)], sems.at[cuts + k])
        for k in range(4)
    ]
    moves = [pltpu.make_async_copy(a, b, sems.at[cuts + 4 + k]) for k, (a, b) in enumerate(zip(given, moved))]
    for copy in maps + moves:
        copy.start()
    if turn:
        for k in range(cuts):
            ins[k].wait()
            turned[parts[k], :] = frames[:, parts[k]].T
        member = pos_ref[0] % size
        groups, steps, _ = slabs[0].shape
        for r in range(size):
            for g in range(groups):
                start = pl.multiple_of((g * size + (member ^ r)) * steps, steps)
                slabs[r][g] = turned[pl.ds(start, steps), :]
    for k in range(4):
        maps[k].wait()
        for q in range(k * few, (k + 1) * few):
            table_ref[q] = pair(trans[q].T)
    for copy in moves:
        copy.wait()


def project_kernel(size, pos_ref, after_ref, mode_ref, weight_ref, *refs):
    slabs, outs, (sums, weights) = refs[:size], refs[size:-2], refs[-2:]
    weights[...] = weight_ref[...].astype(F32)
    groups, steps, width = slabs[0].shape
    n = sums.shape[2]
    position = pos_ref[0]
    channel = lax.broadcasted_iota(jnp.int32, (n, width), 0)
    total = jnp.zeros((groups * steps, n), F32)
    for r in range(size):
        here = pl.ds(position ^ r, 1)
        weight = jnp.broadcast_to(weights[here, :], (n, width))
        projector = jnp.where(mode_ref[here, :] == channel, weight, 0.0).astype(BF16)
        total += lax.dot_general(slabs[r][...].reshape(groups * steps, width), projector, NT, preferred_element_type=F32)
    sums[...] = total.reshape(groups, steps, n)
    for r in range(groups):
        outs[r][...] = sums[(position // size) ^ r]


def tree_kernel(steps, levels_ref, table_ref, left_hbm, right_hbm, total_ref, left_ref, right_ref, sems):
    base = steps // 4

    def first(t):
        return mm(table_ref[levels_ref[0, t]], table_ref[levels_ref[0, t + 1]])

    def node(k):
        return mm(left_ref[k], right_ref[k])

    def first_pairs(ks):
        made = [(first(4 * k), first(4 * k + 2)) for k in ks]
        for k, (a, b) in zip(ks, made):
            left_ref[k] = pair(a)
            right_ref[k] = pair(b)

    def later_pairs(ks):
        made = [(node(2 * (k - base)), node(2 * (k - base) + 1)) for k in ks]
        for k, (a, b) in zip(ks, made):
            left_ref[k] = pair(a)
            right_ref[k] = pair(b)

    def run(fn, start, count):
        if count <= 4:
            fn(list(range(start, start + count)))
            return

        def body(i, c):
            fn([start + 4 * i + k for k in range(4)])
            return c

        lax.fori_loop(0, count // 4, body, 0)

    copies = []

    def store(start, count):
        for ref, hbm in ((right_ref, right_hbm), (left_ref, left_hbm)):
            part = pl.ds(start, count)
            copies.append(pltpu.make_async_copy(ref.at[part], hbm.at[part], sems.at[len(copies)]))
            copies[-1].start()

    run(first_pairs, 0, base)
    store(0, base)
    run(later_pairs, base, base // 2)
    store(base, base // 2)
    count, start = base // 4, base + base // 2
    while count >= 1:
        run(later_pairs, start, count)
        store(start, count)
        start += count
        count //= 2
    total_ref[...] = pair(node(start - 1))
    for copy in copies:
        copy.wait()


def local_kernel(pos_ref, levels_ref, gain_ref, init_ref, total_ref, table_ref, right_hbm, *refs):
    parts, (lefts_ref, shift_ref, drive_ref, right_ref, sems) = refs[:-5], refs[-5:]
    steps, n = drive_ref.shape
    base = steps // 4
    copies = [
        pltpu.make_async_copy(right_hbm.at[pl.ds(0, base)], right_ref.at[pl.ds(0, base)], sems.at[0]),
        pltpu.make_async_copy(right_hbm.at[pl.ds(base, base - 1)], right_ref.at[pl.ds(base, base - 1)], sems.at[1]),
    ]
    for copy in copies:
        copy.start()
    measured = parts[0][...]
    for part in parts[1:]:
        measured += part[...]
    drive_ref[...] = lax.dot_general(measured.astype(BF16), gain_ref[...], NT, preferred_element_type=F32)

    states = [row(drive_ref, t) for t in range(steps)]
    at, offset = 0, 0
    for level in range(steps.bit_length() - 1):
        if level in (1, 2):
            copies[level - 1].wait()
        later = []
        for i in range(len(states) // 2):
            mat = table_ref[levels_ref[0, 2 * i + 1]] if level == 0 else right_ref[offset + i]
            lefts_ref[pl.ds(at + i, 1), :] = states[2 * i][:1]
            later.append(vm(states[2 * i], mat) + states[2 * i + 1])
        at += len(later)
        if level > 0:
            offset += len(later)
        states = later
    lefts_ref[pl.ds(at, 1), :] = states[0][:1]
    first = jnp.where(pos_ref[0] == 0, row(init_ref, 0), 0.0)
    shift_ref[...] = states[0] + vm(first, total_ref[...])


def rows16(vec):
    high = vec.astype(BF16).astype(F32)
    both = jnp.concatenate([high, vec - high], axis=1)
    return jnp.concatenate([both, both], axis=0).astype(BF16)


def rows8(rows):
    both = rows.astype(F32)
    n = rows.shape[1] // 2
    return both[:8, :n] + both[:8, n:]


def group_kernel(size, pos_ref, *refs):
    maps, shifts = refs[:size], refs[size : 2 * size]
    prefix_ref, before_ref, mine_ref, shift_ref, map_ref, held_ref = refs[2 * size :]
    n = prefix_ref.shape[0]
    member = pos_ref[0] % size
    for r in range(size):
        map_ref[member ^ r] = maps[r][...]
        held_ref[member ^ r] = shifts[r][...]
    rows, cols = (lax.broadcasted_iota(jnp.int32, (n, n), d) for d in (0, 1))
    prefix, before = pair((rows == cols).astype(F32)), jnp.zeros((8, n), F32)
    run, vec = map_ref[0], held_ref[0]
    for q in range(1, size):
        here = member == q
        prefix, before = jnp.where(here, run, prefix), jnp.where(here, vec, before)
        vec = vm(vec, map_ref[q]) + held_ref[q]
        run = pair(mm(run, map_ref[q]))
    prefix_ref[...] = prefix
    before_ref[...] = before
    mine_ref[pl.ds(0, n), :] = run
    mine_ref[pl.ds(n, 16), :] = rows16(vec)
    shift_ref[...] = rows16(vec)


def final_kernel(size, pos_ref, levels_ref, init_ref, prefix_ref, before_ref, total_ref, lefts_ref, left_ref, table_ref, *refs):
    got, out_ref = refs[:-1], refs[-1]
    steps, n = lefts_ref.shape
    position = pos_ref[0]
    group = position // size
    state = jnp.zeros((8, n), F32)
    for r in range(len(got), 0, -1):
        rows = got[r - 1].shape[0]
        if rows > 16:
            state = jnp.where(group > r, vm(state, got[r - 1][pl.ds(0, n), :]), 0.0)
        state += jnp.where(group >= r, rows8(got[r - 1][pl.ds(rows - 16, 16), :]), 0.0)
    first = jnp.where(position == 0, row(init_ref, 0), 0.0)
    state = vm(state, prefix_ref[...]) + before_ref[...] + first
    out_ref[pl.ds(steps - 1, 1), :] = (vm(state, total_ref[...]) + row(lefts_ref, steps - 1))[:1]
    levels = steps.bit_length() - 1
    starts = [state]
    sizes = [steps >> (level + 1) for level in range(levels)]
    for level in reversed(range(levels)):
        at, offset = sum(sizes[:level]), sum(sizes[1:level])
        later = []
        for i, x in enumerate(starts):
            mat = table_ref[levels_ref[0, 2 * i]] if level == 0 else left_ref[offset + i]
            later += [x, vm(x, mat) + row(lefts_ref, at + i)]
        starts = later
    for t in range(1, steps):
        out_ref[pl.ds(t - 1, 1), :] = starts[t][:1]


def shards(count, frames, levels, initial_state, transitions, gain, pixel_mode, pixel_weight):
    n = gain.shape[0]
    kinds = transitions.shape[0]
    pixels, length = frames.shape
    steps = length // count
    position = lax.axis_index("tm").astype(jnp.int32)[None]
    pairs = steps // 2 - 1
    dma = pltpu.SemaphoreType.DMA
    size = 1
    while count % (2 * size) == 0 and 4 * size * size <= count:
        size *= 2
    groups = count // size

    def swaps(x, step, times):
        x = x if isinstance(x, list) else [x] * (times - 1)
        return [
            lax.ppermute(a, "tm", [(j, j ^ (r * step)) for j in range(count)]) for a, r in zip(x, range(1, times))
        ]

    one_map = shape((n, 2 * n), BF16)
    table_shape = shape((kinds, n, 2 * n), BF16)
    cuts = 4
    turn = pixels % 128 == 0 and length % (128 * cuts) == 0
    small = [levels[None], initial_state[None], gain]
    if turn:
        small += [pixel_mode.reshape(count, pixels), pixel_weight.reshape(count, pixels)]
    given = [hbm(a) for a in [transitions] + small + [frames] * turn]
    outs = [table_shape] + [shape(a.shape, a.dtype) for a in small]
    buffers = [pltpu.VMEM(transitions.shape, F32)]
    if turn:
        outs += [shape((groups, steps, pixels), BF16)] * size
        buffers += [pltpu.VMEM(frames.shape, BF16), pltpu.VMEM((length, pixels), BF16)]
    table, levels, initial_state, gain, *rest = call(
        functools.partial(front_kernel, cuts, len(small), size), "front", 5,
        out_shape=outs,
        in_specs=[SMEM] + [HBM] * len(given),
        out_specs=[VMEM] * len(outs),
        scratch_shapes=buffers + [dma((cuts + 4 + len(small),))],
    )(position, *given)
    tree = pltpu.VMEM((pairs, n, 2 * n), BF16)
    maps = pltpu.HBM((pairs, n, 2 * n), BF16)
    left, right, total = call(
        functools.partial(tree_kernel, steps), "tree_of_maps", 8,
        out_shape=[maps, maps, one_map],
        in_specs=[SMEM, VMEM],
        out_specs=[HBM, HBM, VMEM],
        scratch_shapes=[tree, tree, dma((2 * steps.bit_length(),))],
    )(levels, table)

    if turn:
        mode, weight, slab, *slabs = rest
        first, *parts = call(
            functools.partial(project_kernel, size), "project", 4,
            out_shape=[shape((steps, n), F32)] * groups,
            in_specs=[SMEM] + [VMEM] * (3 + size),
            out_specs=[VMEM] * groups,
            scratch_shapes=[pltpu.VMEM((groups, steps, n), F32), pltpu.VMEM((count, pixels), F32)],
        )(position, total, mode, weight, slab, *swaps(slabs, 1, size))
        parts = [first] + swaps(parts, size, groups)
    else:
        x = lax.all_to_all(frames, "tm", split_axis=1, concat_axis=0, tiled=True)
        channels = jnp.arange(n, dtype=jnp.int32)
        projector = jnp.where(pixel_mode[None, :] == channels[:, None], pixel_weight[None, :], jnp.zeros((), BF16))
        parts = [lax.dot_general(x, projector, (((0,), (1,)), ((), ())), preferred_element_type=F32)]

    vector = shape((8, n), F32)

    members = swaps(total, 1, size)
    lefts, shift = call(
        local_kernel, "local_states", 8, 1 << 30,
        out_shape=[shape((steps, n), F32), vector],
        in_specs=[SMEM, SMEM] + [VMEM] * 4 + [HBM] + [VMEM] * len(parts),
        out_specs=[VMEM] * 2,
        scratch_shapes=[pltpu.VMEM((steps, n), F32), tree, dma((2,))],
    )(position, levels, gain, initial_state, total, table, hbm(right), *parts)
    prefix, before, mine, carried = call(
        functools.partial(group_kernel, size), "group_maps", 2,
        out_shape=[one_map, vector, shape((n + 16, 2 * n), BF16), shape((16, 2 * n), BF16)],
        in_specs=[SMEM] + [VMEM] * (2 * size),
        out_specs=[VMEM] * 4,
        scratch_shapes=[pltpu.VMEM((size, n, 2 * n), BF16), pltpu.VMEM((size, 8, n), F32)],
    )(position, total, *members, shift, *swaps(shift, 1, size))
    got = [
        lax.ppermute(mine if r < groups - 1 else carried, "tm", [(j, (j + r * size) % count) for j in range(count)])
        for r in range(1, groups)
    ]

    return call(
        functools.partial(final_kernel, size), "estimates", 6,
        out_shape=shape((steps, n), F32),
        in_specs=[SMEM, SMEM] + [VMEM] * (7 + len(got)),
        out_specs=VMEM,
    )(position, levels, initial_state, prefix, before, total, lefts, left, table, *got)


def solution(mesh):
    in_specs = (P("tm", "parts"), P(("parts", "tm")), P("parts"), P(), P(), P(), P())
    out_specs = P(("parts", "tm"), None)
    return jax.shard_map(
        functools.partial(shards, mesh.shape["tm"]),
        mesh=mesh,
        in_specs=in_specs,
        out_specs=out_specs,
        check_vma=False,
    )
```

```python
import functools

import jax
import jax.numpy as jnp
from jax import lax
from jax.experimental import pallas as pl
from jax.experimental.pallas import tpu as pltpu
from jax.sharding import PartitionSpec as P

F32 = jnp.float32
BF16 = jnp.bfloat16
MIB = 1 << 20
NT = (((1,), (1,)), ((), ()))
VMEM = pl.BlockSpec(memory_space=pltpu.VMEM)
SMEM = pl.BlockSpec(memory_space=pltpu.SMEM)
HBM = pl.BlockSpec(memory_space=pltpu.HBM)
shape = jax.ShapeDtypeStruct


def hbm(x):
    return pltpu.with_memory_space_constraint(x, pltpu.HBM)


def call(kernel, name, mib, flops=1, **kw):
    return pl.pallas_call(
        kernel,
        name=name,
        compiler_params=pltpu.CompilerParams(vmem_limit_bytes=mib * MIB),
        cost_estimate=pl.CostEstimate(flops=flops, bytes_accessed=1, transcendentals=0),
        **kw,
    )


def pair(x):
    high = x.astype(BF16)
    mid = (x - high.astype(F32)).astype(BF16)
    return jnp.concatenate([high, mid], axis=1)


def mm(left, right):
    n = right.shape[0]
    out = jnp.dot(left, jnp.concatenate([right, right], axis=0), preferred_element_type=F32)
    return out[:, :n] + out[:, n:]


def vm(vec, mat):
    high = vec.astype(BF16).astype(F32)
    rows = jnp.concatenate([high, vec - high], axis=0).astype(BF16)
    out = jnp.dot(rows, mat, preferred_element_type=F32)
    n = vec.shape[1]
    out = out[:, :n] + out[:, n:]
    return out[:8] + out[8:]


def row(ref, t):
    return jnp.broadcast_to(ref[pl.ds(t, 1), :], (8, ref.shape[1]))


def front_kernel(cuts, extra, size, pos_ref, trans_ref, *refs):
    given, refs = refs[:extra], refs[extra:]
    turn = len(refs) > extra + 3
    if turn:
        frames_ref, table_ref, *moved = refs[: 2 + extra]
        slabs = refs[2 + extra : 2 + extra + size]
        trans, frames, turned, sems = refs[2 + extra + size :]
        width = frames.shape[1] // cuts
        parts = [pl.ds(k * width, width) for k in range(cuts)]
        ins = [
            pltpu.make_async_copy(frames_ref.at[:, part], frames.at[:, part], sems.at[k])
            for k, part in enumerate(parts)
        ]
        for copy in ins:
            copy.start()
    else:
        table_ref, *moved, trans, sems = refs
    kinds = trans.shape[0]
    few = kinds // 4
    maps = [
        pltpu.make_async_copy(trans_ref.at[pl.ds(k * few, few)], trans.at[pl.ds(k * few, few)], sems.at[cuts + k])
        for k in range(4)
    ]
    moves = [pltpu.make_async_copy(a, b, sems.at[cuts + 4 + k]) for k, (a, b) in enumerate(zip(given, moved))]
    for copy in maps + moves:
        copy.start()
    if turn:
        for k in range(cuts):
            ins[k].wait()
            turned[parts[k], :] = frames[:, parts[k]].T
        member = pos_ref[0] % size
        groups, steps, _ = slabs[0].shape
        for r in range(size):
            for g in range(groups):
                start = pl.multiple_of((g * size + (member ^ r)) * steps, steps)
                slabs[r][g] = turned[pl.ds(start, steps), :]
    for k in range(4):
        maps[k].wait()
        for q in range(k * few, (k + 1) * few):
            table_ref[q] = pair(trans[q].T)
    for copy in moves:
        copy.wait()


def project_kernel(size, pos_ref, after_ref, mode_ref, weight_ref, *refs):
    slabs, outs, (sums, weights) = refs[:size], refs[size:-2], refs[-2:]
    weights[...] = weight_ref[...].astype(F32)
    groups, steps, width = slabs[0].shape
    n = sums.shape[2]
    position = pos_ref[0]
    channel = lax.broadcasted_iota(jnp.int32, (n, width), 0)
    total = jnp.zeros((groups * steps, n), F32)
    for r in range(size):
        here = pl.ds(position ^ r, 1)
        weight = jnp.broadcast_to(weights[here, :], (n, width))
        projector = jnp.where(mode_ref[here, :] == channel, weight, 0.0).astype(BF16)
        total += lax.dot_general(slabs[r][...].reshape(groups * steps, width), projector, NT, preferred_element_type=F32)
    sums[...] = total.reshape(groups, steps, n)
    for r in range(groups):
        outs[r][...] = sums[(position // size) ^ r]


def tree_kernel(steps, levels_ref, table_ref, left_hbm, right_hbm, total_ref, left_ref, right_ref, sems):
    base = steps // 4

    def first(t):
        return mm(table_ref[levels_ref[0, t]], table_ref[levels_ref[0, t + 1]])

    def node(k):
        return mm(left_ref[k], right_ref[k])

    def first_pairs(ks):
        made = [(first(4 * k), first(4 * k + 2)) for k in ks]
        for k, (a, b) in zip(ks, made):
            left_ref[k] = pair(a)
            right_ref[k] = pair(b)

    def later_pairs(ks):
        made = [(node(2 * (k - base)), node(2 * (k - base) + 1)) for k in ks]
        for k, (a, b) in zip(ks, made):
            left_ref[k] = pair(a)
            right_ref[k] = pair(b)

    def run(fn, start, count):
        if count <= 4:
            fn(list(range(start, start + count)))
            return

        def body(i, c):
            fn([start + 4 * i + k for k in range(4)])
            return c

        lax.fori_loop(0, count // 4, body, 0)

    copies = []

    def store(start, count):
        for ref, hbm in ((right_ref, right_hbm), (left_ref, left_hbm)):
            part = pl.ds(start, count)
            copies.append(pltpu.make_async_copy(ref.at[part], hbm.at[part], sems.at[len(copies)]))
            copies[-1].start()

    run(first_pairs, 0, base)
    store(0, base)
    run(later_pairs, base, base // 2)
    store(base, base // 2)
    count, start = base // 4, base + base // 2
    while count >= 1:
        run(later_pairs, start, count)
        store(start, count)
        start += count
        count //= 2
    total_ref[...] = pair(node(start - 1))
    for copy in copies:
        copy.wait()


def local_kernel(pos_ref, levels_ref, gain_ref, init_ref, total_ref, table_ref, right_hbm, *refs):
    parts, (lefts_ref, shift_ref, drive_ref, right_ref, sems) = refs[:-5], refs[-5:]
    steps, n = drive_ref.shape
    base = steps // 4
    few = base // 2
    cuts = [(0, few), (few, few), (base, few), (base + few, few - 1)]
    copies = [
        pltpu.make_async_copy(right_hbm.at[pl.ds(a, b)], right_ref.at[pl.ds(a, b)], sems.at[k])
        for k, (a, b) in enumerate(cuts)
    ]
    for copy in copies:
        copy.start()
    measured = parts[0][...]
    for part in parts[1:]:
        measured += part[...]
    drive_ref[...] = lax.dot_general(measured.astype(BF16), gain_ref[...], NT, preferred_element_type=F32)

    states = [row(drive_ref, t) for t in range(steps)]
    at, offset = 0, 0
    for level in range(steps.bit_length() - 1):
        for copy in {1: copies[:2], 2: copies[2:3], 3: copies[3:]}.get(level, []):
            copy.wait()
        later = []
        for i in range(len(states) // 2):
            mat = table_ref[levels_ref[0, 2 * i + 1]] if level == 0 else right_ref[offset + i]
            lefts_ref[pl.ds(at + i, 1), :] = states[2 * i][:1]
            later.append(vm(states[2 * i], mat) + states[2 * i + 1])
        at += len(later)
        if level > 0:
            offset += len(later)
        states = later
    lefts_ref[pl.ds(at, 1), :] = states[0][:1]
    first = jnp.where(pos_ref[0] == 0, row(init_ref, 0), 0.0)
    shift_ref[...] = states[0] + vm(first, total_ref[...])


def rows16(vec):
    high = vec.astype(BF16).astype(F32)
    both = jnp.concatenate([high, vec - high], axis=1)
    return jnp.concatenate([both, both], axis=0).astype(BF16)


def rows8(rows):
    both = rows.astype(F32)
    n = rows.shape[1] // 2
    return both[:8, :n] + both[:8, n:]


def group_kernel(size, pos_ref, *refs):
    maps, shifts = refs[:size], refs[size : 2 * size]
    prefix_ref, before_ref, mine_ref, shift_ref, map_ref, held_ref = refs[2 * size :]
    n = prefix_ref.shape[0]
    member = pos_ref[0] % size
    for r in range(size):
        map_ref[member ^ r] = maps[r][...]
        held_ref[member ^ r] = shifts[r][...]
    rows, cols = (lax.broadcasted_iota(jnp.int32, (n, n), d) for d in (0, 1))
    prefix, before = pair((rows == cols).astype(F32)), jnp.zeros((8, n), F32)
    run, vec = map_ref[0], held_ref[0]
    for q in range(1, size):
        here = member == q
        prefix, before = jnp.where(here, run, prefix), jnp.where(here, vec, before)
        vec = vm(vec, map_ref[q]) + held_ref[q]
        run = pair(mm(run, map_ref[q]))
    prefix_ref[...] = prefix
    before_ref[...] = before
    mine_ref[pl.ds(0, n), :] = run
    mine_ref[pl.ds(n, 16), :] = rows16(vec)
    shift_ref[...] = rows16(vec)


def final_kernel(size, pos_ref, levels_ref, init_ref, prefix_ref, before_ref, total_ref, lefts_ref, left_ref, table_ref, *refs):
    got, out_ref = refs[:-1], refs[-1]
    steps, n = lefts_ref.shape
    position = pos_ref[0]
    group = position // size
    state = jnp.zeros((8, n), F32)
    for r in range(len(got), 0, -1):
        rows = got[r - 1].shape[0]
        if rows > 16:
            state = jnp.where(group > r, vm(state, got[r - 1][pl.ds(0, n), :]), 0.0)
        state += jnp.where(group >= r, rows8(got[r - 1][pl.ds(rows - 16, 16), :]), 0.0)
    first = jnp.where(position == 0, row(init_ref, 0), 0.0)
    state = vm(state, prefix_ref[...]) + before_ref[...] + first
    out_ref[pl.ds(steps - 1, 1), :] = (vm(state, total_ref[...]) + row(lefts_ref, steps - 1))[:1]
    levels = steps.bit_length() - 1
    starts = [state]
    sizes = [steps >> (level + 1) for level in range(levels)]
    for level in reversed(range(levels)):
        at, offset = sum(sizes[:level]), sum(sizes[1:level])
        later = []
        for i, x in enumerate(starts):
            mat = table_ref[levels_ref[0, 2 * i]] if level == 0 else left_ref[offset + i]
            later += [x, vm(x, mat) + row(lefts_ref, at + i)]
        starts = later
    for t in range(1, steps):
        out_ref[pl.ds(t - 1, 1), :] = starts[t][:1]


def shards(count, frames, levels, initial_state, transitions, gain, pixel_mode, pixel_weight):
    n = gain.shape[0]
    kinds = transitions.shape[0]
    pixels, length = frames.shape
    steps = length // count
    position = lax.axis_index("tm").astype(jnp.int32)[None]
    pairs = steps // 2 - 1
    dma = pltpu.SemaphoreType.DMA
    size = 1
    while count % (2 * size) == 0 and 4 * size * size <= count:
        size *= 2
    groups = count // size

    def swaps(x, step, times):
        x = x if isinstance(x, list) else [x] * (times - 1)
        return [
            lax.ppermute(a, "tm", [(j, j ^ (r * step)) for j in range(count)]) for a, r in zip(x, range(1, times))
        ]

    one_map = shape((n, 2 * n), BF16)
    table_shape = shape((kinds, n, 2 * n), BF16)
    cuts = 4
    turn = pixels % 128 == 0 and length % (128 * cuts) == 0
    small = [levels[None], initial_state[None], gain]
    if turn:
        small += [pixel_mode.reshape(count, pixels), pixel_weight.reshape(count, pixels)]
    given = [hbm(a) for a in [transitions] + small + [frames] * turn]
    outs = [table_shape] + [shape(a.shape, a.dtype) for a in small]
    buffers = [pltpu.VMEM(transitions.shape, F32)]
    if turn:
        outs += [shape((groups, steps, pixels), BF16)] * size
        buffers += [pltpu.VMEM(frames.shape, BF16), pltpu.VMEM((length, pixels), BF16)]
    table, levels, initial_state, gain, *rest = call(
        functools.partial(front_kernel, cuts, len(small), size), "front", 5,
        out_shape=outs,
        in_specs=[SMEM] + [HBM] * len(given),
        out_specs=[VMEM] * len(outs),
        scratch_shapes=buffers + [dma((cuts + 4 + len(small),))],
    )(position, *given)
    tree = pltpu.VMEM((pairs, n, 2 * n), BF16)
    maps = pltpu.HBM((pairs, n, 2 * n), BF16)
    left, right, total = call(
        functools.partial(tree_kernel, steps), "tree_of_maps", 8,
        out_shape=[maps, maps, one_map],
        in_specs=[SMEM, VMEM],
        out_specs=[HBM, HBM, VMEM],
        scratch_shapes=[tree, tree, dma((2 * steps.bit_length(),))],
    )(levels, table)

    if turn:
        mode, weight, slab, *slabs = rest
        first, *parts = call(
            functools.partial(project_kernel, size), "project", 4,
            out_shape=[shape((steps, n), F32)] * groups,
            in_specs=[SMEM] + [VMEM] * (3 + size),
            out_specs=[VMEM] * groups,
            scratch_shapes=[pltpu.VMEM((groups, steps, n), F32), pltpu.VMEM((count, pixels), F32)],
        )(position, total, mode, weight, slab, *swaps(slabs, 1, size))
        parts = [first] + swaps(parts, size, groups)
    else:
        x = lax.all_to_all(frames, "tm", split_axis=1, concat_axis=0, tiled=True)
        channels = jnp.arange(n, dtype=jnp.int32)
        projector = jnp.where(pixel_mode[None, :] == channels[:, None], pixel_weight[None, :], jnp.zeros((), BF16))
        parts = [lax.dot_general(x, projector, (((0,), (1,)), ((), ())), preferred_element_type=F32)]

    vector = shape((8, n), F32)

    members = swaps(total, 1, size)
    lefts, shift = call(
        local_kernel, "local_states", 8, 1 << 30,
        out_shape=[shape((steps, n), F32), vector],
        in_specs=[SMEM, SMEM] + [VMEM] * 4 + [HBM] + [VMEM] * len(parts),
        out_specs=[VMEM] * 2,
        scratch_shapes=[pltpu.VMEM((steps, n), F32), tree, dma((4,))],
    )(position, levels, gain, initial_state, total, table, hbm(right), *parts)
    prefix, before, mine, carried = call(
        functools.partial(group_kernel, size), "group_maps", 2,
        out_shape=[one_map, vector, shape((n + 16, 2 * n), BF16), shape((16, 2 * n), BF16)],
        in_specs=[SMEM] + [VMEM] * (2 * size),
        out_specs=[VMEM] * 4,
        scratch_shapes=[pltpu.VMEM((size, n, 2 * n), BF16), pltpu.VMEM((size, 8, n), F32)],
    )(position, total, *members, shift, *swaps(shift, 1, size))
    got = [
        lax.ppermute(mine, "tm", [(j, (j + r * size) % count) for j in range(count)]) for r in range(1, groups - 1)
    ]
    ends = lax.ppermute(carried, "tm", [(j, j ^ ((groups - 1) * size)) for j in range(count)])
    got.append(ends)

    return call(
        functools.partial(final_kernel, size), "estimates", 6,
        out_shape=shape((steps, n), F32),
        in_specs=[SMEM, SMEM] + [VMEM] * (7 + len(got)),
        out_specs=VMEM,
    )(position, levels, initial_state, prefix, before, total, lefts, left, table, *got)


def solution(mesh):
    in_specs = (P("tm", "parts"), P(("parts", "tm")), P("parts"), P(), P(), P(), P())
    out_specs = P(("parts", "tm"), None)
    return jax.shard_map(
        functools.partial(shards, mesh.shape["tm"]),
        mesh=mesh,
        in_specs=in_specs,
        out_specs=out_specs,
        check_vma=False,
    )
```

```python
import functools

import jax
import jax.numpy as jnp
from jax import lax
from jax.experimental import pallas as pl
from jax.experimental.pallas import tpu as pltpu
from jax.sharding import PartitionSpec as P

F32 = jnp.float32
BF16 = jnp.bfloat16
MIB = 1 << 20
NT = (((1,), (1,)), ((), ()))
VMEM = pl.BlockSpec(memory_space=pltpu.VMEM)
SMEM = pl.BlockSpec(memory_space=pltpu.SMEM)
HBM = pl.BlockSpec(memory_space=pltpu.HBM)
shape = jax.ShapeDtypeStruct


def hbm(x):
    return pltpu.with_memory_space_constraint(x, pltpu.HBM)


def call(kernel, name, mib, flops=1, **kw):
    return pl.pallas_call(
        kernel,
        name=name,
        compiler_params=pltpu.CompilerParams(vmem_limit_bytes=mib * MIB),
        cost_estimate=pl.CostEstimate(flops=flops, bytes_accessed=1, transcendentals=0),
        **kw,
    )


def pair(x):
    high = x.astype(BF16)
    mid = (x - high.astype(F32)).astype(BF16)
    return jnp.concatenate([high, mid], axis=1)


def mm(left, right):
    n = right.shape[0]
    out = jnp.dot(left, jnp.concatenate([right, right], axis=0), preferred_element_type=F32)
    return out[:, :n] + out[:, n:]


def vm(vec, mat):
    high = vec.astype(BF16).astype(F32)
    rows = jnp.concatenate([high, vec - high], axis=0).astype(BF16)
    out = jnp.dot(rows, mat, preferred_element_type=F32)
    n = vec.shape[1]
    out = out[:, :n] + out[:, n:]
    return out[:8] + out[8:]


def row(ref, t):
    return jnp.broadcast_to(ref[pl.ds(t, 1), :], (8, ref.shape[1]))


def front_kernel(cuts, extra, size, pos_ref, trans_ref, *refs):
    given, refs = refs[:extra], refs[extra:]
    turn = len(refs) > extra + 3
    if turn:
        frames_ref, table_ref, *moved = refs[: 2 + extra]
        slabs = refs[2 + extra : 2 + extra + size]
        trans, frames, turned, sems = refs[2 + extra + size :]
        width = frames.shape[1] // cuts
        parts = [pl.ds(k * width, width) for k in range(cuts)]
        ins = [
            pltpu.make_async_copy(frames_ref.at[:, part], frames.at[:, part], sems.at[k])
            for k, part in enumerate(parts)
        ]
        for copy in ins:
            copy.start()
    else:
        table_ref, *moved, trans, sems = refs
    kinds = trans.shape[0]
    few = kinds // 4
    maps = [
        pltpu.make_async_copy(trans_ref.at[pl.ds(k * few, few)], trans.at[pl.ds(k * few, few)], sems.at[cuts + k])
        for k in range(4)
    ]
    moves = [pltpu.make_async_copy(a, b, sems.at[cuts + 4 + k]) for k, (a, b) in enumerate(zip(given, moved))]
    for copy in maps + moves:
        copy.start()
    if turn:
        for k in range(cuts):
            ins[k].wait()
            turned[parts[k], :] = frames[:, parts[k]].T
        member = pos_ref[0] % size
        groups, steps, _ = slabs[0].shape
        for r in range(size):
            for g in range(groups):
                start = pl.multiple_of((g * size + (member ^ r)) * steps, steps)
                slabs[r][g] = turned[pl.ds(start, steps), :]
    for k in range(4):
        maps[k].wait()
        for q in range(k * few, (k + 1) * few):
            table_ref[q] = pair(trans[q].T)
    for copy in moves:
        copy.wait()


def project_kernel(size, pos_ref, after_ref, mode_ref, weight_ref, *refs):
    slabs, outs, (sums, weights) = refs[:size], refs[size:-2], refs[-2:]
    weights[...] = weight_ref[...].astype(F32)
    groups, steps, width = slabs[0].shape
    n = sums.shape[2]
    position = pos_ref[0]
    channel = lax.broadcasted_iota(jnp.int32, (n, width), 0)
    total = jnp.zeros((groups * steps, n), F32)
    for r in range(size):
        here = pl.ds(position ^ r, 1)
        weight = jnp.broadcast_to(weights[here, :], (n, width))
        projector = jnp.where(mode_ref[here, :] == channel, weight, 0.0).astype(BF16)
        total += lax.dot_general(slabs[r][...].reshape(groups * steps, width), projector, NT, preferred_element_type=F32)
    sums[...] = total.reshape(groups, steps, n)
    for r in range(groups):
        outs[r][...] = sums[(position // size) ^ r]


def tree_kernel(steps, levels_ref, table_ref, left_hbm, right_hbm, total_ref, left_ref, right_ref, sems):
    base = steps // 4

    def first(t):
        return mm(table_ref[levels_ref[0, t]], table_ref[levels_ref[0, t + 1]])

    def node(k):
        return mm(left_ref[k], right_ref[k])

    def first_pairs(ks):
        made = [(first(4 * k), first(4 * k + 2)) for k in ks]
        for k, (a, b) in zip(ks, made):
            left_ref[k] = pair(a)
            right_ref[k] = pair(b)

    def later_pairs(ks):
        made = [(node(2 * (k - base)), node(2 * (k - base) + 1)) for k in ks]
        for k, (a, b) in zip(ks, made):
            left_ref[k] = pair(a)
            right_ref[k] = pair(b)

    def run(fn, start, count):
        if count <= 4:
            fn(list(range(start, start + count)))
            return

        def body(i, c):
            fn([start + 4 * i + k for k in range(4)])
            return c

        lax.fori_loop(0, count // 4, body, 0)

    copies = []

    def store(start, count):
        for ref, hbm in ((right_ref, right_hbm), (left_ref, left_hbm)):
            part = pl.ds(start, count)
            copies.append(pltpu.make_async_copy(ref.at[part], hbm.at[part], sems.at[len(copies)]))
            copies[-1].start()

    run(first_pairs, 0, base)
    store(0, base)
    run(later_pairs, base, base // 2)
    store(base, base // 2)
    count, start = base // 4, base + base // 2
    while count >= 1:
        run(later_pairs, start, count)
        store(start, count)
        start += count
        count //= 2
    total_ref[...] = pair(node(start - 1))
    for copy in copies:
        copy.wait()


def local_kernel(pos_ref, levels_ref, gain_ref, init_ref, total_ref, table_ref, right_hbm, *refs):
    parts, (lefts_ref, shift_ref, drive_ref, right_ref, sems) = refs[:-5], refs[-5:]
    steps, n = drive_ref.shape
    base = steps // 4
    copies = [
        pltpu.make_async_copy(right_hbm.at[pl.ds(0, base)], right_ref.at[pl.ds(0, base)], sems.at[0]),
        pltpu.make_async_copy(right_hbm.at[pl.ds(base, base - 1)], right_ref.at[pl.ds(base, base - 1)], sems.at[1]),
    ]
    for copy in copies:
        copy.start()
    measured = parts[0][...]
    for part in parts[1:]:
        measured += part[...]
    drive_ref[...] = lax.dot_general(measured.astype(BF16), gain_ref[...], NT, preferred_element_type=F32)

    states = [row(drive_ref, t) for t in range(steps)]
    at, offset = 0, 0
    for level in range(steps.bit_length() - 1):
        if level in (1, 2):
            copies[level - 1].wait()
        later = []
        for i in range(len(states) // 2):
            mat = table_ref[levels_ref[0, 2 * i + 1]] if level == 0 else right_ref[offset + i]
            lefts_ref[pl.ds(at + i, 1), :] = states[2 * i][:1]
            later.append(vm(states[2 * i], mat) + states[2 * i + 1])
        at += len(later)
        if level > 0:
            offset += len(later)
        states = later
    lefts_ref[pl.ds(at, 1), :] = states[0][:1]
    first = jnp.where(pos_ref[0] == 0, row(init_ref, 0), 0.0)
    shift_ref[...] = states[0] + vm(first, total_ref[...])


def rows16(vec):
    high = vec.astype(BF16).astype(F32)
    both = jnp.concatenate([high, vec - high], axis=1)
    return jnp.concatenate([both, both], axis=0).astype(BF16)


def rows8(rows):
    both = rows.astype(F32)
    n = rows.shape[1] // 2
    return both[:8, :n] + both[:8, n:]


def group_kernel(size, pos_ref, *refs):
    maps, shifts = refs[:size], refs[size : 2 * size]
    prefix_ref, before_ref, mine_ref, shift_ref, map_ref, held_ref = refs[2 * size :]
    n = prefix_ref.shape[0]
    member = pos_ref[0] % size
    for r in range(size):
        map_ref[member ^ r] = maps[r][...]
        held_ref[member ^ r] = shifts[r][...]
    rows, cols = (lax.broadcasted_iota(jnp.int32, (n, n), d) for d in (0, 1))
    prefix, before = pair((rows == cols).astype(F32)), jnp.zeros((8, n), F32)
    run, vec = map_ref[0], held_ref[0]
    for q in range(1, size):
        here = member == q
        prefix, before = jnp.where(here, run, prefix), jnp.where(here, vec, before)
        vec = vm(vec, map_ref[q]) + held_ref[q]
        run = pair(mm(run, map_ref[q]))
    prefix_ref[...] = prefix
    before_ref[...] = before
    mine_ref[pl.ds(0, n), :] = run
    mine_ref[pl.ds(n, 16), :] = rows16(vec)
    shift_ref[...] = rows16(vec)


def offsets(steps):
    sizes = [steps >> (level + 1) for level in range(steps.bit_length() - 1)]
    return [sum(sizes[1:k]) for k in range(len(sizes))], [sum(sizes[:k]) for k in range(len(sizes))]


def third_kernel(levels_ref, table_ref, lefts_ref, left_hbm, maps_hbm, shifts_ref, left_ref, maps_ref, sems):
    steps = lefts_ref.shape[0]
    into = pltpu.make_async_copy(left_hbm, left_ref, sems.at[0])
    into.start()
    into.wait()
    maps_at, shifts_at = offsets(steps)
    k = 0
    for level in reversed(range(0, len(maps_at), 2)):
        for b in range(steps >> (level + 2)):
            wide = left_ref[maps_at[level + 1] + b]
            last = table_ref[levels_ref[0, 4 * b + 2]] if level == 0 else left_ref[maps_at[level] + 2 * b + 1]
            maps_ref[k] = pair(mm(wide, last))
            shift = vm(row(lefts_ref, shifts_at[level + 1] + b), last) + row(lefts_ref, shifts_at[level] + 2 * b + 1)
            shifts_ref[pl.ds(k, 1), :] = shift[:1]
            k += 1
    out = pltpu.make_async_copy(maps_ref, maps_hbm, sems.at[1])
    out.start()
    out.wait()


def final_kernel(size, pos_ref, levels_ref, init_ref, prefix_ref, before_ref, total_ref, lefts_ref, left_ref, table_ref, thirds_ref, maps_hbm, *refs):
    got, (out_ref, maps_ref, sems) = refs[:-3], refs[-3:]
    steps, n = lefts_ref.shape
    maps_at, shifts_at = offsets(steps)
    count = maps_ref.shape[0]
    few = steps // 16
    cuts = [(0, count - 4 * few)] + [(count - k * few, few) for k in (4, 3, 2, 1)]
    copies = [
        pltpu.make_async_copy(maps_hbm.at[pl.ds(a, b)], maps_ref.at[pl.ds(a, b)], sems.at[k])
        for k, (a, b) in enumerate(cuts)
    ]
    for copy in copies:
        copy.start()
    position = pos_ref[0]
    group = position // size
    state = jnp.zeros((8, n), F32)
    for r in range(len(got), 0, -1):
        rows = got[r - 1].shape[0]
        if rows > 16:
            state = jnp.where(group > r, vm(state, got[r - 1][pl.ds(0, n), :]), 0.0)
        state += jnp.where(group >= r, rows8(got[r - 1][pl.ds(rows - 16, 16), :]), 0.0)
    first = jnp.where(position == 0, row(init_ref, 0), 0.0)
    state = vm(state, prefix_ref[...]) + before_ref[...] + first
    out_ref[pl.ds(steps - 1, 1), :] = (vm(state, total_ref[...]) + row(lefts_ref, steps - 1))[:1]
    starts, k = [state], 0
    for level in reversed(range(0, len(maps_at), 2)):
        if level == len(maps_at) - 2:
            copies[0].wait()
        if level == 0:
            for copy in copies[1:]:
                copy.wait()
        later = []
        for b, x in enumerate(starts):
            one = table_ref[levels_ref[0, 4 * b]] if level == 0 else left_ref[maps_at[level] + 2 * b]
            later += [
                x,
                vm(x, one) + row(lefts_ref, shifts_at[level] + 2 * b),
                vm(x, left_ref[maps_at[level + 1] + b]) + row(lefts_ref, shifts_at[level + 1] + b),
                vm(x, maps_ref[k]) + row(thirds_ref, k),
            ]
            k += 1
        starts = later
    for t in range(1, steps):
        out_ref[pl.ds(t - 1, 1), :] = starts[t][:1]


def shards(count, frames, levels, initial_state, transitions, gain, pixel_mode, pixel_weight):
    n = gain.shape[0]
    kinds = transitions.shape[0]
    pixels, length = frames.shape
    steps = length // count
    position = lax.axis_index("tm").astype(jnp.int32)[None]
    pairs = steps // 2 - 1
    dma = pltpu.SemaphoreType.DMA
    size = 1
    while count % (2 * size) == 0 and 4 * size * size <= count:
        size *= 2
    groups = count // size

    def swaps(x, step, times):
        x = x if isinstance(x, list) else [x] * (times - 1)
        return [
            lax.ppermute(a, "tm", [(j, j ^ (r * step)) for j in range(count)]) for a, r in zip(x, range(1, times))
        ]

    one_map = shape((n, 2 * n), BF16)
    table_shape = shape((kinds, n, 2 * n), BF16)
    cuts = 4
    turn = pixels % 128 == 0 and length % (128 * cuts) == 0
    small = [levels[None], initial_state[None], gain]
    if turn:
        small += [pixel_mode.reshape(count, pixels), pixel_weight.reshape(count, pixels)]
    given = [hbm(a) for a in [transitions] + small + [frames] * turn]
    outs = [table_shape] + [shape(a.shape, a.dtype) for a in small]
    buffers = [pltpu.VMEM(transitions.shape, F32)]
    if turn:
        outs += [shape((groups, steps, pixels), BF16)] * size
        buffers += [pltpu.VMEM(frames.shape, BF16), pltpu.VMEM((length, pixels), BF16)]
    table, levels, initial_state, gain, *rest = call(
        functools.partial(front_kernel, cuts, len(small), size), "front", 5,
        out_shape=outs,
        in_specs=[SMEM] + [HBM] * len(given),
        out_specs=[VMEM] * len(outs),
        scratch_shapes=buffers + [dma((cuts + 4 + len(small),))],
    )(position, *given)
    tree = pltpu.VMEM((pairs, n, 2 * n), BF16)
    maps = pltpu.HBM((pairs, n, 2 * n), BF16)
    left, right, total = call(
        functools.partial(tree_kernel, steps), "tree_of_maps", 8,
        out_shape=[maps, maps, one_map],
        in_specs=[SMEM, VMEM],
        out_specs=[HBM, HBM, VMEM],
        scratch_shapes=[tree, tree, dma((2 * steps.bit_length(),))],
    )(levels, table)

    if turn:
        mode, weight, slab, *slabs = rest
        first, *parts = call(
            functools.partial(project_kernel, size), "project", 4,
            out_shape=[shape((steps, n), F32)] * groups,
            in_specs=[SMEM] + [VMEM] * (3 + size),
            out_specs=[VMEM] * groups,
            scratch_shapes=[pltpu.VMEM((groups, steps, n), F32), pltpu.VMEM((count, pixels), F32)],
        )(position, total, mode, weight, slab, *swaps(slabs, 1, size))
        parts = [first] + swaps(parts, size, groups)
    else:
        x = lax.all_to_all(frames, "tm", split_axis=1, concat_axis=0, tiled=True)
        channels = jnp.arange(n, dtype=jnp.int32)
        projector = jnp.where(pixel_mode[None, :] == channels[:, None], pixel_weight[None, :], jnp.zeros((), BF16))
        parts = [lax.dot_general(x, projector, (((0,), (1,)), ((), ())), preferred_element_type=F32)]

    vector = shape((8, n), F32)

    members = swaps(total, 1, size)
    lefts, shift = call(
        local_kernel, "local_states", 8, 1 << 30,
        out_shape=[shape((steps, n), F32), vector],
        in_specs=[SMEM, SMEM] + [VMEM] * 4 + [HBM] + [VMEM] * len(parts),
        out_specs=[VMEM] * 2,
        scratch_shapes=[pltpu.VMEM((steps, n), F32), tree, dma((2,))],
    )(position, levels, gain, initial_state, total, table, hbm(right), *parts)
    prefix, before, mine, carried = call(
        functools.partial(group_kernel, size), "group_maps", 2,
        out_shape=[one_map, vector, shape((n + 16, 2 * n), BF16), shape((16, 2 * n), BF16)],
        in_specs=[SMEM] + [VMEM] * (2 * size),
        out_specs=[VMEM] * 4,
        scratch_shapes=[pltpu.VMEM((size, n, 2 * n), BF16), pltpu.VMEM((size, 8, n), F32)],
    )(position, total, *members, shift, *swaps(shift, 1, size))
    got = [
        lax.ppermute(mine if r < groups - 1 else carried, "tm", [(j, (j + r * size) % count) for j in range(count)])
        for r in range(1, groups)
    ]

    nodes = (steps - 1) // 3
    thirds_maps, thirds = call(
        third_kernel, "third_children", 6,
        out_shape=[pltpu.HBM((nodes, n, 2 * n), BF16), shape((nodes, n), F32)],
        in_specs=[SMEM, VMEM, VMEM, HBM],
        out_specs=[HBM, VMEM],
        scratch_shapes=[tree, pltpu.VMEM((nodes, n, 2 * n), BF16), dma((2,))],
    )(levels, table, lefts, hbm(left))
    return call(
        functools.partial(final_kernel, size), "estimates", 8,
        out_shape=shape((steps, n), F32),
        in_specs=[SMEM, SMEM] + [VMEM] * 8 + [HBM] + [VMEM] * len(got),
        out_specs=VMEM,
        scratch_shapes=[pltpu.VMEM((nodes, n, 2 * n), BF16), dma((5,))],
    )(position, levels, initial_state, prefix, before, total, lefts, left, table, thirds, hbm(thirds_maps), *got)


def solution(mesh):
    in_specs = (P("tm", "parts"), P(("parts", "tm")), P("parts"), P(), P(), P(), P())
    out_specs = P(("parts", "tm"), None)
    return jax.shard_map(
        functools.partial(shards, mesh.shape["tm"]),
        mesh=mesh,
        in_specs=in_specs,
        out_specs=out_specs,
        check_vma=False,
    )
```

```python
import functools

import jax
import jax.numpy as jnp
from jax import lax
from jax.experimental import pallas as pl
from jax.experimental.pallas import tpu as pltpu
from jax.sharding import PartitionSpec as P

F32 = jnp.float32
BF16 = jnp.bfloat16
MIB = 1 << 20
NT = (((1,), (1,)), ((), ()))
VMEM = pl.BlockSpec(memory_space=pltpu.VMEM)
SMEM = pl.BlockSpec(memory_space=pltpu.SMEM)
HBM = pl.BlockSpec(memory_space=pltpu.HBM)
shape = jax.ShapeDtypeStruct


def hbm(x):
    return pltpu.with_memory_space_constraint(x, pltpu.HBM)


def call(kernel, name, mib, flops=1, **kw):
    return pl.pallas_call(
        kernel,
        name=name,
        compiler_params=pltpu.CompilerParams(vmem_limit_bytes=mib * MIB),
        cost_estimate=pl.CostEstimate(flops=flops, bytes_accessed=1, transcendentals=0),
        **kw,
    )


def pair(x):
    high = x.astype(BF16)
    mid = (x - high.astype(F32)).astype(BF16)
    return jnp.concatenate([high, mid], axis=1)


def mm(left, right):
    n = right.shape[0]
    out = jnp.dot(left, jnp.concatenate([right, right], axis=0), preferred_element_type=F32)
    return out[:, :n] + out[:, n:]


def vm(vec, mat):
    high = vec.astype(BF16).astype(F32)
    rows = jnp.concatenate([high, vec - high], axis=0).astype(BF16)
    out = jnp.dot(rows, mat, preferred_element_type=F32)
    n = vec.shape[1]
    out = out[:, :n] + out[:, n:]
    return out[:8] + out[8:]


def row(ref, t):
    return jnp.broadcast_to(ref[pl.ds(t, 1), :], (8, ref.shape[1]))


def front_kernel(cuts, extra, size, pos_ref, trans_ref, *refs):
    given, refs = refs[:extra], refs[extra:]
    turn = len(refs) > extra + 3
    if turn:
        frames_ref, table_ref, *moved = refs[: 2 + extra]
        slabs = refs[2 + extra : 2 + extra + size]
        trans, frames, turned, sems = refs[2 + extra + size :]
        width = frames.shape[1] // cuts
        parts = [pl.ds(k * width, width) for k in range(cuts)]
        ins = [
            pltpu.make_async_copy(frames_ref.at[:, part], frames.at[:, part], sems.at[k])
            for k, part in enumerate(parts)
        ]
        for copy in ins:
            copy.start()
    else:
        table_ref, *moved, trans, sems = refs
    kinds = trans.shape[0]
    few = kinds // 4
    maps = [
        pltpu.make_async_copy(trans_ref.at[pl.ds(k * few, few)], trans.at[pl.ds(k * few, few)], sems.at[cuts + k])
        for k in range(4)
    ]
    moves = [pltpu.make_async_copy(a, b, sems.at[cuts + 4 + k]) for k, (a, b) in enumerate(zip(given, moved))]
    for copy in maps + moves:
        copy.start()
    if turn:
        for k in range(cuts):
            ins[k].wait()
            turned[parts[k], :] = frames[:, parts[k]].T
        member = pos_ref[0] % size
        groups, steps, _ = slabs[0].shape
        for r in range(size):
            for g in range(groups):
                start = pl.multiple_of((g * size + (member ^ r)) * steps, steps)
                slabs[r][g] = turned[pl.ds(start, steps), :]
    for k in range(4):
        maps[k].wait()
        for q in range(k * few, (k + 1) * few):
            table_ref[q] = pair(trans[q].T)
    for copy in moves:
        copy.wait()


def project_kernel(size, pos_ref, after_ref, mode_ref, weight_ref, *refs):
    slabs, outs, (sums, weights) = refs[:size], refs[size:-2], refs[-2:]
    weights[...] = weight_ref[...].astype(F32)
    groups, steps, width = slabs[0].shape
    n = sums.shape[2]
    position = pos_ref[0]
    channel = lax.broadcasted_iota(jnp.int32, (n, width), 0)
    total = jnp.zeros((groups * steps, n), F32)
    for r in range(size):
        here = pl.ds(position ^ r, 1)
        weight = jnp.broadcast_to(weights[here, :], (n, width))
        projector = jnp.where(mode_ref[here, :] == channel, weight, 0.0).astype(BF16)
        total += lax.dot_general(slabs[r][...].reshape(groups * steps, width), projector, NT, preferred_element_type=F32)
    sums[...] = total.reshape(groups, steps, n)
    for r in range(groups):
        outs[r][...] = sums[(position // size) ^ r]


def tree_kernel(steps, levels_ref, table_ref, left_hbm, right_hbm, total_ref, left_ref, right_ref, sems):
    base = steps // 4

    def first(t):
        return mm(table_ref[levels_ref[0, t]], table_ref[levels_ref[0, t + 1]])

    def node(k):
        return mm(left_ref[k], right_ref[k])

    def first_pairs(ks):
        made = [(first(4 * k), first(4 * k + 2)) for k in ks]
        for k, (a, b) in zip(ks, made):
            left_ref[k] = pair(a)
            right_ref[k] = pair(b)

    def later_pairs(ks):
        made = [(node(2 * (k - base)), node(2 * (k - base) + 1)) for k in ks]
        for k, (a, b) in zip(ks, made):
            left_ref[k] = pair(a)
            right_ref[k] = pair(b)

    def run(fn, start, count):
        if count <= 8:
            fn(list(range(start, start + count)))
            return

        def body(i, c):
            fn([start + 8 * i + k for k in range(8)])
            return c

        lax.fori_loop(0, count // 8, body, 0)

    copies = []

    def store(start, count):
        for ref, hbm in ((right_ref, right_hbm), (left_ref, left_hbm)):
            part = pl.ds(start, count)
            copies.append(pltpu.make_async_copy(ref.at[part], hbm.at[part], sems.at[len(copies)]))
            copies[-1].start()

    run(first_pairs, 0, base)
    store(0, base)
    run(later_pairs, base, base // 2)
    store(base, base // 2)
    count, start = base // 4, base + base // 2
    while count >= 1:
        run(later_pairs, start, count)
        store(start, count)
        start += count
        count //= 2
    total_ref[...] = pair(node(start - 1))
    for copy in copies:
        copy.wait()


def local_kernel(pos_ref, levels_ref, gain_ref, init_ref, total_ref, table_ref, right_hbm, *refs):
    parts, (lefts_ref, shift_ref, drive_ref, right_ref, sems) = refs[:-5], refs[-5:]
    steps, n = drive_ref.shape
    base = steps // 4
    copies = [
        pltpu.make_async_copy(right_hbm.at[pl.ds(0, base)], right_ref.at[pl.ds(0, base)], sems.at[0]),
        pltpu.make_async_copy(right_hbm.at[pl.ds(base, base - 1)], right_ref.at[pl.ds(base, base - 1)], sems.at[1]),
    ]
    for copy in copies:
        copy.start()
    measured = parts[0][...]
    for part in parts[1:]:
        measured += part[...]
    drive_ref[...] = lax.dot_general(measured.astype(BF16), gain_ref[...], NT, preferred_element_type=F32)

    states = [row(drive_ref, t) for t in range(steps)]
    at, offset = 0, 0
    for level in range(steps.bit_length() - 1):
        if level in (1, 2):
            copies[level - 1].wait()
        later = []
        for i in range(len(states) // 2):
            mat = table_ref[levels_ref[0, 2 * i + 1]] if level == 0 else right_ref[offset + i]
            lefts_ref[pl.ds(at + i, 1), :] = states[2 * i][:1]
            later.append(vm(states[2 * i], mat) + states[2 * i + 1])
        at += len(later)
        if level > 0:
            offset += len(later)
        states = later
    lefts_ref[pl.ds(at, 1), :] = states[0][:1]
    first = jnp.where(pos_ref[0] == 0, row(init_ref, 0), 0.0)
    shift_ref[...] = states[0] + vm(first, total_ref[...])


def rows16(vec):
    high = vec.astype(BF16).astype(F32)
    both = jnp.concatenate([high, vec - high], axis=1)
    return jnp.concatenate([both, both], axis=0).astype(BF16)


def rows8(rows):
    both = rows.astype(F32)
    n = rows.shape[1] // 2
    return both[:8, :n] + both[:8, n:]


def group_kernel(size, pos_ref, *refs):
    maps, shifts = refs[:size], refs[size : 2 * size]
    prefix_ref, before_ref, mine_ref, shift_ref, map_ref, held_ref = refs[2 * size :]
    n = prefix_ref.shape[0]
    member = pos_ref[0] % size
    for r in range(size):
        map_ref[member ^ r] = maps[r][...]
        held_ref[member ^ r] = shifts[r][...]
    rows, cols = (lax.broadcasted_iota(jnp.int32, (n, n), d) for d in (0, 1))
    prefix, before = pair((rows == cols).astype(F32)), jnp.zeros((8, n), F32)
    run, vec = map_ref[0], held_ref[0]
    for q in range(1, size):
        here = member == q
        prefix, before = jnp.where(here, run, prefix), jnp.where(here, vec, before)
        vec = vm(vec, map_ref[q]) + held_ref[q]
        run = pair(mm(run, map_ref[q]))
    prefix_ref[...] = prefix
    before_ref[...] = before
    mine_ref[pl.ds(0, n), :] = run
    mine_ref[pl.ds(n, 16), :] = rows16(vec)
    shift_ref[...] = rows16(vec)


def final_kernel(size, pos_ref, levels_ref, init_ref, prefix_ref, before_ref, total_ref, lefts_ref, left_ref, table_ref, *refs):
    got, out_ref = refs[:-1], refs[-1]
    steps, n = lefts_ref.shape
    position = pos_ref[0]
    group = position // size
    state = jnp.zeros((8, n), F32)
    for r in range(len(got), 0, -1):
        rows = got[r - 1].shape[0]
        if rows > 16:
            state = jnp.where(group > r, vm(state, got[r - 1][pl.ds(0, n), :]), 0.0)
        state += jnp.where(group >= r, rows8(got[r - 1][pl.ds(rows - 16, 16), :]), 0.0)
    first = jnp.where(position == 0, row(init_ref, 0), 0.0)
    state = vm(state, prefix_ref[...]) + before_ref[...] + first
    out_ref[pl.ds(steps - 1, 1), :] = (vm(state, total_ref[...]) + row(lefts_ref, steps - 1))[:1]
    levels = steps.bit_length() - 1
    starts = [state]
    sizes = [steps >> (level + 1) for level in range(levels)]
    for level in reversed(range(levels)):
        at, offset = sum(sizes[:level]), sum(sizes[1:level])
        later = []
        for i, x in enumerate(starts):
            mat = table_ref[levels_ref[0, 2 * i]] if level == 0 else left_ref[offset + i]
            later += [x, vm(x, mat) + row(lefts_ref, at + i)]
        starts = later
    for t in range(1, steps):
        out_ref[pl.ds(t - 1, 1), :] = starts[t][:1]


def shards(count, frames, levels, initial_state, transitions, gain, pixel_mode, pixel_weight):
    n = gain.shape[0]
    kinds = transitions.shape[0]
    pixels, length = frames.shape
    steps = length // count
    position = lax.axis_index("tm").astype(jnp.int32)[None]
    pairs = steps // 2 - 1
    dma = pltpu.SemaphoreType.DMA
    size = 1
    while count % (2 * size) == 0 and 4 * size * size <= count:
        size *= 2
    groups = count // size

    def swaps(x, step, times):
        x = x if isinstance(x, list) else [x] * (times - 1)
        return [
            lax.ppermute(a, "tm", [(j, j ^ (r * step)) for j in range(count)]) for a, r in zip(x, range(1, times))
        ]

    one_map = shape((n, 2 * n), BF16)
    table_shape = shape((kinds, n, 2 * n), BF16)
    cuts = 4
    turn = pixels % 128 == 0 and length % (128 * cuts) == 0
    small = [levels[None], initial_state[None], gain]
    if turn:
        small += [pixel_mode.reshape(count, pixels), pixel_weight.reshape(count, pixels)]
    given = [hbm(a) for a in [transitions] + small + [frames] * turn]
    outs = [table_shape] + [shape(a.shape, a.dtype) for a in small]
    buffers = [pltpu.VMEM(transitions.shape, F32)]
    if turn:
        outs += [shape((groups, steps, pixels), BF16)] * size
        buffers += [pltpu.VMEM(frames.shape, BF16), pltpu.VMEM((length, pixels), BF16)]
    table, levels, initial_state, gain, *rest = call(
        functools.partial(front_kernel, cuts, len(small), size), "front", 5,
        out_shape=outs,
        in_specs=[SMEM] + [HBM] * len(given),
        out_specs=[VMEM] * len(outs),
        scratch_shapes=buffers + [dma((cuts + 4 + len(small),))],
    )(position, *given)
    tree = pltpu.VMEM((pairs, n, 2 * n), BF16)
    maps = pltpu.HBM((pairs, n, 2 * n), BF16)
    left, right, total = call(
        functools.partial(tree_kernel, steps), "tree_of_maps", 8,
        out_shape=[maps, maps, one_map],
        in_specs=[SMEM, VMEM],
        out_specs=[HBM, HBM, VMEM],
        scratch_shapes=[tree, tree, dma((2 * steps.bit_length(),))],
    )(levels, table)

    if turn:
        mode, weight, slab, *slabs = rest
        first, *parts = call(
            functools.partial(project_kernel, size), "project", 4,
            out_shape=[shape((steps, n), F32)] * groups,
            in_specs=[SMEM] + [VMEM] * (3 + size),
            out_specs=[VMEM] * groups,
            scratch_shapes=[pltpu.VMEM((groups, steps, n), F32), pltpu.VMEM((count, pixels), F32)],
        )(position, total, mode, weight, slab, *swaps(slabs, 1, size))
        parts = [first] + swaps(parts, size, groups)
    else:
        x = lax.all_to_all(frames, "tm", split_axis=1, concat_axis=0, tiled=True)
        channels = jnp.arange(n, dtype=jnp.int32)
        projector = jnp.where(pixel_mode[None, :] == channels[:, None], pixel_weight[None, :], jnp.zeros((), BF16))
        parts = [lax.dot_general(x, projector, (((0,), (1,)), ((), ())), preferred_element_type=F32)]

    vector = shape((8, n), F32)

    members = swaps(total, 1, size)
    lefts, shift = call(
        local_kernel, "local_states", 8, 1 << 30,
        out_shape=[shape((steps, n), F32), vector],
        in_specs=[SMEM, SMEM] + [VMEM] * 4 + [HBM] + [VMEM] * len(parts),
        out_specs=[VMEM] * 2,
        scratch_shapes=[pltpu.VMEM((steps, n), F32), tree, dma((2,))],
    )(position, levels, gain, initial_state, total, table, hbm(right), *parts)
    prefix, before, mine, carried = call(
        functools.partial(group_kernel, size), "group_maps", 2,
        out_shape=[one_map, vector, shape((n + 16, 2 * n), BF16), shape((16, 2 * n), BF16)],
        in_specs=[SMEM] + [VMEM] * (2 * size),
        out_specs=[VMEM] * 4,
        scratch_shapes=[pltpu.VMEM((size, n, 2 * n), BF16), pltpu.VMEM((size, 8, n), F32)],
    )(position, total, *members, shift, *swaps(shift, 1, size))
    got = [
        lax.ppermute(mine if r < groups - 1 else carried, "tm", [(j, (j + r * size) % count) for j in range(count)])
        for r in range(1, groups)
    ]

    return call(
        functools.partial(final_kernel, size), "estimates", 6,
        out_shape=shape((steps, n), F32),
        in_specs=[SMEM, SMEM] + [VMEM] * (7 + len(got)),
        out_specs=VMEM,
    )(position, levels, initial_state, prefix, before, total, lefts, left, table, *got)


def solution(mesh):
    in_specs = (P("tm", "parts"), P(("parts", "tm")), P("parts"), P(), P(), P(), P())
    out_specs = P(("parts", "tm"), None)
    return jax.shard_map(
        functools.partial(shards, mesh.shape["tm"]),
        mesh=mesh,
        in_specs=in_specs,
        out_specs=out_specs,
        check_vma=False,
    )
```

```python
import functools

import jax
import jax.numpy as jnp
from jax import lax
from jax.experimental import pallas as pl
from jax.experimental.pallas import tpu as pltpu
from jax.sharding import PartitionSpec as P

F32 = jnp.float32
BF16 = jnp.bfloat16
MIB = 1 << 20
NT = (((1,), (1,)), ((), ()))
VMEM = pl.BlockSpec(memory_space=pltpu.VMEM)
SMEM = pl.BlockSpec(memory_space=pltpu.SMEM)
HBM = pl.BlockSpec(memory_space=pltpu.HBM)
shape = jax.ShapeDtypeStruct


def hbm(x):
    return pltpu.with_memory_space_constraint(x, pltpu.HBM)


def call(kernel, name, mib, flops=1, **kw):
    return pl.pallas_call(
        kernel,
        name=name,
        compiler_params=pltpu.CompilerParams(vmem_limit_bytes=mib * MIB),
        cost_estimate=pl.CostEstimate(flops=flops, bytes_accessed=1, transcendentals=0),
        **kw,
    )


def pair(x):
    high = x.astype(BF16)
    mid = (x - high.astype(F32)).astype(BF16)
    return jnp.concatenate([high, mid], axis=1)


def mm(left, right):
    n = right.shape[0]
    out = jnp.dot(left, jnp.concatenate([right, right], axis=0), preferred_element_type=F32)
    return out[:, :n] + out[:, n:]


def vm(vec, mat):
    high = vec.astype(BF16).astype(F32)
    rows = jnp.concatenate([high, vec - high], axis=0).astype(BF16)
    out = jnp.dot(rows, mat, preferred_element_type=F32)
    n = vec.shape[1]
    out = out[:, :n] + out[:, n:]
    return out[:8] + out[8:]


def row(ref, t):
    return jnp.broadcast_to(ref[pl.ds(t, 1), :], (8, ref.shape[1]))


def front_kernel(cuts, extra, size, pos_ref, trans_ref, *refs):
    given, refs = refs[:extra], refs[extra:]
    turn = len(refs) > extra + 3
    if turn:
        frames_ref, table_ref, *moved = refs[: 2 + extra]
        slabs = refs[2 + extra : 2 + extra + size]
        trans, frames, turned, sems = refs[2 + extra + size :]
        width = frames.shape[1] // cuts
        parts = [pl.ds(k * width, width) for k in range(cuts)]
        ins = [
            pltpu.make_async_copy(frames_ref.at[:, part], frames.at[:, part], sems.at[k])
            for k, part in enumerate(parts)
        ]
        for copy in ins:
            copy.start()
    else:
        table_ref, *moved, trans, sems = refs
    kinds = trans.shape[0]
    few = kinds // 4
    maps = [
        pltpu.make_async_copy(trans_ref.at[pl.ds(k * few, few)], trans.at[pl.ds(k * few, few)], sems.at[cuts + k])
        for k in range(4)
    ]
    moves = [pltpu.make_async_copy(a, b, sems.at[cuts + 4 + k]) for k, (a, b) in enumerate(zip(given, moved))]
    for copy in maps + moves:
        copy.start()
    if turn:
        for k in range(cuts):
            ins[k].wait()
            turned[parts[k], :] = frames[:, parts[k]].T
        member = pos_ref[0] % size
        groups, steps, _ = slabs[0].shape
        for r in range(size):
            for g in range(groups):
                start = pl.multiple_of((g * size + (member ^ r)) * steps, steps)
                slabs[r][g] = turned[pl.ds(start, steps), :]
    for k in range(4):
        maps[k].wait()
        for q in range(k * few, (k + 1) * few):
            table_ref[q] = pair(trans[q].T)
    for copy in moves:
        copy.wait()


def project_kernel(size, pos_ref, after_ref, mode_ref, weight_ref, *refs):
    slabs, outs, (sums, weights) = refs[:size], refs[size:-2], refs[-2:]
    weights[...] = weight_ref[...].astype(F32)
    groups, steps, width = slabs[0].shape
    n = sums.shape[2]
    position = pos_ref[0]
    channel = lax.broadcasted_iota(jnp.int32, (n, width), 0)
    total = jnp.zeros((groups * steps, n), F32)
    for r in range(size):
        here = pl.ds(position ^ r, 1)
        weight = jnp.broadcast_to(weights[here, :], (n, width))
        projector = jnp.where(mode_ref[here, :] == channel, weight, 0.0).astype(BF16)
        total += lax.dot_general(slabs[r][...].reshape(groups * steps, width), projector, NT, preferred_element_type=F32)
    sums[...] = total.reshape(groups, steps, n)
    for r in range(groups):
        outs[r][...] = sums[(position // size) ^ r]


def tree_kernel(steps, levels_ref, table_ref, left_hbm, right_hbm, total_ref, left_ref, right_ref, sems):
    base = steps // 4

    def first(t):
        return mm(table_ref[levels_ref[0, t]], table_ref[levels_ref[0, t + 1]])

    def node(k):
        return mm(left_ref[k], right_ref[k])

    def first_pairs(ks):
        made = [(first(4 * k), first(4 * k + 2)) for k in ks]
        for k, (a, b) in zip(ks, made):
            left_ref[k] = pair(a)
            right_ref[k] = pair(b)

    def later_pairs(ks):
        made = [(node(2 * (k - base)), node(2 * (k - base) + 1)) for k in ks]
        for k, (a, b) in zip(ks, made):
            left_ref[k] = pair(a)
            right_ref[k] = pair(b)

    def run(fn, start, count):
        if count <= 8:
            fn(list(range(start, start + count)))
            return

        def body(i, c):
            fn([start + 8 * i + k for k in range(8)])
            return c

        lax.fori_loop(0, count // 8, body, 0)

    copies = []

    def store(start, count):
        for ref, hbm in ((right_ref, right_hbm), (left_ref, left_hbm)):
            part = pl.ds(start, count)
            copies.append(pltpu.make_async_copy(ref.at[part], hbm.at[part], sems.at[len(copies)]))
            copies[-1].start()

    run(first_pairs, 0, base)
    store(0, base)
    run(later_pairs, base, base // 2)
    store(base, base // 2)
    count, start = base // 4, base + base // 2
    while count >= 1:
        run(later_pairs, start, count)
        store(start, count)
        start += count
        count //= 2
    total_ref[...] = pair(node(start - 1))
    for copy in copies:
        copy.wait()


def local_kernel(pos_ref, levels_ref, gain_ref, init_ref, total_ref, table_ref, right_hbm, *refs):
    parts, (lefts_ref, shift_ref, drive_ref, right_ref, sems) = refs[:-5], refs[-5:]
    steps, n = drive_ref.shape
    base = steps // 4
    copies = [
        pltpu.make_async_copy(right_hbm.at[pl.ds(0, base)], right_ref.at[pl.ds(0, base)], sems.at[0]),
        pltpu.make_async_copy(right_hbm.at[pl.ds(base, base - 1)], right_ref.at[pl.ds(base, base - 1)], sems.at[1]),
    ]
    for copy in copies:
        copy.start()
    measured = parts[0][...]
    for part in parts[1:]:
        measured += part[...]
    drive_ref[...] = lax.dot_general(measured.astype(BF16), gain_ref[...], NT, preferred_element_type=F32)

    states = [row(drive_ref, t) for t in range(steps)]
    at, offset = 0, 0
    for level in range(steps.bit_length() - 1):
        if level in (1, 2):
            copies[level - 1].wait()
        later = []
        for i in range(len(states) // 2):
            mat = table_ref[levels_ref[0, 2 * i + 1]] if level == 0 else right_ref[offset + i]
            lefts_ref[pl.ds(at + i, 1), :] = states[2 * i][:1]
            later.append(vm(states[2 * i], mat) + states[2 * i + 1])
        at += len(later)
        if level > 0:
            offset += len(later)
        states = later
    lefts_ref[pl.ds(at, 1), :] = states[0][:1]
    first = jnp.where(pos_ref[0] == 0, row(init_ref, 0), 0.0)
    shift_ref[...] = states[0] + vm(first, total_ref[...])


def rows16(vec):
    high = vec.astype(BF16).astype(F32)
    both = jnp.concatenate([high, vec - high], axis=1)
    return jnp.concatenate([both, both], axis=0).astype(BF16)


def rows8(rows):
    both = rows.astype(F32)
    n = rows.shape[1] // 2
    return both[:8, :n] + both[:8, n:]


def group_kernel(size, pos_ref, *refs):
    maps, shifts = refs[:size], refs[size : 2 * size]
    prefix_ref, before_ref, mine_ref, shift_ref, map_ref, held_ref = refs[2 * size :]
    n = prefix_ref.shape[0]
    member = pos_ref[0] % size
    for r in range(size):
        map_ref[member ^ r] = maps[r][...]
        held_ref[member ^ r] = shifts[r][...]
    rows, cols = (lax.broadcasted_iota(jnp.int32, (n, n), d) for d in (0, 1))
    prefix, before = pair((rows == cols).astype(F32)), jnp.zeros((8, n), F32)
    run, vec = map_ref[0], held_ref[0]
    for q in range(1, size):
        here = member == q
        prefix, before = jnp.where(here, run, prefix), jnp.where(here, vec, before)
        vec = vm(vec, map_ref[q]) + held_ref[q]
        run = pair(mm(run, map_ref[q]))
    prefix_ref[...] = prefix
    before_ref[...] = before
    mine_ref[pl.ds(0, n), :] = run
    mine_ref[pl.ds(n, 16), :] = rows16(vec)
    shift_ref[...] = rows16(vec)


def final_kernel(size, pos_ref, levels_ref, init_ref, prefix_ref, before_ref, total_ref, lefts_ref, left_ref, table_ref, *refs):
    got, out_ref = refs[:-1], refs[-1]
    steps, n = lefts_ref.shape
    position = pos_ref[0]
    group = position // size
    state = jnp.zeros((8, n), F32)
    for r in range(len(got), 0, -1):
        rows = got[r - 1].shape[0]
        if rows > 16:
            state = jnp.where(group > r, vm(state, got[r - 1][pl.ds(0, n), :]), 0.0)
        state += jnp.where(group >= r, rows8(got[r - 1][pl.ds(rows - 16, 16), :]), 0.0)
    first = jnp.where(position == 0, row(init_ref, 0), 0.0)
    state = vm(state, prefix_ref[...]) + before_ref[...] + first
    out_ref[pl.ds(steps - 1, 1), :] = (vm(state, total_ref[...]) + row(lefts_ref, steps - 1))[:1]
    levels = steps.bit_length() - 1
    starts = [state]
    sizes = [steps >> (level + 1) for level in range(levels)]
    for level in reversed(range(levels)):
        at, offset = sum(sizes[:level]), sum(sizes[1:level])
        later = []
        for i, x in enumerate(starts):
            mat = table_ref[levels_ref[0, 2 * i]] if level == 0 else left_ref[offset + i]
            later += [x, vm(x, mat) + row(lefts_ref, at + i)]
        starts = later
    for t in range(1, steps):
        out_ref[pl.ds(t - 1, 1), :] = starts[t][:1]


def shards(count, frames, levels, initial_state, transitions, gain, pixel_mode, pixel_weight):
    n = gain.shape[0]
    kinds = transitions.shape[0]
    pixels, length = frames.shape
    steps = length // count
    position = lax.axis_index("tm").astype(jnp.int32)[None]
    pairs = steps // 2 - 1
    dma = pltpu.SemaphoreType.DMA
    size = 1
    while count % (2 * size) == 0 and 4 * size * size <= count:
        size *= 2
    groups = count // size

    def swaps(x, step, times):
        x = x if isinstance(x, list) else [x] * (times - 1)
        return [
            lax.ppermute(a, "tm", [(j, j ^ (r * step)) for j in range(count)]) for a, r in zip(x, range(1, times))
        ]

    one_map = shape((n, 2 * n), BF16)
    table_shape = shape((kinds, n, 2 * n), BF16)
    cuts = 4
    turn = pixels % 128 == 0 and length % (128 * cuts) == 0
    small = [levels[None], initial_state[None], gain]
    if turn:
        small += [pixel_mode.reshape(count, pixels), pixel_weight.reshape(count, pixels)]
    given = [hbm(a) for a in [transitions] + small + [frames] * turn]
    outs = [table_shape] + [shape(a.shape, a.dtype) for a in small]
    buffers = [pltpu.VMEM(transitions.shape, F32)]
    if turn:
        outs += [shape((groups, steps, pixels), BF16)] * size
        buffers += [pltpu.VMEM(frames.shape, BF16), pltpu.VMEM((length, pixels), BF16)]
    table, levels, initial_state, gain, *rest = call(
        functools.partial(front_kernel, cuts, len(small), size), "front", 5,
        out_shape=outs,
        in_specs=[SMEM] + [HBM] * len(given),
        out_specs=[VMEM] * len(outs),
        scratch_shapes=buffers + [dma((cuts + 4 + len(small),))],
    )(position, *given)
    tree = pltpu.VMEM((pairs, n, 2 * n), BF16)
    maps = pltpu.HBM((pairs, n, 2 * n), BF16)
    left, right, total = call(
        functools.partial(tree_kernel, steps), "tree_of_maps", 8,
        out_shape=[maps, maps, one_map],
        in_specs=[SMEM, VMEM],
        out_specs=[HBM, HBM, VMEM],
        scratch_shapes=[tree, tree, dma((2 * steps.bit_length(),))],
    )(levels, table)

    if turn:
        mode, weight, slab, *slabs = rest
        first, *parts = call(
            functools.partial(project_kernel, size), "project", 4,
            out_shape=[shape((steps, n), F32)] * groups,
            in_specs=[SMEM] + [VMEM] * (3 + size),
            out_specs=[VMEM] * groups,
            scratch_shapes=[pltpu.VMEM((groups, steps, n), F32), pltpu.VMEM((count, pixels), F32)],
        )(position, total, mode, weight, slab, *swaps(slabs, 1, size))
        parts = [first] + swaps(parts, size, groups)[::-1]
    else:
        x = lax.all_to_all(frames, "tm", split_axis=1, concat_axis=0, tiled=True)
        channels = jnp.arange(n, dtype=jnp.int32)
        projector = jnp.where(pixel_mode[None, :] == channels[:, None], pixel_weight[None, :], jnp.zeros((), BF16))
        parts = [lax.dot_general(x, projector, (((0,), (1,)), ((), ())), preferred_element_type=F32)]

    vector = shape((8, n), F32)

    members = swaps(total, 1, size)
    lefts, shift = call(
        local_kernel, "local_states", 8, 1 << 30,
        out_shape=[shape((steps, n), F32), vector],
        in_specs=[SMEM, SMEM] + [VMEM] * 4 + [HBM] + [VMEM] * len(parts),
        out_specs=[VMEM] * 2,
        scratch_shapes=[pltpu.VMEM((steps, n), F32), tree, dma((2,))],
    )(position, levels, gain, initial_state, total, table, hbm(right), *parts)
    prefix, before, mine, carried = call(
        functools.partial(group_kernel, size), "group_maps", 2,
        out_shape=[one_map, vector, shape((n + 16, 2 * n), BF16), shape((16, 2 * n), BF16)],
        in_specs=[SMEM] + [VMEM] * (2 * size),
        out_specs=[VMEM] * 4,
        scratch_shapes=[pltpu.VMEM((size, n, 2 * n), BF16), pltpu.VMEM((size, 8, n), F32)],
    )(position, total, *members, shift, *swaps(shift, 1, size))
    got = [
        lax.ppermute(mine if r < groups - 1 else carried, "tm", [(j, (j + r * size) % count) for j in range(count)])
        for r in range(1, groups)
    ]

    return call(
        functools.partial(final_kernel, size), "estimates", 6,
        out_shape=shape((steps, n), F32),
        in_specs=[SMEM, SMEM] + [VMEM] * (7 + len(got)),
        out_specs=VMEM,
    )(position, levels, initial_state, prefix, before, total, lefts, left, table, *got)


def solution(mesh):
    in_specs = (P("tm", "parts"), P(("parts", "tm")), P("parts"), P(), P(), P(), P())
    out_specs = P(("parts", "tm"), None)
    return jax.shard_map(
        functools.partial(shards, mesh.shape["tm"]),
        mesh=mesh,
        in_specs=in_specs,
        out_specs=out_specs,
        check_vma=False,
    )
```

```python
import functools

import jax
import jax.numpy as jnp
from jax import lax
from jax.experimental import pallas as pl
from jax.experimental.pallas import tpu as pltpu
from jax.sharding import PartitionSpec as P

F32 = jnp.float32
BF16 = jnp.bfloat16
MIB = 1 << 20
NT = (((1,), (1,)), ((), ()))
VMEM = pl.BlockSpec(memory_space=pltpu.VMEM)
SMEM = pl.BlockSpec(memory_space=pltpu.SMEM)
HBM = pl.BlockSpec(memory_space=pltpu.HBM)
shape = jax.ShapeDtypeStruct


def hbm(x):
    return pltpu.with_memory_space_constraint(x, pltpu.HBM)


def call(kernel, name, mib, flops=1, **kw):
    return pl.pallas_call(
        kernel,
        name=name,
        compiler_params=pltpu.CompilerParams(vmem_limit_bytes=mib * MIB),
        cost_estimate=pl.CostEstimate(flops=flops, bytes_accessed=1, transcendentals=0),
        **kw,
    )


def pair(x):
    high = x.astype(BF16)
    mid = (x - high.astype(F32)).astype(BF16)
    return jnp.concatenate([high, mid], axis=1)


def mm(left, right):
    n = right.shape[0]
    out = jnp.dot(left, jnp.concatenate([right, right], axis=0), preferred_element_type=F32)
    return out[:, :n] + out[:, n:]


def vm(vec, mat):
    high = vec.astype(BF16).astype(F32)
    rows = jnp.concatenate([high, vec - high], axis=0).astype(BF16)
    out = jnp.dot(rows, mat, preferred_element_type=F32)
    n = vec.shape[1]
    out = out[:, :n] + out[:, n:]
    return out[:8] + out[8:]


def row(ref, t):
    return jnp.broadcast_to(ref[pl.ds(t, 1), :], (8, ref.shape[1]))


def front_kernel(cuts, extra, size, pos_ref, trans_ref, *refs):
    given, refs = refs[:extra], refs[extra:]
    turn = len(refs) > extra + 3
    if turn:
        frames_ref, table_ref, *moved = refs[: 2 + extra]
        slabs = refs[2 + extra : 2 + extra + size]
        trans, frames, turned, sems = refs[2 + extra + size :]
        width = frames.shape[1] // cuts
        parts = [pl.ds(k * width, width) for k in range(cuts)]
        ins = [
            pltpu.make_async_copy(frames_ref.at[:, part], frames.at[:, part], sems.at[k])
            for k, part in enumerate(parts)
        ]
        for copy in ins:
            copy.start()
    else:
        table_ref, *moved, trans, sems = refs
    kinds = trans.shape[0]
    few = kinds // 4
    maps = [
        pltpu.make_async_copy(trans_ref.at[pl.ds(k * few, few)], trans.at[pl.ds(k * few, few)], sems.at[cuts + k])
        for k in range(4)
    ]
    moves = [pltpu.make_async_copy(a, b, sems.at[cuts + 4 + k]) for k, (a, b) in enumerate(zip(given, moved))]
    for copy in maps + moves:
        copy.start()
    if turn:
        for k in range(cuts):
            ins[k].wait()
            turned[parts[k], :] = frames[:, parts[k]].T
        member = pos_ref[0] % size
        groups, steps, _ = slabs[0].shape
        for r in range(size):
            for g in range(groups):
                start = pl.multiple_of((g * size + (member ^ r)) * steps, steps)
                slabs[r][g] = turned[pl.ds(start, steps), :]
    for k in range(4):
        maps[k].wait()
        for q in range(k * few, (k + 1) * few):
            table_ref[q] = pair(trans[q].T)
    for copy in moves:
        copy.wait()


def project_kernel(size, pos_ref, after_ref, mode_ref, weight_ref, *refs):
    slabs, outs, (sums, weights) = refs[:size], refs[size:-2], refs[-2:]
    slabs = slabs[:1] + slabs[:0:-1]
    weights[...] = weight_ref[...].astype(F32)
    groups, steps, width = slabs[0].shape
    n = sums.shape[2]
    position = pos_ref[0]
    channel = lax.broadcasted_iota(jnp.int32, (n, width), 0)
    total = jnp.zeros((groups * steps, n), F32)
    for r in range(size):
        here = pl.ds(position ^ r, 1)
        weight = jnp.broadcast_to(weights[here, :], (n, width))
        projector = jnp.where(mode_ref[here, :] == channel, weight, 0.0).astype(BF16)
        total += lax.dot_general(slabs[r][...].reshape(groups * steps, width), projector, NT, preferred_element_type=F32)
    sums[...] = total.reshape(groups, steps, n)
    for r in range(groups):
        outs[r][...] = sums[(position // size) ^ r]


def tree_kernel(steps, levels_ref, table_ref, left_hbm, right_hbm, total_ref, left_ref, right_ref, sems):
    base = steps // 4

    def first(t):
        return mm(table_ref[levels_ref[0, t]], table_ref[levels_ref[0, t + 1]])

    def node(k):
        return mm(left_ref[k], right_ref[k])

    def first_pairs(ks):
        made = [(first(4 * k), first(4 * k + 2)) for k in ks]
        for k, (a, b) in zip(ks, made):
            left_ref[k] = pair(a)
            right_ref[k] = pair(b)

    def later_pairs(ks):
        made = [(node(2 * (k - base)), node(2 * (k - base) + 1)) for k in ks]
        for k, (a, b) in zip(ks, made):
            left_ref[k] = pair(a)
            right_ref[k] = pair(b)

    def run(fn, start, count):
        if count <= 8:
            fn(list(range(start, start + count)))
            return

        def body(i, c):
            fn([start + 8 * i + k for k in range(8)])
            return c

        lax.fori_loop(0, count // 8, body, 0)

    copies = []

    def store(start, count):
        for ref, hbm in ((right_ref, right_hbm), (left_ref, left_hbm)):
            part = pl.ds(start, count)
            copies.append(pltpu.make_async_copy(ref.at[part], hbm.at[part], sems.at[len(copies)]))
            copies[-1].start()

    run(first_pairs, 0, base)
    store(0, base)
    run(later_pairs, base, base // 2)
    store(base, base // 2)
    count, start = base // 4, base + base // 2
    while count >= 1:
        run(later_pairs, start, count)
        store(start, count)
        start += count
        count //= 2
    total_ref[...] = pair(node(start - 1))
    for copy in copies:
        copy.wait()


def local_kernel(pos_ref, levels_ref, gain_ref, init_ref, total_ref, table_ref, right_hbm, *refs):
    parts, (lefts_ref, shift_ref, drive_ref, right_ref, sems) = refs[:-5], refs[-5:]
    steps, n = drive_ref.shape
    base = steps // 4
    copies = [
        pltpu.make_async_copy(right_hbm.at[pl.ds(0, base)], right_ref.at[pl.ds(0, base)], sems.at[0]),
        pltpu.make_async_copy(right_hbm.at[pl.ds(base, base - 1)], right_ref.at[pl.ds(base, base - 1)], sems.at[1]),
    ]
    for copy in copies:
        copy.start()
    measured = parts[0][...]
    for part in parts[1:]:
        measured += part[...]
    drive_ref[...] = lax.dot_general(measured.astype(BF16), gain_ref[...], NT, preferred_element_type=F32)

    states = [row(drive_ref, t) for t in range(steps)]
    at, offset = 0, 0
    for level in range(steps.bit_length() - 1):
        if level in (1, 2):
            copies[level - 1].wait()
        later = []
        for i in range(len(states) // 2):
            mat = table_ref[levels_ref[0, 2 * i + 1]] if level == 0 else right_ref[offset + i]
            lefts_ref[pl.ds(at + i, 1), :] = states[2 * i][:1]
            later.append(vm(states[2 * i], mat) + states[2 * i + 1])
        at += len(later)
        if level > 0:
            offset += len(later)
        states = later
    lefts_ref[pl.ds(at, 1), :] = states[0][:1]
    first = jnp.where(pos_ref[0] == 0, row(init_ref, 0), 0.0)
    shift_ref[...] = states[0] + vm(first, total_ref[...])


def rows16(vec):
    high = vec.astype(BF16).astype(F32)
    both = jnp.concatenate([high, vec - high], axis=1)
    return jnp.concatenate([both, both], axis=0).astype(BF16)


def rows8(rows):
    both = rows.astype(F32)
    n = rows.shape[1] // 2
    return both[:8, :n] + both[:8, n:]


def group_kernel(size, pos_ref, *refs):
    maps, shifts = refs[:size], refs[size : 2 * size]
    prefix_ref, before_ref, mine_ref, shift_ref, map_ref, held_ref = refs[2 * size :]
    n = prefix_ref.shape[0]
    member = pos_ref[0] % size
    for r in range(size):
        map_ref[member ^ r] = maps[r][...]
        held_ref[member ^ r] = shifts[r][...]
    rows, cols = (lax.broadcasted_iota(jnp.int32, (n, n), d) for d in (0, 1))
    prefix, before = pair((rows == cols).astype(F32)), jnp.zeros((8, n), F32)
    run, vec = map_ref[0], held_ref[0]
    for q in range(1, size):
        here = member == q
        prefix, before = jnp.where(here, run, prefix), jnp.where(here, vec, before)
        vec = vm(vec, map_ref[q]) + held_ref[q]
        run = pair(mm(run, map_ref[q]))
    prefix_ref[...] = prefix
    before_ref[...] = before
    mine_ref[pl.ds(0, n), :] = run
    mine_ref[pl.ds(n, 16), :] = rows16(vec)
    shift_ref[...] = rows16(vec)


def final_kernel(size, pos_ref, levels_ref, init_ref, prefix_ref, before_ref, total_ref, lefts_ref, left_ref, table_ref, *refs):
    got, out_ref = refs[:-1], refs[-1]
    steps, n = lefts_ref.shape
    position = pos_ref[0]
    group = position // size
    state = jnp.zeros((8, n), F32)
    for r in range(len(got), 0, -1):
        rows = got[r - 1].shape[0]
        if rows > 16:
            state = jnp.where(group > r, vm(state, got[r - 1][pl.ds(0, n), :]), 0.0)
        state += jnp.where(group >= r, rows8(got[r - 1][pl.ds(rows - 16, 16), :]), 0.0)
    first = jnp.where(position == 0, row(init_ref, 0), 0.0)
    state = vm(state, prefix_ref[...]) + before_ref[...] + first
    out_ref[pl.ds(steps - 1, 1), :] = (vm(state, total_ref[...]) + row(lefts_ref, steps - 1))[:1]
    levels = steps.bit_length() - 1
    starts = [state]
    sizes = [steps >> (level + 1) for level in range(levels)]
    for level in reversed(range(levels)):
        at, offset = sum(sizes[:level]), sum(sizes[1:level])
        later = []
        for i, x in enumerate(starts):
            mat = table_ref[levels_ref[0, 2 * i]] if level == 0 else left_ref[offset + i]
            later += [x, vm(x, mat) + row(lefts_ref, at + i)]
        starts = later
    for t in range(1, steps):
        out_ref[pl.ds(t - 1, 1), :] = starts[t][:1]


def shards(count, frames, levels, initial_state, transitions, gain, pixel_mode, pixel_weight):
    n = gain.shape[0]
    kinds = transitions.shape[0]
    pixels, length = frames.shape
    steps = length // count
    position = lax.axis_index("tm").astype(jnp.int32)[None]
    pairs = steps // 2 - 1
    dma = pltpu.SemaphoreType.DMA
    size = 1
    while count % (2 * size) == 0 and 4 * size * size <= count:
        size *= 2
    groups = count // size

    def swaps(x, step, times):
        x = x if isinstance(x, list) else [x] * (times - 1)
        return [
            lax.ppermute(a, "tm", [(j, j ^ (r * step)) for j in range(count)]) for a, r in zip(x, range(1, times))
        ]

    one_map = shape((n, 2 * n), BF16)
    table_shape = shape((kinds, n, 2 * n), BF16)
    cuts = 4
    turn = pixels % 128 == 0 and length % (128 * cuts) == 0
    small = [levels[None], initial_state[None], gain]
    if turn:
        small += [pixel_mode.reshape(count, pixels), pixel_weight.reshape(count, pixels)]
    given = [hbm(a) for a in [transitions] + small + [frames] * turn]
    outs = [table_shape] + [shape(a.shape, a.dtype) for a in small]
    buffers = [pltpu.VMEM(transitions.shape, F32)]
    if turn:
        outs += [shape((groups, steps, pixels), BF16)] * size
        buffers += [pltpu.VMEM(frames.shape, BF16), pltpu.VMEM((length, pixels), BF16)]
    table, levels, initial_state, gain, *rest = call(
        functools.partial(front_kernel, cuts, len(small), size), "front", 5,
        out_shape=outs,
        in_specs=[SMEM] + [HBM] * len(given),
        out_specs=[VMEM] * len(outs),
        scratch_shapes=buffers + [dma((cuts + 4 + len(small),))],
    )(position, *given)
    tree = pltpu.VMEM((pairs, n, 2 * n), BF16)
    maps = pltpu.HBM((pairs, n, 2 * n), BF16)
    left, right, total = call(
        functools.partial(tree_kernel, steps), "tree_of_maps", 8,
        out_shape=[maps, maps, one_map],
        in_specs=[SMEM, VMEM],
        out_specs=[HBM, HBM, VMEM],
        scratch_shapes=[tree, tree, dma((2 * steps.bit_length(),))],
    )(levels, table)

    if turn:
        mode, weight, slab, *slabs = rest
        first, *parts = call(
            functools.partial(project_kernel, size), "project", 4,
            out_shape=[shape((steps, n), F32)] * groups,
            in_specs=[SMEM] + [VMEM] * (3 + size),
            out_specs=[VMEM] * groups,
            scratch_shapes=[pltpu.VMEM((groups, steps, n), F32), pltpu.VMEM((count, pixels), F32)],
        )(position, total, mode, weight, slab, *swaps(slabs, 1, size)[::-1])
        parts = [first] + swaps(parts, size, groups)
    else:
        x = lax.all_to_all(frames, "tm", split_axis=1, concat_axis=0, tiled=True)
        channels = jnp.arange(n, dtype=jnp.int32)
        projector = jnp.where(pixel_mode[None, :] == channels[:, None], pixel_weight[None, :], jnp.zeros((), BF16))
        parts = [lax.dot_general(x, projector, (((0,), (1,)), ((), ())), preferred_element_type=F32)]

    vector = shape((8, n), F32)

    members = swaps(total, 1, size)
    lefts, shift = call(
        local_kernel, "local_states", 8, 1 << 30,
        out_shape=[shape((steps, n), F32), vector],
        in_specs=[SMEM, SMEM] + [VMEM] * 4 + [HBM] + [VMEM] * len(parts),
        out_specs=[VMEM] * 2,
        scratch_shapes=[pltpu.VMEM((steps, n), F32), tree, dma((2,))],
    )(position, levels, gain, initial_state, total, table, hbm(right), *parts)
    prefix, before, mine, carried = call(
        functools.partial(group_kernel, size), "group_maps", 2,
        out_shape=[one_map, vector, shape((n + 16, 2 * n), BF16), shape((16, 2 * n), BF16)],
        in_specs=[SMEM] + [VMEM] * (2 * size),
        out_specs=[VMEM] * 4,
        scratch_shapes=[pltpu.VMEM((size, n, 2 * n), BF16), pltpu.VMEM((size, 8, n), F32)],
    )(position, total, *members, shift, *swaps(shift, 1, size))
    got = [
        lax.ppermute(mine if r < groups - 1 else carried, "tm", [(j, (j + r * size) % count) for j in range(count)])
        for r in range(1, groups)
    ]

    return call(
        functools.partial(final_kernel, size), "estimates", 6,
        out_shape=shape((steps, n), F32),
        in_specs=[SMEM, SMEM] + [VMEM] * (7 + len(got)),
        out_specs=VMEM,
    )(position, levels, initial_state, prefix, before, total, lefts, left, table, *got)


def solution(mesh):
    in_specs = (P("tm", "parts"), P(("parts", "tm")), P("parts"), P(), P(), P(), P())
    out_specs = P(("parts", "tm"), None)
    return jax.shard_map(
        functools.partial(shards, mesh.shape["tm"]),
        mesh=mesh,
        in_specs=in_specs,
        out_specs=out_specs,
        check_vma=False,
    )
```

```python
import functools

import jax
import jax.numpy as jnp
from jax import lax
from jax.experimental import pallas as pl
from jax.experimental.pallas import tpu as pltpu
from jax.sharding import PartitionSpec as P

F32 = jnp.float32
BF16 = jnp.bfloat16
MIB = 1 << 20
NT = (((1,), (1,)), ((), ()))
VMEM = pl.BlockSpec(memory_space=pltpu.VMEM)
SMEM = pl.BlockSpec(memory_space=pltpu.SMEM)
HBM = pl.BlockSpec(memory_space=pltpu.HBM)
shape = jax.ShapeDtypeStruct


def hbm(x):
    return pltpu.with_memory_space_constraint(x, pltpu.HBM)


def call(kernel, name, mib, flops=1, **kw):
    return pl.pallas_call(
        kernel,
        name=name,
        compiler_params=pltpu.CompilerParams(vmem_limit_bytes=mib * MIB),
        cost_estimate=pl.CostEstimate(flops=flops, bytes_accessed=1, transcendentals=0),
        **kw,
    )


def pair(x):
    high = x.astype(BF16)
    mid = (x - high.astype(F32)).astype(BF16)
    return jnp.concatenate([high, mid], axis=1)


def mm(left, right):
    n = right.shape[0]
    out = jnp.dot(left, jnp.concatenate([right, right], axis=0), preferred_element_type=F32)
    return out[:, :n] + out[:, n:]


def vm(vec, mat):
    high = vec.astype(BF16).astype(F32)
    rows = jnp.concatenate([high, vec - high], axis=0).astype(BF16)
    out = jnp.dot(rows, mat, preferred_element_type=F32)
    n = vec.shape[1]
    out = out[:, :n] + out[:, n:]
    return out[:8] + out[8:]


def row(ref, t):
    return jnp.broadcast_to(ref[pl.ds(t, 1), :], (8, ref.shape[1]))


def front_kernel(cuts, extra, size, pos_ref, trans_ref, *refs):
    given, refs = refs[:extra], refs[extra:]
    turn = len(refs) > extra + 3
    if turn:
        frames_ref, table_ref, *moved = refs[: 2 + extra]
        slabs = refs[2 + extra : 2 + extra + size]
        trans, frames, turned, sems = refs[2 + extra + size :]
        width = frames.shape[1] // cuts
        parts = [pl.ds(k * width, width) for k in range(cuts)]
        ins = [
            pltpu.make_async_copy(frames_ref.at[:, part], frames.at[:, part], sems.at[k])
            for k, part in enumerate(parts)
        ]
        for copy in ins:
            copy.start()
    else:
        table_ref, *moved, trans, sems = refs
    kinds = trans.shape[0]
    few = kinds // 4
    maps = [
        pltpu.make_async_copy(trans_ref.at[pl.ds(k * few, few)], trans.at[pl.ds(k * few, few)], sems.at[cuts + k])
        for k in range(4)
    ]
    moves = [pltpu.make_async_copy(a, b, sems.at[cuts + 4 + k]) for k, (a, b) in enumerate(zip(given, moved))]
    for copy in maps + moves:
        copy.start()
    if turn:
        for k in range(cuts):
            ins[k].wait()
            turned[parts[k], :] = frames[:, parts[k]].T
        member = pos_ref[0] % size
        groups, steps, _ = slabs[0].shape
        for r in range(size):
            for g in range(groups):
                start = pl.multiple_of((g * size + (member ^ r)) * steps, steps)
                slabs[r][g] = turned[pl.ds(start, steps), :]
    for k in range(4):
        maps[k].wait()
        for q in range(k * few, (k + 1) * few):
            table_ref[q] = pair(trans[q].T)
    for copy in moves:
        copy.wait()


def project_kernel(size, pos_ref, after_ref, mode_ref, weight_ref, *refs):
    slabs, outs, (sums, weights) = refs[:size], refs[size:-2], refs[-2:]
    weights[...] = weight_ref[...].astype(F32)
    groups, steps, width = slabs[0].shape
    n = sums.shape[2]
    position = pos_ref[0]
    channel = lax.broadcasted_iota(jnp.int32, (n, width), 0)
    total = jnp.zeros((groups * steps, n), F32)
    for r in range(size):
        here = pl.ds(position ^ r, 1)
        weight = jnp.broadcast_to(weights[here, :], (n, width))
        projector = jnp.where(mode_ref[here, :] == channel, weight, 0.0).astype(BF16)
        total += lax.dot_general(slabs[r][...].reshape(groups * steps, width), projector, NT, preferred_element_type=F32)
    sums[...] = total.reshape(groups, steps, n)
    for r in range(groups):
        outs[r][...] = sums[(position // size) ^ r]


def tree_kernel(steps, levels_ref, table_ref, left_hbm, right_hbm, total_ref, left_ref, right_ref, sems):
    base = steps // 4

    def first(t):
        return mm(table_ref[levels_ref[0, t]], table_ref[levels_ref[0, t + 1]])

    def node(k):
        return mm(left_ref[k], right_ref[k])

    def first_pairs(ks):
        made = [(first(4 * k), first(4 * k + 2)) for k in ks]
        for k, (a, b) in zip(ks, made):
            left_ref[k] = pair(a)
            right_ref[k] = pair(b)

    def later_pairs(ks):
        made = [(node(2 * (k - base)), node(2 * (k - base) + 1)) for k in ks]
        for k, (a, b) in zip(ks, made):
            left_ref[k] = pair(a)
            right_ref[k] = pair(b)

    def run(fn, start, count):
        if count <= 8:
            fn(list(range(start, start + count)))
            return

        def body(i, c):
            fn([start + 8 * i + k for k in range(8)])
            return c

        lax.fori_loop(0, count // 8, body, 0)

    copies = []

    def store(start, count):
        for ref, hbm in ((right_ref, right_hbm), (left_ref, left_hbm)):
            part = pl.ds(start, count)
            copies.append(pltpu.make_async_copy(ref.at[part], hbm.at[part], sems.at[len(copies)]))
            copies[-1].start()

    run(first_pairs, 0, base)
    store(0, base)
    run(later_pairs, base, base // 2)
    store(base, base // 2)
    count, start = base // 4, base + base // 2
    while count >= 1:
        run(later_pairs, start, count)
        store(start, count)
        start += count
        count //= 2
    total_ref[...] = pair(node(start - 1))
    for copy in copies:
        copy.wait()


def local_kernel(pos_ref, levels_ref, gain_ref, init_ref, total_ref, table_ref, right_hbm, *refs):
    parts, (lefts_ref, shift_ref, drive_ref, right_ref, sems) = refs[:-5], refs[-5:]
    steps, n = drive_ref.shape
    base = steps // 4
    copies = [
        pltpu.make_async_copy(right_hbm.at[pl.ds(0, base)], right_ref.at[pl.ds(0, base)], sems.at[0]),
        pltpu.make_async_copy(right_hbm.at[pl.ds(base, base - 1)], right_ref.at[pl.ds(base, base - 1)], sems.at[1]),
    ]
    for copy in copies:
        copy.start()
    measured = parts[0][...]
    for part in parts[1:]:
        measured += part[...]
    drive_ref[...] = lax.dot_general(measured.astype(BF16), gain_ref[...], NT, preferred_element_type=F32)

    states = [row(drive_ref, t) for t in range(steps)]
    at, offset = 0, 0
    for level in range(steps.bit_length() - 1):
        if level in (1, 2):
            copies[level - 1].wait()
        later = []
        for i in range(len(states) // 2):
            mat = table_ref[levels_ref[0, 2 * i + 1]] if level == 0 else right_ref[offset + i]
            lefts_ref[pl.ds(at + i, 1), :] = states[2 * i][:1]
            later.append(vm(states[2 * i], mat) + states[2 * i + 1])
        at += len(later)
        if level > 0:
            offset += len(later)
        states = later
    lefts_ref[pl.ds(at, 1), :] = states[0][:1]
    first = jnp.where(pos_ref[0] == 0, row(init_ref, 0), 0.0)
    shift_ref[...] = states[0] + vm(first, total_ref[...])


def rows16(vec):
    high = vec.astype(BF16).astype(F32)
    both = jnp.concatenate([high, vec - high], axis=1)
    return jnp.concatenate([both, both], axis=0).astype(BF16)


def rows8(rows):
    both = rows.astype(F32)
    n = rows.shape[1] // 2
    return both[:8, :n] + both[:8, n:]


def group_kernel(size, pos_ref, *refs):
    maps, shifts = refs[:size], refs[size : 2 * size]
    prefix_ref, before_ref, mine_ref, shift_ref, map_ref, held_ref = refs[2 * size :]
    n = prefix_ref.shape[0]
    member = pos_ref[0] % size
    for r in range(size):
        map_ref[member ^ r] = maps[r][...]
        held_ref[member ^ r] = shifts[r][...]
    rows, cols = (lax.broadcasted_iota(jnp.int32, (n, n), d) for d in (0, 1))
    prefix, before = pair((rows == cols).astype(F32)), jnp.zeros((8, n), F32)
    run, vec = map_ref[0], held_ref[0]
    for q in range(1, size):
        here = member == q
        prefix, before = jnp.where(here, run, prefix), jnp.where(here, vec, before)
        vec = vm(vec, map_ref[q]) + held_ref[q]
        run = pair(mm(run, map_ref[q]))
    prefix_ref[...] = prefix
    before_ref[...] = before
    mine_ref[pl.ds(0, n), :] = run
    mine_ref[pl.ds(n, 16), :] = rows16(vec)
    shift_ref[...] = rows16(vec)


def final_kernel(size, pos_ref, levels_ref, init_ref, prefix_ref, before_ref, total_ref, lefts_ref, left_ref, table_ref, *refs):
    got, out_ref = refs[:-1], refs[-1]
    steps, n = lefts_ref.shape
    position = pos_ref[0]
    group = position // size
    state = jnp.zeros((8, n), F32)
    for r in range(len(got), 0, -1):
        rows = got[r - 1].shape[0]
        if rows > 16:
            state = jnp.where(group > r, vm(state, got[r - 1][pl.ds(0, n), :]), 0.0)
        state += jnp.where(group >= r, rows8(got[r - 1][pl.ds(rows - 16, 16), :]), 0.0)
    first = jnp.where(position == 0, row(init_ref, 0), 0.0)
    state = vm(state, prefix_ref[...]) + before_ref[...] + first
    out_ref[pl.ds(steps - 1, 1), :] = (vm(state, total_ref[...]) + row(lefts_ref, steps - 1))[:1]
    levels = steps.bit_length() - 1
    starts = [state]
    sizes = [steps >> (level + 1) for level in range(levels)]
    for level in reversed(range(levels)):
        at, offset = sum(sizes[:level]), sum(sizes[1:level])
        later = []
        for i, x in enumerate(starts):
            mat = table_ref[levels_ref[0, 2 * i]] if level == 0 else left_ref[offset + i]
            later += [x, vm(x, mat) + row(lefts_ref, at + i)]
        starts = later
    for t in range(1, steps):
        out_ref[pl.ds(t - 1, 1), :] = starts[t][:1]


def shards(count, frames, levels, initial_state, transitions, gain, pixel_mode, pixel_weight):
    n = gain.shape[0]
    kinds = transitions.shape[0]
    pixels, length = frames.shape
    steps = length // count
    position = lax.axis_index("tm").astype(jnp.int32)[None]
    pairs = steps // 2 - 1
    dma = pltpu.SemaphoreType.DMA
    size = 1
    while count % (2 * size) == 0 and 4 * size * size <= count:
        size *= 2
    groups = count // size

    def swaps(x, step, times):
        x = x if isinstance(x, list) else [x] * (times - 1)
        return [
            lax.ppermute(a, "tm", [(j, j ^ (r * step)) for j in range(count)]) for a, r in zip(x, range(1, times))
        ]

    one_map = shape((n, 2 * n), BF16)
    table_shape = shape((kinds, n, 2 * n), BF16)
    cuts = 4
    turn = pixels % 128 == 0 and length % (128 * cuts) == 0
    small = [levels[None], initial_state[None], gain]
    if turn:
        small += [pixel_mode.reshape(count, pixels), pixel_weight.reshape(count, pixels)]
    given = [hbm(a) for a in [transitions] + small + [frames] * turn]
    outs = [table_shape] + [shape(a.shape, a.dtype) for a in small]
    buffers = [pltpu.VMEM(transitions.shape, F32)]
    if turn:
        outs += [shape((groups, steps, pixels), BF16)] * size
        buffers += [pltpu.VMEM(frames.shape, BF16), pltpu.VMEM((length, pixels), BF16)]
    table, levels, initial_state, gain, *rest = call(
        functools.partial(front_kernel, cuts, len(small), size), "front", 5,
        out_shape=outs,
        in_specs=[SMEM] + [HBM] * len(given),
        out_specs=[VMEM] * len(outs),
        scratch_shapes=buffers + [dma((cuts + 4 + len(small),))],
    )(position, *given)
    tree = pltpu.VMEM((pairs, n, 2 * n), BF16)
    maps = pltpu.HBM((pairs, n, 2 * n), BF16)
    left, right, total = call(
        functools.partial(tree_kernel, steps), "tree_of_maps", 8,
        out_shape=[maps, maps, one_map],
        in_specs=[SMEM, VMEM],
        out_specs=[HBM, HBM, VMEM],
        scratch_shapes=[tree, tree, dma((2 * steps.bit_length(),))],
    )(levels, table)

    if turn:
        mode, weight, slab, *slabs = rest
        first, *parts = call(
            functools.partial(project_kernel, size), "project", 4,
            out_shape=[shape((steps, n), F32)] * groups,
            in_specs=[SMEM] + [VMEM] * (3 + size),
            out_specs=[VMEM] * groups,
            scratch_shapes=[pltpu.VMEM((groups, steps, n), F32), pltpu.VMEM((count, pixels), F32)],
        )(position, total, mode, weight, slab, *swaps(slabs, 1, size))
        parts = [first] + swaps(parts, size, groups)[::-1]
    else:
        x = lax.all_to_all(frames, "tm", split_axis=1, concat_axis=0, tiled=True)
        channels = jnp.arange(n, dtype=jnp.int32)
        projector = jnp.where(pixel_mode[None, :] == channels[:, None], pixel_weight[None, :], jnp.zeros((), BF16))
        parts = [lax.dot_general(x, projector, (((0,), (1,)), ((), ())), preferred_element_type=F32)]

    vector = shape((8, n), F32)

    members = swaps(total, 1, size)
    lefts, shift = call(
        local_kernel, "local_states", 8, 1 << 30,
        out_shape=[shape((steps, n), F32), vector],
        in_specs=[SMEM, SMEM] + [VMEM] * 4 + [HBM] + [VMEM] * len(parts),
        out_specs=[VMEM] * 2,
        scratch_shapes=[pltpu.VMEM((steps, n), F32), tree, dma((2,))],
    )(position, levels, gain, initial_state, total, table, hbm(right), *parts)
    prefix, before, mine, carried = call(
        functools.partial(group_kernel, size), "group_maps", 2,
        out_shape=[one_map, vector, shape((n + 16, 2 * n), BF16), shape((16, 2 * n), BF16)],
        in_specs=[SMEM] + [VMEM] * (2 * size),
        out_specs=[VMEM] * 4,
        scratch_shapes=[pltpu.VMEM((size, n, 2 * n), BF16), pltpu.VMEM((size, 8, n), F32)],
    )(position, total, *members, shift, *swaps(shift, 1, size))
    got = [
        lax.ppermute(mine, "tm", [(j, (j + r * size) % count) for j in range(count)]) for r in range(1, groups - 1)
    ]
    got.append(lax.ppermute(carried, "tm", [(j, j ^ ((groups - 1) * size)) for j in range(count)]))

    return call(
        functools.partial(final_kernel, size), "estimates", 6,
        out_shape=shape((steps, n), F32),
        in_specs=[SMEM, SMEM] + [VMEM] * (7 + len(got)),
        out_specs=VMEM,
    )(position, levels, initial_state, prefix, before, total, lefts, left, table, *got)


def solution(mesh):
    in_specs = (P("tm", "parts"), P(("parts", "tm")), P("parts"), P(), P(), P(), P())
    out_specs = P(("parts", "tm"), None)
    return jax.shard_map(
        functools.partial(shards, mesh.shape["tm"]),
        mesh=mesh,
        in_specs=in_specs,
        out_specs=out_specs,
        check_vma=False,
    )
```
